32 devices in a mesh: pages: 4 (over y, core), row: 2 (over x), col: 4 (over z).
Axes of the slice: x: 2, y: 2, z: 4, core: 2. Of those that a mesh axis runs over, the one named last changes fastest.
Arguments:
- residual: bfloat16 [128, 2, 2048], P('pages', None, ('row', 'col')), may hold values from -6 to 6
- fresh_qkv: bfloat16 [128, 2, 3, 2048], P('pages', None, None, 'col'), may hold values from -27 to 27
- prefix_pages: bfloat16 [64, 2, 128, 2048], P('pages', None, 'row', 'col'), may hold values from -6 to 6
- tail_pages: bfloat16 [128, 2, 128, 2048], P('pages', None, 'row', 'col'), may hold values from -6 to 6
- prefix_item: int32 [64], replicated, may hold values from 0 to 63, as said below
- tail_item: int32 [128], replicated, may hold values from 0 to 127, as said below
- prefix_length: int32 [8], replicated, may hold values from 1 to 1024, 5120 in all
- tail_length: int32 [128], replicated, may hold values from 1 to 128, 10240 in all
- out_weight: bfloat16 [2048, 2048], P('col', 'row'), may hold values from -0.125 to 0.125
- out_bias: bfloat16 [2048], P(('row', 'col')), may hold values from -4 to 4
- mlp_gain: bfloat16 [2048], P('row'), may hold values from 0.25 to 1.75
- mlp_shift: bfloat16 [2048], P('row'), may hold values from -4 to 4
- up_weight: bfloat16 [2048, 8192], P('row', 'col'), may hold values from -0.125 to 0.125
- up_bias: bfloat16 [8192], P(('col', 'row')), may hold values from -4 to 4
- down_weight: bfloat16 [8192, 2048], P('col', 'row'), may hold values from -0.0625 to 0.0625
- down_bias: bfloat16 [2048], P(('row', 'col')), may hold values from -4 to 4
- next_gain: bfloat16 [2048], P('row'), may hold values from 0.25 to 1.75
- next_shift: bfloat16 [2048], P('row'), may hold values from -4 to 4
- score_weight: bfloat16 [2048], P('row'), may hold values from -0.125 to 0.125
- qkv_weight: bfloat16 [2048, 6144], P('row', 'col'), may hold values from -0.125 to 0.125
- qkv_bias: bfloat16 [6144], P(('col', 'row')), may hold values from -4 to 4
Outputs:
- layer_out: bfloat16 [128, 2, 2048], P('pages', None, ('row', 'col'))
- score_out: float32 [128, 2], P('pages')
- projected_next: bfloat16 [128, 2, 6144], P('pages', None, ('col', 'row'))
The draws below stay inside these ranges and needn't reach their ends.
Inputs may be any that keep to these rules, and one draw needn't show every extreme that they name: `prefix_item`: each of the 64 prompt pages is held by exactly one slot; slot h * 16 + g * 4 + k (k < 4) holds a page of one of the prompts g * 2 to (g + 1) * 2 - 1. `tail_item`: each continuation's tail is held by exactly one slot; slot h * 32 + g * 8 + k (k < 8) holds the tail of one of the continuations g * 32 to (g + 1) * 32 - 1. `prefix_length`: some prompt has exactly 1024 cached tokens. `tail_length`: some continuation has exactly 128 tail tokens.
All inputs are finite; a program needn't handle non-finite values.
Results may differ from the reference program's by a relative error of at most 0.023.
Values may be sent and summed in bfloat16 or wider, within the bound.
A program may use at most 64 MiB of HBM per device.

```python
import math
import jax
import jax.numpy as jnp
import numpy as np
from jax import lax

D = 2048
H = 16
HD = 128
FF = 8192
PAGE = 128
MAXPAGES = 8
CONT = 16
GROUPS = 4
PROMPTS = 8
BATCH_GRP = 32
BATCH = 128
PSLOTS = 16
PAIR_PAGES = 4
PAIR_TAILS = 8


def spread_items(base_key, per_group, groups_total, pair_count):
    orders = jax.vmap(lambda group_id: jax.random.permutation(jax.random.fold_in(base_key, group_id), per_group))(jnp.arange(groups_total, dtype=jnp.int32))
    item_table = orders.astype(jnp.int32) + (jnp.arange(groups_total, dtype=jnp.int32) * per_group)[:, None]
    return item_table.reshape(groups_total, groups_total, pair_count).transpose(1, 0, 2).reshape(-1)


def draw_prefix_item(key, part):
    return spread_items(jax.random.fold_in(key, 7), PSLOTS, GROUPS, PAIR_PAGES)


def draw_tail_item(key, part):
    return spread_items(jax.random.fold_in(key, 11), BATCH_GRP, GROUPS, PAIR_TAILS)


def draw_fresh_qkv(key, part):
    full_shape = (BATCH, 2, 3, D)
    return jnp.clip(jax.random.normal(key, full_shape, jnp.float32), -6.0, 6.0).astype(jnp.bfloat16)


def block_scale(key, extent, shards, smallest, high):
    factor_of = 1.0
    for axis_at, parts in shards:
        draws = jax.random.uniform(jax.random.fold_in(jax.random.fold_in(key, 6), axis_at), (parts,), jnp.float32, smallest / len(shards), high / len(shards))
        factor_of = factor_of * jnp.repeat(jnp.exp(draws), extent[axis_at] // parts).reshape((-1,) + (1,) * (len(extent) - 1 - axis_at))
    return factor_of


def split_up(number_of, total, limit, skew):
    weights = [(1 << 20) // math.isqrt(standing ** skew) + 1 for standing in range(2, number_of + 1)]
    rest, given = total - limit - (number_of - 1), [1] * (number_of - 1)
    while rest > 0:
        candidates = [i for i in range(number_of - 1) if given[i] < limit]
        pool, left = sum([weights[i] for i in candidates]), rest
        for i in candidates:
            more = min(limit - given[i], max(1, left * weights[i] // pool), rest)
            given[i] = given[i] + more
            rest = rest - more
    return np.array([limit] + given)


def uneven(rng, count, total, most, skew):
    if count == 2:
        one = jax.random.randint(rng, (), max(1, total - most), min(most, total - 1) + 1)
        return jnp.stack([one, total - one])
    lengths = jnp.asarray(split_up(count, total, most, skew), jnp.int32)
    twos = (count - 1) // 2
    giver, taker = lengths[1:1 + 2 * twos:2], lengths[2:2 + 2 * twos:2]
    slack = jnp.minimum(giver - 1, most - taker)
    passed = jax.random.randint(jax.random.fold_in(rng, 1), (twos,), 0, 1 << 20) % (slack + 1)
    lengths = lengths.at[1:1 + 2 * twos:2].set(giver - passed).at[2:2 + 2 * twos:2].set(taker + passed)
    return lengths[jax.random.permutation(jax.random.fold_in(rng, 2), count)]


def gaussian(rng, dims, scale, most, pieces=(), kind=jnp.bfloat16):
    factor_of = block_scale(rng, dims, pieces, -0.22, 0.18) if pieces else 1.0
    values = jax.random.normal(rng, dims, jnp.float32) * scale * factor_of
    return jnp.minimum(jnp.maximum(values, -most), most).astype(kind)


def setup_inputs(seed: int = 0) -> dict:
    splits = jax.random.split(jax.random.key(seed), 22)
    return {
        "residual": gaussian(splits[0], (BATCH, 2, D), 1.0, 6.0, ((0, 4), (2, 8))),
        "fresh_qkv": draw_fresh_qkv(jax.random.fold_in(splits[21], 71), 0),
        "prefix_pages": gaussian(splits[2], (PROMPTS * MAXPAGES, 2, PAGE, D), 1.0, 6.0, ((0, 4), (2, 2), (3, 4))),
        "tail_pages": gaussian(splits[3], (BATCH, 2, PAGE, D), 1.0, 6.0, ((0, 4), (2, 2), (3, 4))),
        "prefix_item": draw_prefix_item(jax.random.fold_in(splits[21], 71), 0),
        "tail_item": draw_tail_item(jax.random.fold_in(splits[21], 71), 0),
        "prefix_length": uneven(splits[6], PROMPTS, PROMPTS * MAXPAGES * PAGE * 5 // 8, MAXPAGES * PAGE, 1).astype(jnp.int32),
        "tail_length": uneven(splits[7], BATCH, BATCH * PAGE * 5 // 8, PAGE, 1).astype(jnp.int32),
        "out_weight": gaussian(splits[8], (D, D), D ** -0.5, 0.125, ((0, 4), (1, 2))),
        "out_bias": gaussian(splits[9], (D,), 0.3, 4.0, ((0, 8),)),
        "mlp_gain": jnp.clip(1.0 + 0.15 * jax.random.normal(splits[10], (D,), jnp.float32), 0.25, 1.75).astype(jnp.bfloat16),
        "mlp_shift": gaussian(splits[11], (D,), 0.3, 4.0, ((0, 2),)),
        "up_weight": gaussian(splits[12], (D, FF), D ** -0.5, 0.125, ((0, 2), (1, 4))),
        "up_bias": gaussian(splits[13], (FF,), 0.5, 4.0, ((0, 8),)),
        "down_weight": gaussian(splits[14], (FF, D), FF ** -0.5, 0.0625, ((0, 4), (1, 2))),
        "down_bias": gaussian(splits[15], (D,), 0.3, 4.0, ((0, 8),)),
        "next_gain": jnp.clip(1.0 + 0.15 * jax.random.normal(splits[16], (D,), jnp.float32), 0.25, 1.75).astype(jnp.bfloat16),
        "next_shift": gaussian(splits[17], (D,), 0.3, 4.0, ((0, 2),)),
        "score_weight": gaussian(splits[18], (D,), D ** -0.5, 0.125, ((0, 2),)),
        "qkv_weight": gaussian(splits[19], (D, 3 * D), D ** -0.5, 0.125, ((0, 2), (1, 4))),
        "qkv_bias": gaussian(splits[20], (3 * D,), 0.3, 4.0, ((0, 8),)),
    }


masked_score = -1e+30
norm_eps = 1e-05

def layer_norm(values, gain, shift):
    center = lax.optimization_barrier(jnp.mean(values, axis=-1, keepdims=True))
    spread = lax.optimization_barrier(jnp.mean(values * values, axis=-1, keepdims=True)) - center * center
    return (values - center) * lax.rsqrt(spread + norm_eps) * gain.astype(jnp.float32) + shift.astype(jnp.float32)

def reference(residual, fresh_qkv, prefix_pages, tail_pages, prefix_item, tail_item, prefix_length, tail_length, out_weight, out_bias, mlp_gain, mlp_shift, up_weight, up_bias, down_weight, down_bias, next_gain, next_shift, score_weight, qkv_weight, qkv_bias):
    highest = lax.Precision.HIGHEST
    page_slot = jnp.zeros((PROMPTS * MAXPAGES,), jnp.int32).at[prefix_item].set(jnp.arange(PROMPTS * MAXPAGES, dtype=jnp.int32))
    tail_slot = jnp.zeros((BATCH,), jnp.int32).at[tail_item].set(jnp.arange(BATCH, dtype=jnp.int32))
    head_index = jnp.arange(H, dtype=jnp.int32)
    slopes = jnp.exp2(-8.0 * (head_index + 1).astype(jnp.float32) / H)
    span_one = MAXPAGES * PAGE

    def one_prompt(prompt):
        page_rows = page_slot[prompt * MAXPAGES + jnp.arange(MAXPAGES, dtype=jnp.int32)]
        cached = prefix_pages[page_rows].astype(jnp.float32)
        prefix_keys = cached[:, 0].reshape(span_one, H, HD)
        prefix_values = cached[:, 1].reshape(span_one, H, HD)
        members = prompt * CONT + jnp.arange(CONT, dtype=jnp.int32)
        tail_rows = tail_pages[tail_slot[members]].astype(jnp.float32)
        tail_keys = tail_rows[:, 0].reshape(CONT, PAGE, H, HD)
        tail_values = tail_rows[:, 1].reshape(CONT, PAGE, H, HD)
        fresh_rows = fresh_qkv[members].astype(jnp.float32).reshape(CONT, 2, 3, H, HD)
        queries = fresh_rows[:, :, 0]
        prompt_len = prefix_length[prompt]
        tail_lens = tail_length[members]
        step_index = jnp.arange(2, dtype=jnp.int32)
        query_pos = prompt_len + tail_lens[:, None] + step_index[None, :]
        prefix_pos = jnp.arange(span_one, dtype=jnp.int32)
        tail_pos = jnp.arange(PAGE, dtype=jnp.int32)
        slope_grid = slopes[None, None, :, None]
        prefix_scores = jnp.einsum('cuhd,khd->cuhk', queries, prefix_keys, precision=highest) / math.sqrt(HD)
        prefix_scores = prefix_scores + slope_grid * (prefix_pos[None, None, None, :] - query_pos[:, :, None, None]).astype(jnp.float32)
        prefix_usable = jnp.broadcast_to((prefix_pos < prompt_len)[None, None, None, :], prefix_scores.shape)
        tail_scores = jnp.einsum('cuhd,cjhd->cuhj', queries, tail_keys, precision=highest) / math.sqrt(HD)
        tail_scores = tail_scores + slope_grid * (tail_pos[None, None, None, :] - tail_lens[:, None, None, None] - step_index[None, :, None, None]).astype(jnp.float32)
        tail_usable = jnp.broadcast_to((tail_pos[None, :] < tail_lens[:, None])[:, None, None, :], tail_scores.shape)
        new_scores = jnp.einsum('cuhd,cvhd->cuhv', queries, fresh_rows[:, :, 1], precision=highest) / math.sqrt(HD)
        new_scores = new_scores + slope_grid * (step_index[None, None, None, :] - step_index[None, :, None, None]).astype(jnp.float32)
        new_usable = jnp.broadcast_to((step_index[None, :] <= step_index[:, None])[None, :, None, :], new_scores.shape)
        scores = jnp.concatenate([prefix_scores, tail_scores, new_scores], axis=3)
        usable = jnp.concatenate([prefix_usable, tail_usable, new_usable], axis=3)
        scores = jnp.where(usable, scores, masked_score)
        row_max = lax.optimization_barrier(jnp.max(scores, axis=3, keepdims=True))
        weights = jnp.where(usable, jnp.exp(scores - row_max), 0.0)
        weight_sum = lax.optimization_barrier(jnp.sum(weights, axis=3))
        outputs = jnp.einsum('cuhk,khd->cuhd', weights[..., :span_one], prefix_values, precision=highest)
        outputs = outputs + jnp.einsum('cuhj,cjhd->cuhd', weights[..., span_one:span_one + PAGE], tail_values, precision=highest)
        outputs = outputs + jnp.einsum('cuhv,cvhd->cuhd', weights[..., span_one + PAGE:], fresh_rows[:, :, 2], precision=highest)
        return (outputs / weight_sum[..., None]).reshape(CONT, 2, D).astype(jnp.bfloat16)
    attended = lax.map(one_prompt, jnp.arange(PROMPTS, dtype=jnp.int32)).reshape(BATCH * 2, D)
    hidden_one = residual.reshape(BATCH * 2, D).astype(jnp.float32) + jnp.dot(attended, out_weight, preferred_element_type=jnp.float32) + out_bias.astype(jnp.float32)
    normed_a = layer_norm(hidden_one, mlp_gain, mlp_shift).astype(jnp.bfloat16)
    hidden_two = jax.nn.gelu(jnp.dot(normed_a, up_weight, preferred_element_type=jnp.float32) + up_bias.astype(jnp.float32), approximate=True).astype(jnp.bfloat16)
    layer_out = (hidden_one + jnp.dot(hidden_two, down_weight, preferred_element_type=jnp.float32) + down_bias.astype(jnp.float32)).astype(jnp.bfloat16)
    out_wide = layer_out.astype(jnp.float32)
    score_out = lax.optimization_barrier(jnp.sum(out_wide * score_weight.astype(jnp.float32), axis=1))
    normed_b = layer_norm(out_wide, next_gain, next_shift).astype(jnp.bfloat16)
    projected_next = (jnp.dot(normed_b, qkv_weight, preferred_element_type=jnp.float32) + qkv_bias.astype(jnp.float32)).astype(jnp.bfloat16)
    return (layer_out.reshape(BATCH, 2, D), score_out.reshape(BATCH, 2), projected_next.reshape(BATCH, 2, 3 * D))
```

```python
import math

import jax
import jax.numpy as jnp
from jax import lax
from jax.experimental import pallas as pl
from jax.experimental.pallas import tpu as pltpu
from jax.sharding import PartitionSpec as P

D = 2048
H = 16
HD = 128
PAGE = 128
MAXPAGES = 8
CONT = 16


masked_score = -1e30
norm_eps = 1e-05


def combined_all(shard, axis, combine):
    everything = jax.tree.map(lambda part: lax.all_gather(part, axis), shard)
    first = jax.tree.map(lambda part: part[0], everything)

    def step(k, so_far):
        return combine(so_far, jax.tree.map(lambda part: part[k], everything))

    return lax.fori_loop(1, lax.axis_size(axis), step, first)


def head_slopes(first_head, how_many):
    head_index = first_head + jnp.arange(how_many, dtype=jnp.int32)
    return jnp.exp2(-8.0 * (head_index + 1).astype(jnp.float32) / H)


def slot_partials(queries, page_keys, page_values, usable, offset, slopes):
    scores = jnp.einsum(
        "sqhd,skhd->sqhk", queries, page_keys, preferred_element_type=jnp.float32
    ) / math.sqrt(HD)
    scores = scores + slopes[None, None, :, None] * offset[:, :, None, :]
    usable_full = usable[:, :, None, :]
    scores = jnp.where(usable_full, scores, masked_score)
    maxima = jnp.max(scores, axis=3)
    weights = jnp.where(usable_full, jnp.exp(scores - maxima[..., None]), 0.0)
    totals = jnp.sum(weights, axis=3)
    outputs = jnp.einsum(
        "sqhk,skhd->sqhd", weights, page_values.astype(jnp.float32), precision=lax.Precision.HIGHEST
    )
    return (maxima, totals, outputs)


def merge_pair(left_part, right_part):
    left_max, left_total, left_out = left_part
    right_max, right_total, right_out = right_part
    joined = jnp.maximum(left_max, right_max)
    left_scale = jnp.exp(left_max - joined)
    right_scale = jnp.exp(right_max - joined)
    return (
        joined,
        left_scale * left_total + right_scale * right_total,
        left_scale[..., None] * left_out + right_scale[..., None] * right_out,
    )


def fold_sources(maxima, totals, outputs):
    joined = jnp.max(maxima, axis=0)
    rescale = jnp.exp(maxima - joined[None])
    return (
        joined,
        jnp.sum(rescale * totals, axis=0),
        jnp.sum(rescale[..., None] * outputs, axis=0),
    )


def cache_partials(
    queries,
    page_block,
    page_item,
    tail_block,
    tail_owner,
    prefix_length,
    tail_length,
    row_index,
    slopes,
):
    cont_count = queries.shape[0]
    prompts = cont_count // CONT
    head_count = queries.shape[2]
    slot_count = page_block.shape[0]
    tokens = page_block.shape[2]
    token_index = row_index * tokens + jnp.arange(tokens, dtype=jnp.int32)
    step_index = jnp.arange(2, dtype=jnp.int32)
    slot_prompt = page_item // MAXPAGES
    slot_page = page_item % MAXPAGES
    by_prompt = queries.reshape(prompts, CONT * 2, head_count, HD)
    key_pos = slot_page[:, None] * PAGE + token_index[None, :]
    slot_len = prefix_length[slot_prompt]
    slot_tails = tail_length.reshape(prompts, CONT)[slot_prompt]
    query_pos = (
        slot_len[:, None, None] + slot_tails[:, :, None] + step_index[None, None, :]
    ).reshape(slot_count, CONT * 2)
    offset = (key_pos[:, None, :] - query_pos[:, :, None]).astype(jnp.float32)
    usable = jnp.broadcast_to((key_pos < slot_len[:, None])[:, None, :], offset.shape)
    page_keys = page_block[:, 0].reshape(slot_count, tokens, head_count, HD)
    page_values = page_block[:, 1].reshape(slot_count, tokens, head_count, HD)
    maxima, totals, outputs = slot_partials(
        by_prompt[slot_prompt], page_keys, page_values, usable, offset, slopes
    )
    prompt_max = (
        jnp.full((prompts, CONT * 2, head_count), masked_score, jnp.float32)
        .at[slot_prompt]
        .max(maxima)
    )
    rescale = jnp.exp(maxima - prompt_max[slot_prompt])
    prompt_total = (
        jnp.zeros((prompts, CONT * 2, head_count), jnp.float32)
        .at[slot_prompt]
        .add(rescale * totals)
    )
    prompt_out = (
        jnp.zeros((prompts, CONT * 2, head_count, HD), jnp.float32)
        .at[slot_prompt]
        .add(rescale[..., None] * outputs)
    )
    prefix_part = (
        prompt_max.reshape(cont_count, 2, head_count),
        prompt_total.reshape(cont_count, 2, head_count),
        prompt_out.reshape(cont_count, 2, head_count, HD),
    )
    tail_count = tail_block.shape[0]
    tail_lens = tail_length[tail_owner]
    tail_usable = jnp.broadcast_to(
        (token_index[None, :] < tail_lens[:, None])[:, None, :], (tail_count, 2, tokens)
    )
    tail_offset = (
        token_index[None, None, :] - tail_lens[:, None, None] - step_index[None, :, None]
    ).astype(jnp.float32)
    tail_keys = tail_block[:, 0].reshape(tail_count, tokens, head_count, HD)
    tail_values = tail_block[:, 1].reshape(tail_count, tokens, head_count, HD)
    tail_max, tail_total, tail_out = slot_partials(
        queries[tail_owner], tail_keys, tail_values, tail_usable, tail_offset, slopes
    )
    cont_max = (
        jnp.full((cont_count, 2, head_count), masked_score, jnp.float32)
        .at[tail_owner]
        .set(tail_max)
    )
    cont_total = jnp.zeros((cont_count, 2, head_count), jnp.float32).at[tail_owner].set(tail_total)
    cont_out = jnp.zeros((cont_count, 2, head_count, HD), jnp.float32).at[tail_owner].set(tail_out)
    return merge_pair(prefix_part, (cont_max, cont_total, cont_out))


def normalize(values, sum_one, sum_two, gain, shift):
    center = sum_one / D
    spread = sum_two / D - center * center
    return (
        (values - center[:, None])
        * lax.rsqrt(spread + norm_eps)[:, None]
        * gain.astype(jnp.float32)
        + shift.astype(jnp.float32)
    ).astype(jnp.bfloat16)


def plain_shards(
    residual,
    fresh_qkv,
    prefix_pages,
    tail_pages,
    prefix_item,
    tail_item,
    prefix_length,
    tail_length,
    out_weight,
    out_bias,
    mlp_gain,
    mlp_shift,
    up_weight,
    up_bias,
    down_weight,
    down_bias,
    next_gain,
    next_shift,
    score_weight,
    qkv_weight,
    qkv_bias,
):
    group_index = lax.axis_index("pages")
    row_index = lax.axis_index("row")
    col_index = lax.axis_index("col")
    group_count = lax.axis_size("pages")
    cont_local = residual.shape[0]
    row_total = cont_local * 2
    share = residual.shape[2]
    head_count = fresh_qkv.shape[3] // HD
    slopes = head_slopes(col_index * head_count, head_count)
    fresh_rows = fresh_qkv.reshape(cont_local, 2, 3, head_count, HD)
    slot_count = prefix_pages.shape[0]
    tail_slots = tail_pages.shape[0]
    everyone = lax.all_gather(fresh_qkv[:, :, 0], "pages", axis=0, tiled=True)
    page_item = lax.dynamic_slice_in_dim(prefix_item, group_index * slot_count, slot_count)
    tail_owner = lax.dynamic_slice_in_dim(tail_item, group_index * tail_slots, tail_slots)
    maxima, totals, outputs = cache_partials(
        everyone.reshape(everyone.shape[0], 2, head_count, HD),
        prefix_pages,
        page_item,
        tail_pages,
        tail_owner,
        prefix_length,
        tail_length,
        row_index,
        slopes,
    )
    maxima, totals, outputs = (
        lax.all_to_all(
            maxima.reshape(group_count, row_total, head_count),
            "pages",
            split_axis=0,
            concat_axis=0,
            tiled=True,
        ),
        lax.all_to_all(
            totals.reshape(group_count, row_total, head_count),
            "pages",
            split_axis=0,
            concat_axis=0,
            tiled=True,
        ),
        lax.all_to_all(
            outputs.reshape(group_count, row_total, head_count, HD),
            "pages",
            split_axis=0,
            concat_axis=0,
            tiled=True,
        ),
    )
    cache_max, cache_total, cache_out = fold_sources(maxima, totals, outputs)
    cache_max, cache_total, cache_out = combined_all(
        (cache_max, cache_total, cache_out), "row", merge_pair
    )
    step_index = jnp.arange(2, dtype=jnp.int32)
    new_usable = jnp.broadcast_to(
        (step_index[None, :] <= step_index[:, None])[None], (cont_local, 2, 2)
    )
    new_offset = jnp.broadcast_to(
        (step_index[None, :] - step_index[:, None]).astype(jnp.float32)[None], (cont_local, 2, 2)
    )
    new_part = slot_partials(
        fresh_rows[:, :, 0],
        fresh_rows[:, :, 1],
        fresh_rows[:, :, 2],
        new_usable,
        new_offset,
        slopes,
    )
    joined_max, joined_total, joined_out = merge_pair(
        (
            cache_max.reshape(cont_local, 2, head_count),
            cache_total.reshape(cont_local, 2, head_count),
            cache_out.reshape(cont_local, 2, head_count, HD),
        ),
        new_part,
    )
    attended = (
        (joined_out / joined_total[..., None])
        .astype(jnp.bfloat16)
        .reshape(row_total, head_count * HD)
    )
    head_term = jnp.dot(attended, out_weight, preferred_element_type=jnp.float32)
    hidden_one = (
        residual.reshape(row_total, share).astype(jnp.float32)
        + lax.psum_scatter(head_term, "col", scatter_dimension=1, tiled=True)
        + out_bias.astype(jnp.float32)
    )
    gain_part = lax.dynamic_slice_in_dim(mlp_gain, col_index * share, share)
    shift_part = lax.dynamic_slice_in_dim(mlp_shift, col_index * share, share)
    sum_one, sum_two = lax.psum(
        (jnp.sum(hidden_one, axis=1), jnp.sum(hidden_one * hidden_one, axis=1)), ("row", "col")
    )
    normed_a = lax.all_gather(
        normalize(hidden_one, sum_one, sum_two, gain_part, shift_part), "col", axis=1, tiled=True
    )
    up_share = lax.psum_scatter(
        jnp.dot(normed_a, up_weight, preferred_element_type=jnp.float32),
        "row",
        scatter_dimension=1,
        tiled=True,
    )
    hidden_two = jax.nn.gelu(up_share + up_bias.astype(jnp.float32), approximate=True).astype(
        jnp.bfloat16
    )
    down_sum = jnp.dot(
        lax.all_gather(hidden_two, "row", axis=1, tiled=True),
        down_weight,
        preferred_element_type=jnp.float32,
    )
    down_share = lax.psum_scatter(
        down_sum.astype(jnp.bfloat16), "col", scatter_dimension=1, tiled=True
    ).astype(jnp.float32)
    layer_out = (hidden_one + down_share + down_bias.astype(jnp.float32)).astype(jnp.bfloat16)
    out_wide = layer_out.astype(jnp.float32)
    gain_part = lax.dynamic_slice_in_dim(next_gain, col_index * share, share)
    shift_part = lax.dynamic_slice_in_dim(next_shift, col_index * share, share)
    score_part = lax.dynamic_slice_in_dim(score_weight, col_index * share, share).astype(
        jnp.float32
    )
    sum_one, sum_two, score_sum = lax.psum(
        (
            jnp.sum(out_wide, axis=1),
            jnp.sum(out_wide * out_wide, axis=1),
            jnp.sum(out_wide * score_part, axis=1),
        ),
        ("row", "col"),
    )
    normed_b = lax.all_gather(
        normalize(out_wide, sum_one, sum_two, gain_part, shift_part), "col", axis=1, tiled=True
    )
    qkv_share = lax.psum_scatter(
        jnp.dot(normed_b, qkv_weight, preferred_element_type=jnp.float32).astype(jnp.bfloat16),
        "row",
        scatter_dimension=1,
        tiled=True,
    ).astype(jnp.float32)
    projected_next = (qkv_share + qkv_bias.astype(jnp.float32)).astype(jnp.bfloat16)
    return (
        layer_out.reshape(cont_local, 2, share),
        score_sum.reshape(cont_local, 2),
        projected_next.reshape(cont_local, 2, qkv_share.shape[1]),
    )


empty_floor = -1e20
STAT = 8
LANES = 128


def columns_to_tile(columns):
    rows = columns[0].shape[0]
    lane = lax.broadcasted_iota(jnp.int32, (rows, LANES), 1)
    wide = jnp.zeros((rows, LANES), jnp.float32)
    for k, column in enumerate(columns):
        wide = jnp.where(lane == k, column, wide)
    if rows < LANES:
        wide = jnp.concatenate([wide, jnp.zeros((LANES - rows, LANES), jnp.float32)], axis=0)
    return jnp.transpose(wide)[:STAT]


def tile_to_columns(tile, rows):
    have = tile.shape[0]
    if have < LANES:
        tile = jnp.concatenate([tile, jnp.zeros((LANES - have, LANES), jnp.float32)], axis=0)
    return jnp.transpose(tile)[:rows]


def layer_kernel(
    sizes,
    prefix_item,
    tail_item,
    prefix_length,
    tail_length,
    tail_row,
    fresh,
    residual,
    vectors,
    prefix_hbm,
    tail_hbm,
    out_hbm,
    up_hbm,
    down_hbm,
    qkv_hbm,
    layer_ref,
    stat_ref,
    proj_ref,
    prefix_v,
    tail_v,
    out_w,
    up_w,
    down_w,
    qkv_w,
    q_buf,
    p_stage,
    l_stage,
    p_buf,
    l_buf,
    att,
    a_stage,
    a_buf,
    hidden,
    x_buf,
    s_buf,
    normed,
    u_own,
    u_stage,
    u_buf,
    acc,
    d_stage,
    d_buf,
    y_buf,
    t_buf,
    z_stage,
    z_buf,
    page_sem,
    w_sem,
    q_send,
    q_recv,
    p_send,
    p_recv,
    l_send,
    l_recv,
    a_send,
    a_recv,
    x_send,
    x_recv,
    s_send,
    s_recv,
    u_send,
    u_recv,
    d_send,
    d_recv,
    y_send,
    y_recv,
    t_send,
    t_recv,
    z_send,
    z_recv,
):
    G, R, C = sizes["pages"], sizes["row"], sizes["col"]
    f32, bf16, i32 = jnp.float32, jnp.bfloat16, jnp.int32
    me = lax.axis_index("pages")
    row = lax.axis_index("row")
    col = lax.axis_index("col")
    rows = residual.shape[0]
    share = residual.shape[1]
    width = C * share
    heads = fresh.shape[2] // HD
    slots, _, tokens, _ = prefix_v.shape
    tails = tail_v.shape[0]
    pair_pages, pair_tails = slots // G, tails // G
    chunks, _, chunk = u_buf.shape
    pieces, _, piece = z_buf.shape

    def group_at(i):
        return lax.rem(lax.div(me, 2) + lax.div(i, 2), G // 2) * 2 + lax.rem(me + i, 2)

    def row_at(k):
        return lax.rem(row + k, R)

    def col_at(k):
        return lax.rem(col + k, C)

    def remote(src, dst, send_sem, recv_sem, target):
        return pltpu.make_async_remote_copy(
            src_ref=src,
            dst_ref=dst,
            send_sem=send_sem,
            recv_sem=recv_sem,
            device_id=target,
            device_id_type=pl.DeviceIdType.MESH,
        )

    def prefix_copy(g):
        part = pl.ds(g * pair_pages, pair_pages)
        return pltpu.make_async_copy(prefix_hbm.at[part], prefix_v.at[part], page_sem.at[g, 0])

    def tail_copy(g):
        part = pl.ds(g * pair_tails, pair_tails)
        return pltpu.make_async_copy(tail_hbm.at[part], tail_v.at[part], page_sem.at[g, 1])

    weight_copies = [
        pltpu.make_async_copy(src, dst, w_sem.at[k])
        for k, (src, dst) in enumerate(
            ((out_hbm, out_w), (up_hbm, up_w), (down_hbm, down_w), (qkv_hbm, qkv_w))
        )
    ]

    for i in range(G):
        prefix_copy(group_at(jnp.int32(i))).start()
        tail_copy(group_at(jnp.int32(i))).start()

    barrier = pltpu.get_barrier_semaphore()
    met = 0
    for i in range(G):
        for k in range(R):
            if i or k:
                met += 1
                pl.semaphore_signal(
                    barrier,
                    inc=1,
                    device_id=(group_at(jnp.int32(i)), row_at(k), col),
                    device_id_type=pl.DeviceIdType.MESH,
                )
    for k in range(R):
        for j in range(1, C):
            met += 1
            pl.semaphore_signal(
                barrier,
                inc=1,
                device_id=(me, row_at(k), col_at(j)),
                device_id_type=pl.DeviceIdType.MESH,
            )
    pl.semaphore_wait(barrier, met)

    sends = []
    for i in range(1, G):
        copy = remote(
            fresh.at[0],
            q_buf.at[me],
            q_send.at[i],
            q_recv.at[me],
            (group_at(jnp.int32(i)), row, col),
        )
        copy.start()
        sends.append(copy)
    q_buf[me] = fresh[0]
    for copy in weight_copies:
        copy.start()

    row_id = lax.broadcasted_iota(i32, (rows, 1), 0)
    step = lax.rem(row_id, 2)
    row_cont = lax.div(row_id, 2)
    contract_last = (((1,), (1,)), ((), ()))
    scale = 1.0 / math.sqrt(HD)

    def slope_row(h, size):
        index = jnp.full((1, size), col * heads + h + 1, i32).astype(f32)
        return jnp.exp(index * (-8.0 / H * math.log(2.0)))

    def attend(i):
        g = group_at(i)
        prefix_copy(g).wait()
        tail_copy(g).wait()
        cont = g * lax.div(rows, 2) + row_cont
        prompt_of_row = lax.div(cont, CONT)
        spots = lax.broadcasted_iota(i32, (rows, tail_row.shape[1]), 1)
        own_tail = jnp.sum(
            jnp.where(spots == cont, tail_row[...], 0.0), axis=1, keepdims=True
        )
        query_off = own_tail + step.astype(f32)

        lane = lax.broadcasted_iota(i32, (1, pair_pages * tokens), 1)
        slot = lax.div(lane, tokens)
        token = lax.rem(lane, tokens) + row * tokens
        owner = jnp.zeros_like(lane)
        place = jnp.zeros_like(lane)
        length = jnp.zeros_like(lane)
        for k in range(pair_pages):
            item = prefix_item[me * slots + g * pair_pages + k]
            prompt = lax.div(item, MAXPAGES)
            hit = slot == k
            owner = jnp.where(hit, prompt, owner)
            place = jnp.where(hit, (item - prompt * MAXPAGES) * PAGE, place)
            length = jnp.where(hit, prefix_length[prompt], length)
        place = place + token
        gap = (place - length).astype(f32)
        open_prompt = jnp.where(place < length, owner, -1)
        prefix_gap = jnp.where(open_prompt == prompt_of_row, gap - query_off, masked_score)

        lane = lax.broadcasted_iota(i32, (1, pair_tails * tokens), 1)
        slot = lax.div(lane, tokens)
        token = lax.rem(lane, tokens) + row * tokens
        owner = jnp.zeros_like(lane)
        length = jnp.zeros_like(lane)
        for k in range(pair_tails):
            item = tail_item[me * tails + g * pair_tails + k]
            hit = slot == k
            owner = jnp.where(hit, item, owner)
            length = jnp.where(hit, tail_length[item], length)
        gap = (token - length).astype(f32)
        open_cont = jnp.where(token < length, owner, -1)
        tail_gap = jnp.where(open_cont == cont, gap - step.astype(f32), masked_score)

        pre = pl.ds(g * pair_pages, pair_pages)
        tai = pl.ds(g * pair_tails, pair_tails)
        levels = []
        for h in range(heads):
            hs = slice(h * HD, (h + 1) * HD)
            query = q_buf[g, :, hs]
            keys = prefix_v[pre, 0, :, hs].reshape(pair_pages * tokens, HD)
            tail_keys = tail_v[tai, 0, :, hs].reshape(pair_tails * tokens, HD)
            s_one = (
                lax.dot_general(query, keys, contract_last, preferred_element_type=f32) * scale
                + slope_row(h, pair_pages * tokens) * prefix_gap
            )
            s_two = (
                lax.dot_general(query, tail_keys, contract_last, preferred_element_type=f32)
                * scale
                + slope_row(h, pair_tails * tokens) * tail_gap
            )
            top = jnp.maximum(
                jnp.max(s_one, axis=1, keepdims=True), jnp.max(s_two, axis=1, keepdims=True)
            )
            top = jnp.maximum(top, empty_floor)
            w_one = jnp.exp(s_one - top)
            w_two = jnp.exp(s_two - top)
            total = jnp.sum(w_one, axis=1, keepdims=True) + jnp.sum(w_two, axis=1, keepdims=True)
            total = jnp.maximum(total, 1e-30)
            values = prefix_v[pre, 1, :, hs].reshape(pair_pages * tokens, HD)
            tail_values = tail_v[tai, 1, :, hs].reshape(pair_tails * tokens, HD)
            out = jnp.dot(w_one.astype(bf16), values, preferred_element_type=f32) + jnp.dot(
                w_two.astype(bf16), tail_values, preferred_element_type=f32
            )
            p_stage[g, :, hs] = (out / total).astype(bf16)
            levels.append(top + jnp.log(total))
        l_stage[g] = columns_to_tile(levels)

    def partial_copies(i, k):
        g = group_at(i)
        target = (g, row_at(k), col)
        return (
            remote(
                p_stage.at[g], p_buf.at[me, row], p_send.at[g, k], p_recv.at[me, row], target
            ),
            remote(
                l_stage.at[g], l_buf.at[me, row], l_send.at[g, k], l_recv.at[me, row], target
            ),
        )

    def partial_arrivals(i, k):
        g, r = group_at(i), row_at(k)
        return (
            remote(p_stage.at[g], p_buf.at[g, r], p_send.at[g, k], p_recv.at[g, r], (g, r, col)),
            remote(l_stage.at[g], l_buf.at[g, r], l_send.at[g, k], l_recv.at[g, r], (g, r, col)),
        )

    attend(jnp.int32(0))
    for k in range(1, R):
        for copy in partial_copies(jnp.int32(0), k):
            copy.start()
    p_buf[me, row] = p_stage[me]
    l_buf[me, row] = l_stage[me]

    def next_group(i, carry):
        g = group_at(i)
        remote(fresh.at[0], q_buf.at[g], q_send.at[i], q_recv.at[g], (g, row, col)).wait_recv()
        attend(i)
        for k in range(R):
            for copy in partial_copies(i, k):
                copy.start()
        return carry

    lax.fori_loop(1, G, next_group, 0)

    key_id = lax.broadcasted_iota(i32, (rows, rows), 1)
    new_ok = jnp.logical_and(lax.div(key_id, 2) == row_cont, lax.rem(key_id, 2) <= step)
    new_gap = jnp.where(new_ok, (lax.rem(key_id, 2) - step).astype(f32), masked_score)
    levels, new_outs = [], []
    for h in range(heads):
        hs = slice(h * HD, (h + 1) * HD)
        scores = (
            lax.dot_general(
                fresh[0, :, hs], fresh[1, :, hs], contract_last, preferred_element_type=f32
            )
            * scale
            + slope_row(h, rows) * new_gap
        )
        top = jnp.max(scores, axis=1, keepdims=True)
        weights = jnp.exp(scores - top)
        total = jnp.sum(weights, axis=1, keepdims=True)
        new_outs.append(
            jnp.dot(weights.astype(bf16), fresh[2, :, hs], preferred_element_type=f32) / total
        )
        levels.append(top + jnp.log(total))
    new_level = columns_to_tile(levels)

    for i in range(G):
        for k in range(R):
            if i or k:
                for copy in partial_arrivals(jnp.int32(i), k):
                    copy.wait_recv()

    peers = [l_buf[g, r] for g in range(G) for r in range(R)] + [new_level]
    peak = peers[0]
    for level in peers[1:]:
        peak = jnp.maximum(peak, level)
    shares = [jnp.exp(level - peak) for level in peers]
    total = shares[0]
    for part in shares[1:]:
        total = total + part
    scaled = [part / total for part in shares]
    groups_of_tiles = [
        tile_to_columns(jnp.concatenate(scaled[at : at + LANES // STAT], axis=0), rows)
        for at in range(0, len(scaled), LANES // STAT)
    ]

    def weight_of(peer, h):
        block, spot = divmod(peer, LANES // STAT)
        at = spot * STAT + h
        return groups_of_tiles[block][:, at : at + 1]

    for h in range(heads):
        hs = slice(h * HD, (h + 1) * HD)
        joined = weight_of(G * R, h) * new_outs[h]
        for g in range(G):
            for r in range(R):
                joined = joined + weight_of(g * R + r, h) * p_buf[g, r, :, hs].astype(f32)
        att[:, hs] = joined.astype(bf16)

    def share_of(k):
        return pl.ds(pl.multiple_of(col_at(k) * share, LANES), share)

    weight_copies[0].wait()
    for k in range(1, C):
        t = col_at(k)
        a_stage[k] = jnp.dot(
            att[...], out_w[:, share_of(k)], preferred_element_type=f32
        ).astype(bf16)
        copy = remote(a_stage.at[k], a_buf.at[col], a_send.at[k], a_recv.at[col], (me, row, t))
        copy.start()
        sends.append(copy)
    vec = {}
    at = 0
    for name, size in (
        ("out_bias", share),
        ("down_bias", share),
        ("mlp_gain", width),
        ("mlp_shift", width),
        ("next_gain", width),
        ("next_shift", width),
        ("score_weight", width),
        ("up_bias", chunks * chunk // R),
        ("qkv_bias", pieces * piece),
    ):
        vec[name] = (at, size)
        at += size

    def vector(name, start=0, size=None):
        base, full = vec[name]
        return vectors[:, base + start : base + start + (full if size is None else size)]

    total = (
        jnp.dot(att[...], out_w[:, share_of(0)], preferred_element_type=f32)
        + residual[...].astype(f32)
        + vector("out_bias")
    )
    for k in range(1, C):
        src = col_at(C - k)
        remote(
            a_stage.at[k], a_buf.at[src], a_send.at[k], a_recv.at[src], (me, row, src)
        ).wait_recv()
        total = total + a_buf[src].astype(f32)
    hidden[...] = total

    def gather(own, tile, wide_buf, wide_send, wide_recv, small_buf, small_send, small_recv):
        small_buf[row, col] = tile
        wide_buf[col] = own
        for k in range(R):
            for j in range(C):
                if k or j:
                    copy = remote(
                        small_buf.at[row, col],
                        small_buf.at[row, col],
                        small_send.at[k, j],
                        small_recv.at[row, col],
                        (me, row_at(k), col_at(j)),
                    )
                    copy.start()
                    sends.append(copy)
        for j in range(1, C):
            copy = remote(
                wide_buf.at[col],
                wide_buf.at[col],
                wide_send.at[j],
                wide_recv.at[col],
                (me, row, col_at(j)),
            )
            copy.start()
            sends.append(copy)
        for k in range(R):
            for j in range(C):
                if k or j:
                    r, c = row_at(k), col_at(j)
                    remote(
                        small_buf.at[row, col],
                        small_buf.at[r, c],
                        small_send.at[k, j],
                        small_recv.at[r, c],
                        (me, r, c),
                    ).wait_recv()
        sums = small_buf[0, 0]
        for k in range(1, R * C):
            sums = sums + small_buf[k // C, k % C]
        for j in range(1, C):
            c = col_at(j)
            remote(
                wide_buf.at[col], wide_buf.at[c], wide_send.at[j], wide_recv.at[c], (me, row, c)
            ).wait_recv()
        return sums

    def norm_into(sums, wide_buf, gain, shift):
        columns = tile_to_columns(sums, rows)
        center = columns[:, 0:1] / D
        spread = columns[:, 1:2] / D - center * center
        factor = lax.rsqrt(spread + norm_eps)
        for c in range(C):
            normed[:, c * share : (c + 1) * share] = (
                (wide_buf[c].astype(f32) - center) * factor * vector(gain, c * share, share)
                + vector(shift, c * share, share)
            ).astype(bf16)

    sums = gather(
        total.astype(bf16),
        columns_to_tile(
            [
                jnp.sum(total, axis=1, keepdims=True),
                jnp.sum(total * total, axis=1, keepdims=True),
            ]
        ),
        x_buf,
        x_send,
        x_recv,
        s_buf,
        s_send,
        s_recv,
    )
    norm_into(sums, x_buf, "mlp_gain", "mlp_shift")

    partner = (me, row_at(1), col)
    weight_copies[1].wait()
    per_row = chunks // R
    for n in range(chunks):
        part = jnp.dot(
            normed[...], up_w[:, n * chunk : (n + 1) * chunk], preferred_element_type=f32
        )
        mine = jnp.where(jnp.full((1, chunk), row, i32) == n // per_row, 1.0, 0.0)
        part = part + mine * vector("up_bias", (n % per_row) * chunk, chunk)
        u_own[n] = part
        u_stage[n] = part.astype(bf16)
        copy = remote(u_stage.at[n], u_buf.at[n], u_send.at[n], u_recv.at[n], partner)
        copy.start()
        sends.append(copy)

    weight_copies[2].wait()
    last = chunks - 1
    for n in range(chunks):
        remote(u_stage.at[n], u_buf.at[n], u_send.at[n], u_recv.at[n], partner).wait_recv()
        v = u_own[n] + u_buf[n].astype(f32)
        gelu = (0.5 * v * (1.0 + jnp.tanh(0.7978845608 * (v + 0.044715 * (v * v * v))))).astype(
            bf16
        )
        if n < last:
            term = jnp.dot(
                gelu, down_w[n * chunk : (n + 1) * chunk, :], preferred_element_type=f32
            )
            acc[...] = term if n == 0 else acc[...] + term

    def down_for(k):
        return acc[:, share_of(k)] + jnp.dot(
            gelu, down_w[last * chunk :, share_of(k)], preferred_element_type=f32
        )

    for k in range(1, C):
        d_stage[k] = down_for(k).astype(bf16)
        copy = remote(
            d_stage.at[k], d_buf.at[col], d_send.at[k], d_recv.at[col], (me, row, col_at(k))
        )
        copy.start()
        sends.append(copy)
    total = down_for(0) + hidden[...] + vector("down_bias")
    for k in range(1, C):
        src = col_at(C - k)
        remote(
            d_stage.at[k], d_buf.at[src], d_send.at[k], d_recv.at[src], (me, row, src)
        ).wait_recv()
        total = total + d_buf[src].astype(f32)
    layer_out = total.astype(bf16)
    layer_ref[...] = layer_out
    wide = layer_out.astype(f32)
    base = vec["score_weight"][0]
    score_part = vectors[:, pl.ds(pl.multiple_of(base + col * share, LANES), share)]
    sums = gather(
        layer_out,
        columns_to_tile(
            [
                jnp.sum(wide, axis=1, keepdims=True),
                jnp.sum(wide * wide, axis=1, keepdims=True),
                jnp.sum(wide * score_part, axis=1, keepdims=True),
            ]
        ),
        y_buf,
        y_send,
        y_recv,
        t_buf,
        t_send,
        t_recv,
    )
    stat_ref[...] = sums
    norm_into(sums, y_buf, "next_gain", "next_shift")

    weight_copies[3].wait()
    half = pieces * piece

    def qkv_piece(r, n):
        at = pl.ds(pl.multiple_of(r * half + n * piece, LANES), piece)
        return jnp.dot(normed[...], qkv_w[:, at], preferred_element_type=f32)

    for n in range(pieces):
        z_stage[n] = qkv_piece(row_at(1), n).astype(bf16)
        copy = remote(z_stage.at[n], z_buf.at[n], z_send.at[n], z_recv.at[n], partner)
        copy.start()
        sends.append(copy)
    for n in range(pieces):
        own = qkv_piece(row, n) + vector("qkv_bias", n * piece, piece)
        remote(z_stage.at[n], z_buf.at[n], z_send.at[n], z_recv.at[n], partner).wait_recv()
        proj_ref[:, n * piece : (n + 1) * piece] = (own + z_buf[n].astype(f32)).astype(bf16)

    for copy in sends:
        copy.wait_send()
    for i in range(G):
        for k in range(R):
            if i or k:
                for copy in partial_copies(jnp.int32(i), k):
                    copy.wait_send()


def fused_shards(
    sizes,
    residual,
    fresh_qkv,
    prefix_pages,
    tail_pages,
    prefix_item,
    tail_item,
    prefix_length,
    tail_length,
    out_weight,
    out_bias,
    mlp_gain,
    mlp_shift,
    up_weight,
    up_bias,
    down_weight,
    down_bias,
    next_gain,
    next_shift,
    score_weight,
    qkv_weight,
    qkv_bias,
):
    G, R, C = sizes["pages"], sizes["row"], sizes["col"]
    f32, bf16 = jnp.float32, jnp.bfloat16
    cont_local, _, share = residual.shape
    rows = cont_local * 2
    head_width = fresh_qkv.shape[3]
    ff_local = up_weight.shape[1]
    out_local = qkv_bias.shape[0]
    chunk = ff_local // 4
    piece = out_local // 2
    vectors = jnp.concatenate(
        [
            out_bias,
            down_bias,
            mlp_gain,
            mlp_shift,
            next_gain,
            next_shift,
            score_weight,
            up_bias,
            qkv_bias,
        ]
    ).astype(f32)[None, :]
    fresh = fresh_qkv.reshape(rows, 3, head_width).transpose(1, 0, 2)
    vmem = pl.BlockSpec(memory_space=pltpu.VMEM)
    smem = pl.BlockSpec(memory_space=pltpu.SMEM)
    anywhere = pl.BlockSpec(memory_space=pl.ANY)
    dma = pltpu.SemaphoreType.DMA
    layer_out, stats, projected = pl.pallas_call(
        lambda *refs: layer_kernel(sizes, *refs),
        out_shape=(
            jax.ShapeDtypeStruct((rows, share), bf16),
            jax.ShapeDtypeStruct((STAT, LANES), f32),
            jax.ShapeDtypeStruct((rows, out_local), bf16),
        ),
        in_specs=[smem] * 4 + [vmem] * 4 + [anywhere] * 6,
        out_specs=(vmem, vmem, vmem),
        scratch_shapes=[
            pltpu.VMEM(prefix_pages.shape, bf16),
            pltpu.VMEM(tail_pages.shape, bf16),
            pltpu.VMEM(out_weight.shape, bf16),
            pltpu.VMEM(up_weight.shape, bf16),
            pltpu.VMEM(down_weight.shape, bf16),
            pltpu.VMEM(qkv_weight.shape, bf16),
            pltpu.VMEM((G, rows, head_width), bf16),
            pltpu.VMEM((G, rows, head_width), bf16),
            pltpu.VMEM((G, STAT, LANES), f32),
            pltpu.VMEM((G, R, rows, head_width), bf16),
            pltpu.VMEM((G, R, STAT, LANES), f32),
            pltpu.VMEM((rows, head_width), bf16),
            pltpu.VMEM((C, rows, share), bf16),
            pltpu.VMEM((C, rows, share), bf16),
            pltpu.VMEM((rows, share), f32),
            pltpu.VMEM((C, rows, share), bf16),
            pltpu.VMEM((R, C, STAT, LANES), f32),
            pltpu.VMEM((rows, C * share), bf16),
            pltpu.VMEM((ff_local // chunk, rows, chunk), f32),
            pltpu.VMEM((ff_local // chunk, rows, chunk), bf16),
            pltpu.VMEM((ff_local // chunk, rows, chunk), bf16),
            pltpu.VMEM((rows, C * share), f32),
            pltpu.VMEM((C, rows, share), bf16),
            pltpu.VMEM((C, rows, share), bf16),
            pltpu.VMEM((C, rows, share), bf16),
            pltpu.VMEM((R, C, STAT, LANES), f32),
            pltpu.VMEM((out_local // piece, rows, piece), bf16),
            pltpu.VMEM((out_local // piece, rows, piece), bf16),
            dma((G, 2)),
            dma((4,)),
            dma((G,)),
            dma((G,)),
            dma((G, R)),
            dma((G, R)),
            dma((G, R)),
            dma((G, R)),
            dma((C,)),
            dma((C,)),
            dma((C,)),
            dma((C,)),
            dma((R, C)),
            dma((R, C)),
            dma((ff_local // chunk,)),
            dma((ff_local // chunk,)),
            dma((C,)),
            dma((C,)),
            dma((C,)),
            dma((C,)),
            dma((R, C)),
            dma((R, C)),
            dma((out_local // piece,)),
            dma((out_local // piece,)),
        ],
        compiler_params=pltpu.CompilerParams(
            collective_id=0, has_side_effects=True, vmem_limit_bytes=48 * 1024 * 1024
        ),
        name="fused_layer",
    )(
        prefix_item,
        tail_item,
        prefix_length,
        tail_length,
        tail_length.astype(f32)[None, :],
        fresh,
        residual.reshape(rows, share),
        vectors,
        prefix_pages,
        tail_pages,
        out_weight,
        up_weight,
        down_weight,
        qkv_weight,
    )
    return (
        layer_out.reshape(cont_local, 2, share),
        stats[2, :rows].reshape(cont_local, 2),
        projected.reshape(cont_local, 2, out_local),
    )


def shards(residual, fresh_qkv, prefix_pages, *others):
    sizes = {axis: lax.axis_size(axis) for axis in ("pages", "row", "col")}
    share, tokens = residual.shape[2], prefix_pages.shape[2]
    if sizes["row"] == 2 and sizes["pages"] % 2 == 0 and share % LANES == 0 and tokens % 16 == 0:
        return fused_shards(sizes, residual, fresh_qkv, prefix_pages, *others)
    return plain_shards(residual, fresh_qkv, prefix_pages, *others)


def solution(mesh):
    in_specs = (
        P("pages", None, ("row", "col")),
        P("pages", None, None, "col"),
        P("pages", None, "row", "col"),
        P("pages", None, "row", "col"),
        P(),
        P(),
        P(),
        P(),
        P("col", "row"),
        P(("row", "col")),
        P("row"),
        P("row"),
        P("row", "col"),
        P(("col", "row")),
        P("col", "row"),
        P(("row", "col")),
        P("row"),
        P("row"),
        P("row"),
        P("row", "col"),
        P(("col", "row")),
    )
    out_specs = (
        P("pages", None, ("row", "col")),
        P("pages", None),
        P("pages", None, ("col", "row")),
    )
    return jax.shard_map(shards, mesh=mesh, in_specs=in_specs, out_specs=out_specs, check_vma=False)
```

```python
import math

import jax
import jax.numpy as jnp
from jax import lax
from jax.experimental import pallas as pl
from jax.experimental.pallas import tpu as pltpu
from jax.sharding import PartitionSpec as P

D = 2048
H = 16
HD = 128
PAGE = 128
MAXPAGES = 8
CONT = 16


masked_score = -1e30
norm_eps = 1e-05


def combined_all(shard, axis, combine):
    everything = jax.tree.map(lambda part: lax.all_gather(part, axis), shard)
    first = jax.tree.map(lambda part: part[0], everything)

    def step(k, so_far):
        return combine(so_far, jax.tree.map(lambda part: part[k], everything))

    return lax.fori_loop(1, lax.axis_size(axis), step, first)


def head_slopes(first_head, how_many):
    head_index = first_head + jnp.arange(how_many, dtype=jnp.int32)
    return jnp.exp2(-8.0 * (head_index + 1).astype(jnp.float32) / H)


def slot_partials(queries, page_keys, page_values, usable, offset, slopes):
    scores = jnp.einsum(
        "sqhd,skhd->sqhk", queries, page_keys, preferred_element_type=jnp.float32
    ) / math.sqrt(HD)
    scores = scores + slopes[None, None, :, None] * offset[:, :, None, :]
    usable_full = usable[:, :, None, :]
    scores = jnp.where(usable_full, scores, masked_score)
    maxima = jnp.max(scores, axis=3)
    weights = jnp.where(usable_full, jnp.exp(scores - maxima[..., None]), 0.0)
    totals = jnp.sum(weights, axis=3)
    outputs = jnp.einsum(
        "sqhk,skhd->sqhd", weights, page_values.astype(jnp.float32), precision=lax.Precision.HIGHEST
    )
    return (maxima, totals, outputs)


def merge_pair(left_part, right_part):
    left_max, left_total, left_out = left_part
    right_max, right_total, right_out = right_part
    joined = jnp.maximum(left_max, right_max)
    left_scale = jnp.exp(left_max - joined)
    right_scale = jnp.exp(right_max - joined)
    return (
        joined,
        left_scale * left_total + right_scale * right_total,
        left_scale[..., None] * left_out + right_scale[..., None] * right_out,
    )


def fold_sources(maxima, totals, outputs):
    joined = jnp.max(maxima, axis=0)
    rescale = jnp.exp(maxima - joined[None])
    return (
        joined,
        jnp.sum(rescale * totals, axis=0),
        jnp.sum(rescale[..., None] * outputs, axis=0),
    )


def cache_partials(
    queries,
    page_block,
    page_item,
    tail_block,
    tail_owner,
    prefix_length,
    tail_length,
    row_index,
    slopes,
):
    cont_count = queries.shape[0]
    prompts = cont_count // CONT
    head_count = queries.shape[2]
    slot_count = page_block.shape[0]
    tokens = page_block.shape[2]
    token_index = row_index * tokens + jnp.arange(tokens, dtype=jnp.int32)
    step_index = jnp.arange(2, dtype=jnp.int32)
    slot_prompt = page_item // MAXPAGES
    slot_page = page_item % MAXPAGES
    by_prompt = queries.reshape(prompts, CONT * 2, head_count, HD)
    key_pos = slot_page[:, None] * PAGE + token_index[None, :]
    slot_len = prefix_length[slot_prompt]
    slot_tails = tail_length.reshape(prompts, CONT)[slot_prompt]
    query_pos = (
        slot_len[:, None, None] + slot_tails[:, :, None] + step_index[None, None, :]
    ).reshape(slot_count, CONT * 2)
    offset = (key_pos[:, None, :] - query_pos[:, :, None]).astype(jnp.float32)
    usable = jnp.broadcast_to((key_pos < slot_len[:, None])[:, None, :], offset.shape)
    page_keys = page_block[:, 0].reshape(slot_count, tokens, head_count, HD)
    page_values = page_block[:, 1].reshape(slot_count, tokens, head_count, HD)
    maxima, totals, outputs = slot_partials(
        by_prompt[slot_prompt], page_keys, page_values, usable, offset, slopes
    )
    prompt_max = (
        jnp.full((prompts, CONT * 2, head_count), masked_score, jnp.float32)
        .at[slot_prompt]
        .max(maxima)
    )
    rescale = jnp.exp(maxima - prompt_max[slot_prompt])
    prompt_total = (
        jnp.zeros((prompts, CONT * 2, head_count), jnp.float32)
        .at[slot_prompt]
        .add(rescale * totals)
    )
    prompt_out = (
        jnp.zeros((prompts, CONT * 2, head_count, HD), jnp.float32)
        .at[slot_prompt]
        .add(rescale[..., None] * outputs)
    )
    prefix_part = (
        prompt_max.reshape(cont_count, 2, head_count),
        prompt_total.reshape(cont_count, 2, head_count),
        prompt_out.reshape(cont_count, 2, head_count, HD),
    )
    tail_count = tail_block.shape[0]
    tail_lens = tail_length[tail_owner]
    tail_usable = jnp.broadcast_to(
        (token_index[None, :] < tail_lens[:, None])[:, None, :], (tail_count, 2, tokens)
    )
    tail_offset = (
        token_index[None, None, :] - tail_lens[:, None, None] - step_index[None, :, None]
    ).astype(jnp.float32)
    tail_keys = tail_block[:, 0].reshape(tail_count, tokens, head_count, HD)
    tail_values = tail_block[:, 1].reshape(tail_count, tokens, head_count, HD)
    tail_max, tail_total, tail_out = slot_partials(
        queries[tail_owner], tail_keys, tail_values, tail_usable, tail_offset, slopes
    )
    cont_max = (
        jnp.full((cont_count, 2, head_count), masked_score, jnp.float32)
        .at[tail_owner]
        .set(tail_max)
    )
    cont_total = jnp.zeros((cont_count, 2, head_count), jnp.float32).at[tail_owner].set(tail_total)
    cont_out = jnp.zeros((cont_count, 2, head_count, HD), jnp.float32).at[tail_owner].set(tail_out)
    return merge_pair(prefix_part, (cont_max, cont_total, cont_out))


def normalize(values, sum_one, sum_two, gain, shift):
    center = sum_one / D
    spread = sum_two / D - center * center
    return (
        (values - center[:, None])
        * lax.rsqrt(spread + norm_eps)[:, None]
        * gain.astype(jnp.float32)
        + shift.astype(jnp.float32)
    ).astype(jnp.bfloat16)


def plain_shards(
    residual,
    fresh_qkv,
    prefix_pages,
    tail_pages,
    prefix_item,
    tail_item,
    prefix_length,
    tail_length,
    out_weight,
    out_bias,
    mlp_gain,
    mlp_shift,
    up_weight,
    up_bias,
    down_weight,
    down_bias,
    next_gain,
    next_shift,
    score_weight,
    qkv_weight,
    qkv_bias,
):
    group_index = lax.axis_index("pages")
    row_index = lax.axis_index("row")
    col_index = lax.axis_index("col")
    group_count = lax.axis_size("pages")
    cont_local = residual.shape[0]
    row_total = cont_local * 2
    share = residual.shape[2]
    head_count = fresh_qkv.shape[3] // HD
    slopes = head_slopes(col_index * head_count, head_count)
    fresh_rows = fresh_qkv.reshape(cont_local, 2, 3, head_count, HD)
    slot_count = prefix_pages.shape[0]
    tail_slots = tail_pages.shape[0]
    everyone = lax.all_gather(fresh_qkv[:, :, 0], "pages", axis=0, tiled=True)
    page_item = lax.dynamic_slice_in_dim(prefix_item, group_index * slot_count, slot_count)
    tail_owner = lax.dynamic_slice_in_dim(tail_item, group_index * tail_slots, tail_slots)
    maxima, totals, outputs = cache_partials(
        everyone.reshape(everyone.shape[0], 2, head_count, HD),
        prefix_pages,
        page_item,
        tail_pages,
        tail_owner,
        prefix_length,
        tail_length,
        row_index,
        slopes,
    )
    maxima, totals, outputs = (
        lax.all_to_all(
            maxima.reshape(group_count, row_total, head_count),
            "pages",
            split_axis=0,
            concat_axis=0,
            tiled=True,
        ),
        lax.all_to_all(
            totals.reshape(group_count, row_total, head_count),
            "pages",
            split_axis=0,
            concat_axis=0,
            tiled=True,
        ),
        lax.all_to_all(
            outputs.reshape(group_count, row_total, head_count, HD),
            "pages",
            split_axis=0,
            concat_axis=0,
            tiled=True,
        ),
    )
    cache_max, cache_total, cache_out = fold_sources(maxima, totals, outputs)
    cache_max, cache_total, cache_out = combined_all(
        (cache_max, cache_total, cache_out), "row", merge_pair
    )
    step_index = jnp.arange(2, dtype=jnp.int32)
    new_usable = jnp.broadcast_to(
        (step_index[None, :] <= step_index[:, None])[None], (cont_local, 2, 2)
    )
    new_offset = jnp.broadcast_to(
        (step_index[None, :] - step_index[:, None]).astype(jnp.float32)[None], (cont_local, 2, 2)
    )
    new_part = slot_partials(
        fresh_rows[:, :, 0],
        fresh_rows[:, :, 1],
        fresh_rows[:, :, 2],
        new_usable,
        new_offset,
        slopes,
    )
    joined_max, joined_total, joined_out = merge_pair(
        (
            cache_max.reshape(cont_local, 2, head_count),
            cache_total.reshape(cont_local, 2, head_count),
            cache_out.reshape(cont_local, 2, head_count, HD),
        ),
        new_part,
    )
    attended = (
        (joined_out / joined_total[..., None])
        .astype(jnp.bfloat16)
        .reshape(row_total, head_count * HD)
    )
    head_term = jnp.dot(attended, out_weight, preferred_element_type=jnp.float32)
    hidden_one = (
        residual.reshape(row_total, share).astype(jnp.float32)
        + lax.psum_scatter(head_term, "col", scatter_dimension=1, tiled=True)
        + out_bias.astype(jnp.float32)
    )
    gain_part = lax.dynamic_slice_in_dim(mlp_gain, col_index * share, share)
    shift_part = lax.dynamic_slice_in_dim(mlp_shift, col_index * share, share)
    sum_one, sum_two = lax.psum(
        (jnp.sum(hidden_one, axis=1), jnp.sum(hidden_one * hidden_one, axis=1)), ("row", "col")
    )
    normed_a = lax.all_gather(
        normalize(hidden_one, sum_one, sum_two, gain_part, shift_part), "col", axis=1, tiled=True
    )
    up_share = lax.psum_scatter(
        jnp.dot(normed_a, up_weight, preferred_element_type=jnp.float32),
        "row",
        scatter_dimension=1,
        tiled=True,
    )
    hidden_two = jax.nn.gelu(up_share + up_bias.astype(jnp.float32), approximate=True).astype(
        jnp.bfloat16
    )
    down_sum = jnp.dot(
        lax.all_gather(hidden_two, "row", axis=1, tiled=True),
        down_weight,
        preferred_element_type=jnp.float32,
    )
    down_share = lax.psum_scatter(
        down_sum.astype(jnp.bfloat16), "col", scatter_dimension=1, tiled=True
    ).astype(jnp.float32)
    layer_out = (hidden_one + down_share + down_bias.astype(jnp.float32)).astype(jnp.bfloat16)
    out_wide = layer_out.astype(jnp.float32)
    gain_part = lax.dynamic_slice_in_dim(next_gain, col_index * share, share)
    shift_part = lax.dynamic_slice_in_dim(next_shift, col_index * share, share)
    score_part = lax.dynamic_slice_in_dim(score_weight, col_index * share, share).astype(
        jnp.float32
    )
    sum_one, sum_two, score_sum = lax.psum(
        (
            jnp.sum(out_wide, axis=1),
            jnp.sum(out_wide * out_wide, axis=1),
            jnp.sum(out_wide * score_part, axis=1),
        ),
        ("row", "col"),
    )
    normed_b = lax.all_gather(
        normalize(out_wide, sum_one, sum_two, gain_part, shift_part), "col", axis=1, tiled=True
    )
    qkv_share = lax.psum_scatter(
        jnp.dot(normed_b, qkv_weight, preferred_element_type=jnp.float32).astype(jnp.bfloat16),
        "row",
        scatter_dimension=1,
        tiled=True,
    ).astype(jnp.float32)
    projected_next = (qkv_share + qkv_bias.astype(jnp.float32)).astype(jnp.bfloat16)
    return (
        layer_out.reshape(cont_local, 2, share),
        score_sum.reshape(cont_local, 2),
        projected_next.reshape(cont_local, 2, qkv_share.shape[1]),
    )


empty_floor = -1e20
STAT = 8
LANES = 128


def columns_to_tile(columns):
    rows = columns[0].shape[0]
    lane = lax.broadcasted_iota(jnp.int32, (rows, LANES), 1)
    wide = jnp.zeros((rows, LANES), jnp.float32)
    for k, column in enumerate(columns):
        wide = jnp.where(lane == k, column, wide)
    if rows < LANES:
        wide = jnp.concatenate([wide, jnp.zeros((LANES - rows, LANES), jnp.float32)], axis=0)
    return jnp.transpose(wide)[:STAT]


def tile_to_columns(tile, rows):
    have = tile.shape[0]
    if have < LANES:
        tile = jnp.concatenate([tile, jnp.zeros((LANES - have, LANES), jnp.float32)], axis=0)
    return jnp.transpose(tile)[:rows]


def layer_kernel(
    sizes,
    item_hbm,
    owner_hbm,
    length_hbm,
    span_hbm,
    fresh_hbm,
    residual_hbm,
    out_bias_hbm,
    mlp_gain_hbm,
    mlp_shift_hbm,
    up_bias_hbm,
    down_bias_hbm,
    next_gain_hbm,
    next_shift_hbm,
    score_hbm,
    qkv_bias_hbm,
    prefix_hbm,
    tail_hbm,
    out_hbm,
    up_hbm,
    down_hbm,
    qkv_hbm,
    layer_ref,
    stat_ref,
    proj_ref,
    prefix_item,
    tail_item,
    prefix_length,
    tail_length,
    tail_row,
    fresh_raw,
    residual,
    out_bias,
    mlp_gain,
    mlp_shift,
    up_bias,
    down_bias,
    next_gain,
    next_shift,
    score_weight,
    qkv_bias,
    fresh,
    new_out,
    small_sem,
    prefix_v,
    tail_v,
    out_w,
    up_w,
    down_w,
    qkv_w,
    q_buf,
    p_stage,
    l_stage,
    p_buf,
    l_buf,
    att,
    a_stage,
    a_buf,
    hidden,
    x_buf,
    s_buf,
    normed,
    u_own,
    u_stage,
    u_buf,
    acc,
    d_stage,
    d_buf,
    y_buf,
    t_buf,
    z_stage,
    z_buf,
    page_sem,
    w_sem,
    q_send,
    q_recv,
    p_send,
    p_recv,
    l_send,
    l_recv,
    a_send,
    a_recv,
    x_send,
    x_recv,
    s_send,
    s_recv,
    u_send,
    u_recv,
    d_send,
    d_recv,
    y_send,
    y_recv,
    t_send,
    t_recv,
    z_send,
    z_recv,
):
    G, R, C = sizes["pages"], sizes["row"], sizes["col"]
    f32, bf16, i32 = jnp.float32, jnp.bfloat16, jnp.int32
    me = lax.axis_index("pages")
    row = lax.axis_index("row")
    col = lax.axis_index("col")
    rows = fresh.shape[1]
    share = residual.shape[2]
    width = C * share
    heads = fresh.shape[2] // HD
    slots, _, tokens, _ = prefix_v.shape
    tails = tail_v.shape[0]
    pair_pages, pair_tails = slots // G, tails // G
    chunks, _, chunk = u_buf.shape
    pieces, _, piece = z_buf.shape

    def group_at(i):
        if isinstance(i, int) and i == 0:
            return me
        j = lax.rem(jnp.int32(i), G - 1) + 1
        return lax.rem(lax.div(me, 2) + lax.div(j, 2), G // 2) * 2 + lax.rem(me + j, 2)

    def row_at(k):
        return lax.rem(row + k, R)

    def col_at(k):
        return lax.rem(col + k, C)

    def remote(src, dst, send_sem, recv_sem, target):
        return pltpu.make_async_remote_copy(
            src_ref=src,
            dst_ref=dst,
            send_sem=send_sem,
            recv_sem=recv_sem,
            device_id=target,
            device_id_type=pl.DeviceIdType.MESH,
        )

    def prefix_copy(g):
        part = pl.ds(g * pair_pages, pair_pages)
        return pltpu.make_async_copy(prefix_hbm.at[part], prefix_v.at[part], page_sem.at[g, 0])

    def tail_copy(g):
        part = pl.ds(g * pair_tails, pair_tails)
        return pltpu.make_async_copy(tail_hbm.at[part], tail_v.at[part], page_sem.at[g, 1])

    weight_copies = [
        pltpu.make_async_copy(src, dst, w_sem.at[k])
        for k, (src, dst) in enumerate(
            ((out_hbm, out_w), (up_hbm, up_w), (down_hbm, down_w), (qkv_hbm, qkv_w))
        )
    ]

    small_pairs = (
        (fresh_hbm, fresh_raw),
        (item_hbm, prefix_item),
        (owner_hbm, tail_item),
        (length_hbm, prefix_length),
        (span_hbm, tail_length),
        (span_hbm, tail_row),
        (residual_hbm, residual),
        (out_bias_hbm, out_bias),
        (mlp_gain_hbm, mlp_gain),
        (mlp_shift_hbm, mlp_shift),
        (up_bias_hbm, up_bias),
        (down_bias_hbm, down_bias),
        (next_gain_hbm, next_gain),
        (next_shift_hbm, next_shift),
        (score_hbm, score_weight),
        (qkv_bias_hbm, qkv_bias),
    )
    small_copies = [
        pltpu.make_async_copy(src, dst, small_sem.at[k])
        for k, (src, dst) in enumerate(small_pairs)
    ]

    barrier = pltpu.get_barrier_semaphore()
    met = 0
    for i in range(G):
        for k in range(R):
            if i or k:
                met += 1
                pl.semaphore_signal(
                    barrier,
                    inc=1,
                    device_id=(group_at(i), row_at(k), col),
                    device_id_type=pl.DeviceIdType.MESH,
                )
    for k in range(R):
        for j in range(1, C):
            met += 1
            pl.semaphore_signal(
                barrier,
                inc=1,
                device_id=(me, row_at(k), col_at(j)),
                device_id_type=pl.DeviceIdType.MESH,
            )
    for copy in small_copies[:6]:
        copy.start()
    for i in range(G):
        prefix_copy(group_at(i)).start()
        tail_copy(group_at(i)).start()
    for copy in small_copies[6:]:
        copy.start()

    row_id = lax.broadcasted_iota(i32, (rows, 1), 0)
    step = lax.rem(row_id, 2)
    row_cont = lax.div(row_id, 2)
    contract_last = (((1,), (1,)), ((), ()))
    scale = 1.0 / math.sqrt(HD)

    def slope_row(h, size):
        index = jnp.full((1, size), col * heads + h + 1, i32).astype(f32)
        return jnp.exp(index * (-8.0 / H * math.log(2.0)))

    small_copies[0].wait()
    for part in range(3):
        fresh[part] = fresh_raw[:, part].reshape(rows, heads * HD)
    q_buf[me] = fresh[0]
    key_id = lax.broadcasted_iota(i32, (rows, rows), 1)
    new_ok = jnp.logical_and(lax.div(key_id, 2) == row_cont, lax.rem(key_id, 2) <= step)
    new_gap = jnp.where(new_ok, (lax.rem(key_id, 2) - step).astype(f32), masked_score)
    levels = []
    for h in range(heads):
        hs = slice(h * HD, (h + 1) * HD)
        scores = (
            lax.dot_general(
                fresh[0, :, hs], fresh[1, :, hs], contract_last, preferred_element_type=f32
            )
            * scale
            + slope_row(h, rows) * new_gap
        )
        top = jnp.max(scores, axis=1, keepdims=True)
        weights = jnp.exp(scores - top)
        total = jnp.sum(weights, axis=1, keepdims=True)
        new_out[:, hs] = (
            jnp.dot(weights.astype(bf16), fresh[2, :, hs], preferred_element_type=f32) / total
        )
        levels.append(top + jnp.log(total))
    new_level = columns_to_tile(levels)

    pl.semaphore_wait(barrier, met)

    sends = []
    for i in range(1, G):
        copy = remote(
            fresh.at[0],
            q_buf.at[me],
            q_send.at[i],
            q_recv.at[me],
            (group_at(i), row, col),
        )
        copy.start()
        sends.append(copy)
    for copy in weight_copies:
        copy.start()
    for copy in small_copies[1:]:
        copy.wait()

    def attend(i):
        g = group_at(i)
        prefix_copy(g).wait()
        tail_copy(g).wait()
        cont = g * lax.div(rows, 2) + row_cont
        prompt_of_row = lax.div(cont, CONT)
        spots = lax.broadcasted_iota(i32, (rows, tail_row.shape[0]), 1)
        tail_spans = tail_row[...].reshape(1, tail_row.shape[0]).astype(f32)
        own_tail = jnp.sum(
            jnp.where(spots == cont, tail_spans, 0.0), axis=1, keepdims=True
        )
        query_off = own_tail + step.astype(f32)

        lane = lax.broadcasted_iota(i32, (1, pair_pages * tokens), 1)
        slot = lax.div(lane, tokens)
        token = lax.rem(lane, tokens) + row * tokens
        owner = jnp.zeros_like(lane)
        place = jnp.zeros_like(lane)
        length = jnp.zeros_like(lane)
        for k in range(pair_pages):
            item = prefix_item[me * slots + g * pair_pages + k]
            prompt = lax.div(item, MAXPAGES)
            hit = slot == k
            owner = jnp.where(hit, prompt, owner)
            place = jnp.where(hit, (item - prompt * MAXPAGES) * PAGE, place)
            length = jnp.where(hit, prefix_length[prompt], length)
        place = place + token
        gap = (place - length).astype(f32)
        open_prompt = jnp.where(place < length, owner, -1)
        prefix_gap = jnp.where(open_prompt == prompt_of_row, gap - query_off, masked_score)

        lane = lax.broadcasted_iota(i32, (1, pair_tails * tokens), 1)
        slot = lax.div(lane, tokens)
        token = lax.rem(lane, tokens) + row * tokens
        owner = jnp.zeros_like(lane)
        length = jnp.zeros_like(lane)
        for k in range(pair_tails):
            item = tail_item[me * tails + g * pair_tails + k]
            hit = slot == k
            owner = jnp.where(hit, item, owner)
            length = jnp.where(hit, tail_length[item], length)
        gap = (token - length).astype(f32)
        open_cont = jnp.where(token < length, owner, -1)
        tail_gap = jnp.where(open_cont == cont, gap - step.astype(f32), masked_score)

        pre = pl.ds(g * pair_pages, pair_pages)
        tai = pl.ds(g * pair_tails, pair_tails)
        levels = []
        for h in range(heads):
            hs = slice(h * HD, (h + 1) * HD)
            query = q_buf[g, :, hs]
            keys = prefix_v[pre, 0, :, hs].reshape(pair_pages * tokens, HD)
            tail_keys = tail_v[tai, 0, :, hs].reshape(pair_tails * tokens, HD)
            s_one = (
                lax.dot_general(query, keys, contract_last, preferred_element_type=f32) * scale
                + slope_row(h, pair_pages * tokens) * prefix_gap
            )
            s_two = (
                lax.dot_general(query, tail_keys, contract_last, preferred_element_type=f32)
                * scale
                + slope_row(h, pair_tails * tokens) * tail_gap
            )
            top = jnp.maximum(
                jnp.max(s_one, axis=1, keepdims=True), jnp.max(s_two, axis=1, keepdims=True)
            )
            top = jnp.maximum(top, empty_floor)
            w_one = jnp.exp(s_one - top)
            w_two = jnp.exp(s_two - top)
            total = jnp.sum(w_one, axis=1, keepdims=True) + jnp.sum(w_two, axis=1, keepdims=True)
            total = jnp.maximum(total, 1e-30)
            values = prefix_v[pre, 1, :, hs].reshape(pair_pages * tokens, HD)
            tail_values = tail_v[tai, 1, :, hs].reshape(pair_tails * tokens, HD)
            out = jnp.dot(w_one.astype(bf16), values, preferred_element_type=f32) + jnp.dot(
                w_two.astype(bf16), tail_values, preferred_element_type=f32
            )
            p_stage[g, :, hs] = (out / total).astype(bf16)
            levels.append(top + jnp.log(total))
        l_stage[g] = columns_to_tile(levels)

    def partial_copies(i, k):
        g = group_at(i)
        target = (g, row_at(k), col)
        return (
            remote(
                p_stage.at[g], p_buf.at[me, row], p_send.at[g, k], p_recv.at[me, row], target
            ),
            remote(
                l_stage.at[g], l_buf.at[me, row], l_send.at[g, k], l_recv.at[me, row], target
            ),
        )

    def partial_arrivals(i, k):
        g, r = group_at(i), row_at(k)
        return (
            remote(p_stage.at[g], p_buf.at[g, r], p_send.at[g, k], p_recv.at[g, r], (g, r, col)),
            remote(l_stage.at[g], l_buf.at[g, r], l_send.at[g, k], l_recv.at[g, r], (g, r, col)),
        )

    attend(0)
    for k in range(1, R):
        for copy in partial_copies(0, k):
            copy.start()
    p_buf[me, row] = p_stage[me]
    l_buf[me, row] = l_stage[me]

    def next_group(i, carry):
        g = group_at(i)
        remote(fresh.at[0], q_buf.at[g], q_send.at[i], q_recv.at[g], (g, row, col)).wait_recv()
        attend(i)
        for k in range(R):
            for copy in partial_copies(i, k):
                copy.start()
        return carry

    lax.fori_loop(1, G, next_group, 0)

    for i in range(G):
        for k in range(R):
            if i or k:
                for copy in partial_arrivals(i, k):
                    copy.wait_recv()

    peers = [l_buf[g, r] for g in range(G) for r in range(R)] + [new_level]
    peak = peers[0]
    for level in peers[1:]:
        peak = jnp.maximum(peak, level)
    shares = [jnp.exp(level - peak) for level in peers]
    total = shares[0]
    for part in shares[1:]:
        total = total + part
    scaled = [part / total for part in shares]
    groups_of_tiles = [
        tile_to_columns(jnp.concatenate(scaled[at : at + LANES // STAT], axis=0), rows)
        for at in range(0, len(scaled), LANES // STAT)
    ]

    def weight_of(peer, h):
        block, spot = divmod(peer, LANES // STAT)
        at = spot * STAT + h
        return groups_of_tiles[block][:, at : at + 1]

    for h in range(heads):
        hs = slice(h * HD, (h + 1) * HD)
        joined = weight_of(G * R, h) * new_out[:, hs]
        for g in range(G):
            for r in range(R):
                joined = joined + weight_of(g * R + r, h) * p_buf[g, r, :, hs].astype(f32)
        att[:, hs] = joined.astype(bf16)

    def share_of(k):
        return pl.ds(pl.multiple_of(col_at(k) * share, LANES), share)

    weight_copies[0].wait()
    for k in range(1, C):
        t = col_at(k)
        a_stage[k] = jnp.dot(
            att[...], out_w[:, share_of(k)], preferred_element_type=f32
        ).astype(bf16)
        copy = remote(a_stage.at[k], a_buf.at[col], a_send.at[k], a_recv.at[col], (me, row, t))
        copy.start()
        sends.append(copy)

    def vector(ref):
        return ref[...].astype(f32).reshape(1, ref.shape[0])

    total = (
        jnp.dot(att[...], out_w[:, share_of(0)], preferred_element_type=f32)
        + residual[...].astype(f32).reshape(rows, share)
        + vector(out_bias)
    )
    for k in range(1, C):
        src = col_at(C - k)
        remote(
            a_stage.at[k], a_buf.at[src], a_send.at[k], a_recv.at[src], (me, row, src)
        ).wait_recv()
        total = total + a_buf[src].astype(f32)
    hidden[...] = total

    def gather(own, tile, wide_buf, wide_send, wide_recv, small_buf, small_send, small_recv):
        small_buf[row, col] = tile
        wide_buf[col] = own
        for k in range(R):
            for j in range(C):
                if k or j:
                    copy = remote(
                        small_buf.at[row, col],
                        small_buf.at[row, col],
                        small_send.at[k, j],
                        small_recv.at[row, col],
                        (me, row_at(k), col_at(j)),
                    )
                    copy.start()
                    sends.append(copy)
        for j in range(1, C):
            copy = remote(
                wide_buf.at[col],
                wide_buf.at[col],
                wide_send.at[j],
                wide_recv.at[col],
                (me, row, col_at(j)),
            )
            copy.start()
            sends.append(copy)
        for k in range(R):
            for j in range(C):
                if k or j:
                    r, c = row_at(k), col_at(j)
                    remote(
                        small_buf.at[row, col],
                        small_buf.at[r, c],
                        small_send.at[k, j],
                        small_recv.at[r, c],
                        (me, r, c),
                    ).wait_recv()
        sums = small_buf[0, 0]
        for k in range(1, R * C):
            sums = sums + small_buf[k // C, k % C]
        for j in range(1, C):
            c = col_at(j)
            remote(
                wide_buf.at[col], wide_buf.at[c], wide_send.at[j], wide_recv.at[c], (me, row, c)
            ).wait_recv()
        return sums

    def norm_into(sums, wide_buf, gain, shift):
        columns = tile_to_columns(sums, rows)
        center = columns[:, 0:1] / D
        spread = columns[:, 1:2] / D - center * center
        factor = lax.rsqrt(spread + norm_eps)
        gains, shifts = vector(gain), vector(shift)
        for c in range(C):
            at = slice(c * share, (c + 1) * share)
            normed[:, at] = (
                (wide_buf[c].astype(f32) - center) * factor * gains[:, at] + shifts[:, at]
            ).astype(bf16)

    sums = gather(
        total.astype(bf16),
        columns_to_tile(
            [
                jnp.sum(total, axis=1, keepdims=True),
                jnp.sum(total * total, axis=1, keepdims=True),
            ]
        ),
        x_buf,
        x_send,
        x_recv,
        s_buf,
        s_send,
        s_recv,
    )
    norm_into(sums, x_buf, mlp_gain, mlp_shift)

    partner = (me, row_at(1), col)
    weight_copies[1].wait()
    per_row = chunks // R
    up_shift = vector(up_bias)
    for n in range(chunks):
        part = jnp.dot(
            normed[...], up_w[:, n * chunk : (n + 1) * chunk], preferred_element_type=f32
        )
        mine = jnp.where(jnp.full((1, chunk), row, i32) == n // per_row, 1.0, 0.0)
        part = part + mine * up_shift[:, (n % per_row) * chunk : (n % per_row + 1) * chunk]
        u_own[n] = part
        u_stage[n] = part.astype(bf16)
        copy = remote(u_stage.at[n], u_buf.at[n], u_send.at[n], u_recv.at[n], partner)
        copy.start()
        sends.append(copy)

    weight_copies[2].wait()
    last = chunks - 1
    for n in range(chunks):
        remote(u_stage.at[n], u_buf.at[n], u_send.at[n], u_recv.at[n], partner).wait_recv()
        v = u_own[n] + u_buf[n].astype(f32)
        gelu = (0.5 * v * (1.0 + jnp.tanh(0.7978845608 * (v + 0.044715 * (v * v * v))))).astype(
            bf16
        )
        if n < last:
            term = jnp.dot(
                gelu, down_w[n * chunk : (n + 1) * chunk, :], preferred_element_type=f32
            )
            acc[...] = term if n == 0 else acc[...] + term

    def down_for(k):
        return acc[:, share_of(k)] + jnp.dot(
            gelu, down_w[last * chunk :, share_of(k)], preferred_element_type=f32
        )

    for k in range(1, C):
        d_stage[k] = down_for(k).astype(bf16)
        copy = remote(
            d_stage.at[k], d_buf.at[col], d_send.at[k], d_recv.at[col], (me, row, col_at(k))
        )
        copy.start()
        sends.append(copy)
    total = down_for(0) + hidden[...] + vector(down_bias)
    for k in range(1, C):
        src = col_at(C - k)
        remote(
            d_stage.at[k], d_buf.at[src], d_send.at[k], d_recv.at[src], (me, row, src)
        ).wait_recv()
        total = total + d_buf[src].astype(f32)
    layer_out = total.astype(bf16)
    layer_ref[...] = layer_out
    wide = layer_out.astype(f32)
    scores = vector(score_weight)
    score_part = scores[:, :share]
    for c in range(1, C):
        score_part = jnp.where(
            jnp.full((1, share), col, i32) == c, scores[:, c * share : (c + 1) * share], score_part
        )
    sums = gather(
        layer_out,
        columns_to_tile(
            [
                jnp.sum(wide, axis=1, keepdims=True),
                jnp.sum(wide * wide, axis=1, keepdims=True),
                jnp.sum(wide * score_part, axis=1, keepdims=True),
            ]
        ),
        y_buf,
        y_send,
        y_recv,
        t_buf,
        t_send,
        t_recv,
    )
    stat_ref[...] = sums
    norm_into(sums, y_buf, next_gain, next_shift)

    weight_copies[3].wait()
    half = pieces * piece
    qkv_shift = vector(qkv_bias)

    def qkv_piece(r, n):
        at = pl.ds(pl.multiple_of(r * half + n * piece, LANES), piece)
        return jnp.dot(normed[...], qkv_w[:, at], preferred_element_type=f32)

    for n in range(pieces):
        z_stage[n] = qkv_piece(row_at(1), n).astype(bf16)
        copy = remote(z_stage.at[n], z_buf.at[n], z_send.at[n], z_recv.at[n], partner)
        copy.start()
        sends.append(copy)
    for n in range(pieces):
        own = qkv_piece(row, n) + qkv_shift[:, n * piece : (n + 1) * piece]
        remote(z_stage.at[n], z_buf.at[n], z_send.at[n], z_recv.at[n], partner).wait_recv()
        proj_ref[:, n * piece : (n + 1) * piece] = (own + z_buf[n].astype(f32)).astype(bf16)

    for copy in sends:
        copy.wait_send()
    for i in range(G):
        for k in range(R):
            if i or k:
                for copy in partial_copies(i, k):
                    copy.wait_send()


def fused_shards(
    sizes,
    residual,
    fresh_qkv,
    prefix_pages,
    tail_pages,
    prefix_item,
    tail_item,
    prefix_length,
    tail_length,
    out_weight,
    out_bias,
    mlp_gain,
    mlp_shift,
    up_weight,
    up_bias,
    down_weight,
    down_bias,
    next_gain,
    next_shift,
    score_weight,
    qkv_weight,
    qkv_bias,
):
    G, R, C = sizes["pages"], sizes["row"], sizes["col"]
    f32, bf16 = jnp.float32, jnp.bfloat16
    cont_local, _, share = residual.shape
    rows = cont_local * 2
    head_width = fresh_qkv.shape[3]
    ff_local = up_weight.shape[1]
    out_local = qkv_bias.shape[0]
    chunk = ff_local // 4
    piece = out_local // 2
    fresh = fresh_qkv.transpose(0, 2, 1, 3)
    one_row = (out_bias, mlp_gain, mlp_shift, up_bias, down_bias)
    one_row = one_row + (next_gain, next_shift, score_weight, qkv_bias)
    vmem = pl.BlockSpec(memory_space=pltpu.VMEM)
    hbm = pl.BlockSpec(memory_space=pltpu.MemorySpace.HBM)
    dma = pltpu.SemaphoreType.DMA
    layer_out, stats, projected = pl.pallas_call(
        lambda *refs: layer_kernel(sizes, *refs),
        out_shape=(
            jax.ShapeDtypeStruct((rows, share), bf16),
            jax.ShapeDtypeStruct((STAT, LANES), f32),
            jax.ShapeDtypeStruct((rows, out_local), bf16),
        ),
        in_specs=[hbm] * (12 + len(one_row)),
        out_specs=(vmem, vmem, vmem),
        scratch_shapes=[
            pltpu.SMEM(prefix_item.shape, jnp.int32),
            pltpu.SMEM(tail_item.shape, jnp.int32),
            pltpu.SMEM(prefix_length.shape, jnp.int32),
            pltpu.SMEM(tail_length.shape, jnp.int32),
            pltpu.VMEM(tail_length.shape, jnp.int32),
            pltpu.VMEM(fresh.shape, bf16),
            pltpu.VMEM(residual.shape, bf16),
            *(pltpu.VMEM(v.shape, bf16) for v in one_row),
            pltpu.VMEM((3, rows, head_width), bf16),
            pltpu.VMEM((rows, head_width), f32),
            dma((7 + len(one_row),)),
            pltpu.VMEM(prefix_pages.shape, bf16),
            pltpu.VMEM(tail_pages.shape, bf16),
            pltpu.VMEM(out_weight.shape, bf16),
            pltpu.VMEM(up_weight.shape, bf16),
            pltpu.VMEM(down_weight.shape, bf16),
            pltpu.VMEM(qkv_weight.shape, bf16),
            pltpu.VMEM((G, rows, head_width), bf16),
            pltpu.VMEM((G, rows, head_width), bf16),
            pltpu.VMEM((G, STAT, LANES), f32),
            pltpu.VMEM((G, R, rows, head_width), bf16),
            pltpu.VMEM((G, R, STAT, LANES), f32),
            pltpu.VMEM((rows, head_width), bf16),
            pltpu.VMEM((C, rows, share), bf16),
            pltpu.VMEM((C, rows, share), bf16),
            pltpu.VMEM((rows, share), f32),
            pltpu.VMEM((C, rows, share), bf16),
            pltpu.VMEM((R, C, STAT, LANES), f32),
            pltpu.VMEM((rows, C * share), bf16),
            pltpu.VMEM((ff_local // chunk, rows, chunk), f32),
            pltpu.VMEM((ff_local // chunk, rows, chunk), bf16),
            pltpu.VMEM((ff_local // chunk, rows, chunk), bf16),
            pltpu.VMEM((rows, C * share), f32),
            pltpu.VMEM((C, rows, share), bf16),
            pltpu.VMEM((C, rows, share), bf16),
            pltpu.VMEM((C, rows, share), bf16),
            pltpu.VMEM((R, C, STAT, LANES), f32),
            pltpu.VMEM((out_local // piece, rows, piece), bf16),
            pltpu.VMEM((out_local // piece, rows, piece), bf16),
            dma((G, 2)),
            dma((4,)),
            dma((G,)),
            dma((G,)),
            dma((G, R)),
            dma((G, R)),
            dma((G, R)),
            dma((G, R)),
            dma((C,)),
            dma((C,)),
            dma((C,)),
            dma((C,)),
            dma((R, C)),
            dma((R, C)),
            dma((ff_local // chunk,)),
            dma((ff_local // chunk,)),
            dma((C,)),
            dma((C,)),
            dma((C,)),
            dma((C,)),
            dma((R, C)),
            dma((R, C)),
            dma((out_local // piece,)),
            dma((out_local // piece,)),
        ],
        compiler_params=pltpu.CompilerParams(
            collective_id=0, has_side_effects=True, vmem_limit_bytes=64 * 1024 * 1024
        ),
        name="fused_layer",
    )(
        prefix_item,
        tail_item,
        prefix_length,
        tail_length,
        fresh,
        residual,
        *one_row,
        prefix_pages,
        tail_pages,
        out_weight,
        up_weight,
        down_weight,
        qkv_weight,
    )
    return (
        layer_out.reshape(cont_local, 2, share),
        stats[2, :rows].reshape(cont_local, 2),
        projected.reshape(cont_local, 2, out_local),
    )


def shards(residual, fresh_qkv, prefix_pages, *others):
    sizes = {axis: lax.axis_size(axis) for axis in ("pages", "row", "col")}
    share, tokens = residual.shape[2], prefix_pages.shape[2]
    if sizes["row"] == 2 and sizes["pages"] % 2 == 0 and share % LANES == 0 and tokens % 16 == 0:
        return fused_shards(sizes, residual, fresh_qkv, prefix_pages, *others)
    return plain_shards(residual, fresh_qkv, prefix_pages, *others)


def solution(mesh):
    in_specs = (
        P("pages", None, ("row", "col")),
        P("pages", None, None, "col"),
        P("pages", None, "row", "col"),
        P("pages", None, "row", "col"),
        P(),
        P(),
        P(),
        P(),
        P("col", "row"),
        P(("row", "col")),
        P("row"),
        P("row"),
        P("row", "col"),
        P(("col", "row")),
        P("col", "row"),
        P(("row", "col")),
        P("row"),
        P("row"),
        P("row"),
        P("row", "col"),
        P(("col", "row")),
    )
    out_specs = (
        P("pages", None, ("row", "col")),
        P("pages", None),
        P("pages", None, ("col", "row")),
    )
    return jax.shard_map(shards, mesh=mesh, in_specs=in_specs, out_specs=out_specs, check_vma=False)
```

```python
import math

import jax
import jax.numpy as jnp
from jax import lax
from jax.experimental import pallas as pl
from jax.experimental.pallas import tpu as pltpu
from jax.sharding import PartitionSpec as P

D = 2048
H = 16
HD = 128
PAGE = 128
MAXPAGES = 8
CONT = 16


masked_score = -1e30
norm_eps = 1e-05


def combined_all(shard, axis, combine):
    everything = jax.tree.map(lambda part: lax.all_gather(part, axis), shard)
    first = jax.tree.map(lambda part: part[0], everything)

    def step(k, so_far):
        return combine(so_far, jax.tree.map(lambda part: part[k], everything))

    return lax.fori_loop(1, lax.axis_size(axis), step, first)


def head_slopes(first_head, how_many):
    head_index = first_head + jnp.arange(how_many, dtype=jnp.int32)
    return jnp.exp2(-8.0 * (head_index + 1).astype(jnp.float32) / H)


def slot_partials(queries, page_keys, page_values, usable, offset, slopes):
    scores = jnp.einsum(
        "sqhd,skhd->sqhk", queries, page_keys, preferred_element_type=jnp.float32
    ) / math.sqrt(HD)
    scores = scores + slopes[None, None, :, None] * offset[:, :, None, :]
    usable_full = usable[:, :, None, :]
    scores = jnp.where(usable_full, scores, masked_score)
    maxima = jnp.max(scores, axis=3)
    weights = jnp.where(usable_full, jnp.exp(scores - maxima[..., None]), 0.0)
    totals = jnp.sum(weights, axis=3)
    outputs = jnp.einsum(
        "sqhk,skhd->sqhd", weights, page_values.astype(jnp.float32), precision=lax.Precision.HIGHEST
    )
    return (maxima, totals, outputs)


def merge_pair(left_part, right_part):
    left_max, left_total, left_out = left_part
    right_max, right_total, right_out = right_part
    joined = jnp.maximum(left_max, right_max)
    left_scale = jnp.exp(left_max - joined)
    right_scale = jnp.exp(right_max - joined)
    return (
        joined,
        left_scale * left_total + right_scale * right_total,
        left_scale[..., None] * left_out + right_scale[..., None] * right_out,
    )


def fold_sources(maxima, totals, outputs):
    joined = jnp.max(maxima, axis=0)
    rescale = jnp.exp(maxima - joined[None])
    return (
        joined,
        jnp.sum(rescale * totals, axis=0),
        jnp.sum(rescale[..., None] * outputs, axis=0),
    )


def cache_partials(
    queries,
    page_block,
    page_item,
    tail_block,
    tail_owner,
    prefix_length,
    tail_length,
    row_index,
    slopes,
):
    cont_count = queries.shape[0]
    prompts = cont_count // CONT
    head_count = queries.shape[2]
    slot_count = page_block.shape[0]
    tokens = page_block.shape[2]
    token_index = row_index * tokens + jnp.arange(tokens, dtype=jnp.int32)
    step_index = jnp.arange(2, dtype=jnp.int32)
    slot_prompt = page_item // MAXPAGES
    slot_page = page_item % MAXPAGES
    by_prompt = queries.reshape(prompts, CONT * 2, head_count, HD)
    key_pos = slot_page[:, None] * PAGE + token_index[None, :]
    slot_len = prefix_length[slot_prompt]
    slot_tails = tail_length.reshape(prompts, CONT)[slot_prompt]
    query_pos = (
        slot_len[:, None, None] + slot_tails[:, :, None] + step_index[None, None, :]
    ).reshape(slot_count, CONT * 2)
    offset = (key_pos[:, None, :] - query_pos[:, :, None]).astype(jnp.float32)
    usable = jnp.broadcast_to((key_pos < slot_len[:, None])[:, None, :], offset.shape)
    page_keys = page_block[:, 0].reshape(slot_count, tokens, head_count, HD)
    page_values = page_block[:, 1].reshape(slot_count, tokens, head_count, HD)
    maxima, totals, outputs = slot_partials(
        by_prompt[slot_prompt], page_keys, page_values, usable, offset, slopes
    )
    prompt_max = (
        jnp.full((prompts, CONT * 2, head_count), masked_score, jnp.float32)
        .at[slot_prompt]
        .max(maxima)
    )
    rescale = jnp.exp(maxima - prompt_max[slot_prompt])
    prompt_total = (
        jnp.zeros((prompts, CONT * 2, head_count), jnp.float32)
        .at[slot_prompt]
        .add(rescale * totals)
    )
    prompt_out = (
        jnp.zeros((prompts, CONT * 2, head_count, HD), jnp.float32)
        .at[slot_prompt]
        .add(rescale[..., None] * outputs)
    )
    prefix_part = (
        prompt_max.reshape(cont_count, 2, head_count),
        prompt_total.reshape(cont_count, 2, head_count),
        prompt_out.reshape(cont_count, 2, head_count, HD),
    )
    tail_count = tail_block.shape[0]
    tail_lens = tail_length[tail_owner]
    tail_usable = jnp.broadcast_to(
        (token_index[None, :] < tail_lens[:, None])[:, None, :], (tail_count, 2, tokens)
    )
    tail_offset = (
        token_index[None, None, :] - tail_lens[:, None, None] - step_index[None, :, None]
    ).astype(jnp.float32)
    tail_keys = tail_block[:, 0].reshape(tail_count, tokens, head_count, HD)
    tail_values = tail_block[:, 1].reshape(tail_count, tokens, head_count, HD)
    tail_max, tail_total, tail_out = slot_partials(
        queries[tail_owner], tail_keys, tail_values, tail_usable, tail_offset, slopes
    )
    cont_max = (
        jnp.full((cont_count, 2, head_count), masked_score, jnp.float32)
        .at[tail_owner]
        .set(tail_max)
    )
    cont_total = jnp.zeros((cont_count, 2, head_count), jnp.float32).at[tail_owner].set(tail_total)
    cont_out = jnp.zeros((cont_count, 2, head_count, HD), jnp.float32).at[tail_owner].set(tail_out)
    return merge_pair(prefix_part, (cont_max, cont_total, cont_out))


def normalize(values, sum_one, sum_two, gain, shift):
    center = sum_one / D
    spread = sum_two / D - center * center
    return (
        (values - center[:, None])
        * lax.rsqrt(spread + norm_eps)[:, None]
        * gain.astype(jnp.float32)
        + shift.astype(jnp.float32)
    ).astype(jnp.bfloat16)


def plain_shards(
    residual,
    fresh_qkv,
    prefix_pages,
    tail_pages,
    prefix_item,
    tail_item,
    prefix_length,
    tail_length,
    out_weight,
    out_bias,
    mlp_gain,
    mlp_shift,
    up_weight,
    up_bias,
    down_weight,
    down_bias,
    next_gain,
    next_shift,
    score_weight,
    qkv_weight,
    qkv_bias,
):
    group_index = lax.axis_index("pages")
    row_index = lax.axis_index("row")
    col_index = lax.axis_index("col")
    group_count = lax.axis_size("pages")
    cont_local = residual.shape[0]
    row_total = cont_local * 2
    share = residual.shape[2]
    head_count = fresh_qkv.shape[3] // HD
    slopes = head_slopes(col_index * head_count, head_count)
    fresh_rows = fresh_qkv.reshape(cont_local, 2, 3, head_count, HD)
    slot_count = prefix_pages.shape[0]
    tail_slots = tail_pages.shape[0]
    everyone = lax.all_gather(fresh_qkv[:, :, 0], "pages", axis=0, tiled=True)
    page_item = lax.dynamic_slice_in_dim(prefix_item, group_index * slot_count, slot_count)
    tail_owner = lax.dynamic_slice_in_dim(tail_item, group_index * tail_slots, tail_slots)
    maxima, totals, outputs = cache_partials(
        everyone.reshape(everyone.shape[0], 2, head_count, HD),
        prefix_pages,
        page_item,
        tail_pages,
        tail_owner,
        prefix_length,
        tail_length,
        row_index,
        slopes,
    )
    maxima, totals, outputs = (
        lax.all_to_all(
            maxima.reshape(group_count, row_total, head_count),
            "pages",
            split_axis=0,
            concat_axis=0,
            tiled=True,
        ),
        lax.all_to_all(
            totals.reshape(group_count, row_total, head_count),
            "pages",
            split_axis=0,
            concat_axis=0,
            tiled=True,
        ),
        lax.all_to_all(
            outputs.reshape(group_count, row_total, head_count, HD),
            "pages",
            split_axis=0,
            concat_axis=0,
            tiled=True,
        ),
    )
    cache_max, cache_total, cache_out = fold_sources(maxima, totals, outputs)
    cache_max, cache_total, cache_out = combined_all(
        (cache_max, cache_total, cache_out), "row", merge_pair
    )
    step_index = jnp.arange(2, dtype=jnp.int32)
    new_usable = jnp.broadcast_to(
        (step_index[None, :] <= step_index[:, None])[None], (cont_local, 2, 2)
    )
    new_offset = jnp.broadcast_to(
        (step_index[None, :] - step_index[:, None]).astype(jnp.float32)[None], (cont_local, 2, 2)
    )
    new_part = slot_partials(
        fresh_rows[:, :, 0],
        fresh_rows[:, :, 1],
        fresh_rows[:, :, 2],
        new_usable,
        new_offset,
        slopes,
    )
    joined_max, joined_total, joined_out = merge_pair(
        (
            cache_max.reshape(cont_local, 2, head_count),
            cache_total.reshape(cont_local, 2, head_count),
            cache_out.reshape(cont_local, 2, head_count, HD),
        ),
        new_part,
    )
    attended = (
        (joined_out / joined_total[..., None])
        .astype(jnp.bfloat16)
        .reshape(row_total, head_count * HD)
    )
    head_term = jnp.dot(attended, out_weight, preferred_element_type=jnp.float32)
    hidden_one = (
        residual.reshape(row_total, share).astype(jnp.float32)
        + lax.psum_scatter(head_term, "col", scatter_dimension=1, tiled=True)
        + out_bias.astype(jnp.float32)
    )
    gain_part = lax.dynamic_slice_in_dim(mlp_gain, col_index * share, share)
    shift_part = lax.dynamic_slice_in_dim(mlp_shift, col_index * share, share)
    sum_one, sum_two = lax.psum(
        (jnp.sum(hidden_one, axis=1), jnp.sum(hidden_one * hidden_one, axis=1)), ("row", "col")
    )
    normed_a = lax.all_gather(
        normalize(hidden_one, sum_one, sum_two, gain_part, shift_part), "col", axis=1, tiled=True
    )
    up_share = lax.psum_scatter(
        jnp.dot(normed_a, up_weight, preferred_element_type=jnp.float32),
        "row",
        scatter_dimension=1,
        tiled=True,
    )
    hidden_two = jax.nn.gelu(up_share + up_bias.astype(jnp.float32), approximate=True).astype(
        jnp.bfloat16
    )
    down_sum = jnp.dot(
        lax.all_gather(hidden_two, "row", axis=1, tiled=True),
        down_weight,
        preferred_element_type=jnp.float32,
    )
    down_share = lax.psum_scatter(
        down_sum.astype(jnp.bfloat16), "col", scatter_dimension=1, tiled=True
    ).astype(jnp.float32)
    layer_out = (hidden_one + down_share + down_bias.astype(jnp.float32)).astype(jnp.bfloat16)
    out_wide = layer_out.astype(jnp.float32)
    gain_part = lax.dynamic_slice_in_dim(next_gain, col_index * share, share)
    shift_part = lax.dynamic_slice_in_dim(next_shift, col_index * share, share)
    score_part = lax.dynamic_slice_in_dim(score_weight, col_index * share, share).astype(
        jnp.float32
    )
    sum_one, sum_two, score_sum = lax.psum(
        (
            jnp.sum(out_wide, axis=1),
            jnp.sum(out_wide * out_wide, axis=1),
            jnp.sum(out_wide * score_part, axis=1),
        ),
        ("row", "col"),
    )
    normed_b = lax.all_gather(
        normalize(out_wide, sum_one, sum_two, gain_part, shift_part), "col", axis=1, tiled=True
    )
    qkv_share = lax.psum_scatter(
        jnp.dot(normed_b, qkv_weight, preferred_element_type=jnp.float32).astype(jnp.bfloat16),
        "row",
        scatter_dimension=1,
        tiled=True,
    ).astype(jnp.float32)
    projected_next = (qkv_share + qkv_bias.astype(jnp.float32)).astype(jnp.bfloat16)
    return (
        layer_out.reshape(cont_local, 2, share),
        score_sum.reshape(cont_local, 2),
        projected_next.reshape(cont_local, 2, qkv_share.shape[1]),
    )


empty_floor = -1e20
STAT = 8
LANES = 128


def columns_to_tile(columns):
    rows = columns[0].shape[0]
    lane = lax.broadcasted_iota(jnp.int32, (rows, LANES), 1)
    wide = jnp.zeros((rows, LANES), jnp.float32)
    for k, column in enumerate(columns):
        wide = jnp.where(lane == k, column, wide)
    if rows < LANES:
        wide = jnp.concatenate([wide, jnp.zeros((LANES - rows, LANES), jnp.float32)], axis=0)
    return jnp.transpose(wide)[:STAT]


def tile_to_columns(tile, rows):
    have = tile.shape[0]
    if have < LANES:
        tile = jnp.concatenate([tile, jnp.zeros((LANES - have, LANES), jnp.float32)], axis=0)
    return jnp.transpose(tile)[:rows]


def layer_kernel(
    sizes,
    item_hbm,
    owner_hbm,
    length_hbm,
    span_hbm,
    fresh_hbm,
    residual_hbm,
    out_bias_hbm,
    mlp_gain_hbm,
    mlp_shift_hbm,
    up_bias_hbm,
    down_bias_hbm,
    next_gain_hbm,
    next_shift_hbm,
    score_hbm,
    qkv_bias_hbm,
    prefix_hbm,
    tail_hbm,
    out_hbm,
    up_hbm,
    down_hbm,
    qkv_hbm,
    layer_ref,
    score_ref,
    proj_ref,
    prefix_item,
    tail_item,
    prefix_length,
    tail_length,
    tail_row,
    fresh_raw,
    residual,
    out_bias,
    mlp_gain,
    mlp_shift,
    up_bias,
    down_bias,
    next_gain,
    next_shift,
    score_weight,
    qkv_bias,
    fresh,
    new_out,
    small_sem,
    prefix_v,
    tail_v,
    out_w,
    up_w,
    down_w,
    qkv_w,
    q_buf,
    p_stage,
    l_stage,
    p_buf,
    l_buf,
    att,
    a_stage,
    a_buf,
    hidden,
    x_buf,
    s_buf,
    normed,
    u_own,
    u_stage,
    u_buf,
    acc,
    d_stage,
    d_buf,
    y_buf,
    t_buf,
    z_stage,
    z_buf,
    page_sem,
    w_sem,
    q_send,
    q_recv,
    p_send,
    p_recv,
    l_send,
    l_recv,
    a_send,
    a_recv,
    x_send,
    x_recv,
    s_send,
    s_recv,
    u_send,
    u_recv,
    d_send,
    d_recv,
    y_send,
    y_recv,
    t_send,
    t_recv,
    z_send,
    z_recv,
):
    G, R, C = sizes["pages"], sizes["row"], sizes["col"]
    f32, bf16, i32 = jnp.float32, jnp.bfloat16, jnp.int32
    me = lax.axis_index("pages")
    row = lax.axis_index("row")
    col = lax.axis_index("col")
    rows = fresh.shape[1]
    share = residual.shape[2]
    width = C * share
    heads = fresh.shape[2] // HD
    slots, _, tokens, _ = prefix_v.shape
    tails = tail_v.shape[0]
    pair_pages, pair_tails = slots // G, tails // G
    chunks, _, chunk = u_buf.shape
    pieces, _, piece = z_buf.shape

    def group_at(i):
        if isinstance(i, int) and i == 0:
            return me
        j = lax.rem(jnp.int32(i), G - 1) + 1
        return lax.rem(lax.div(me, 2) + lax.div(j, 2), G // 2) * 2 + lax.rem(me + j, 2)

    def row_at(k):
        return lax.rem(row + k, R)

    def col_at(k):
        return lax.rem(col + k, C)

    def remote(src, dst, send_sem, recv_sem, target):
        return pltpu.make_async_remote_copy(
            src_ref=src,
            dst_ref=dst,
            send_sem=send_sem,
            recv_sem=recv_sem,
            device_id=target,
            device_id_type=pl.DeviceIdType.MESH,
        )

    def prefix_copy(g):
        part = pl.ds(g * pair_pages, pair_pages)
        return pltpu.make_async_copy(prefix_hbm.at[part], prefix_v.at[part], page_sem.at[g, 0])

    def tail_copy(g):
        part = pl.ds(g * pair_tails, pair_tails)
        return pltpu.make_async_copy(tail_hbm.at[part], tail_v.at[part], page_sem.at[g, 1])

    weight_copies = [
        pltpu.make_async_copy(src, dst, w_sem.at[k])
        for k, (src, dst) in enumerate(
            ((out_hbm, out_w), (up_hbm, up_w), (down_hbm, down_w), (qkv_hbm, qkv_w))
        )
    ]

    small_pairs = (
        (fresh_hbm, fresh_raw),
        (item_hbm, prefix_item),
        (owner_hbm, tail_item),
        (length_hbm, prefix_length),
        (span_hbm, tail_length),
        (span_hbm, tail_row),
        (residual_hbm, residual),
        (out_bias_hbm, out_bias),
        (mlp_gain_hbm, mlp_gain),
        (mlp_shift_hbm, mlp_shift),
        (up_bias_hbm, up_bias),
        (down_bias_hbm, down_bias),
        (next_gain_hbm, next_gain),
        (next_shift_hbm, next_shift),
        (score_hbm, score_weight),
        (qkv_bias_hbm, qkv_bias),
    )
    small_copies = [
        pltpu.make_async_copy(src, dst, small_sem.at[k])
        for k, (src, dst) in enumerate(small_pairs)
    ]

    barrier = pltpu.get_barrier_semaphore()
    met = 0
    for i in range(G):
        for k in range(R):
            if i or k:
                met += 1
                pl.semaphore_signal(
                    barrier,
                    inc=1,
                    device_id=(group_at(i), row_at(k), col),
                    device_id_type=pl.DeviceIdType.MESH,
                )
    for k in range(R):
        for j in range(1, C):
            met += 1
            pl.semaphore_signal(
                barrier,
                inc=1,
                device_id=(me, row_at(k), col_at(j)),
                device_id_type=pl.DeviceIdType.MESH,
            )
    for copy in small_copies[:6]:
        copy.start()
    for i in range(G):
        prefix_copy(group_at(i)).start()
        tail_copy(group_at(i)).start()
    for copy in small_copies[6:]:
        copy.start()

    row_id = lax.broadcasted_iota(i32, (rows, 1), 0)
    step = lax.rem(row_id, 2)
    row_cont = lax.div(row_id, 2)
    contract_last = (((1,), (1,)), ((), ()))
    scale = 1.0 / math.sqrt(HD)

    def slope_row(h, size):
        index = jnp.full((1, size), col * heads + h + 1, i32).astype(f32)
        return jnp.exp(index * (-8.0 / H * math.log(2.0)))

    small_copies[0].wait()
    for part in range(3):
        fresh[part] = fresh_raw[:, part].reshape(rows, heads * HD)
    q_buf[me] = fresh[0]
    key_id = lax.broadcasted_iota(i32, (rows, rows), 1)
    new_ok = jnp.logical_and(lax.div(key_id, 2) == row_cont, lax.rem(key_id, 2) <= step)
    new_gap = jnp.where(new_ok, (lax.rem(key_id, 2) - step).astype(f32), masked_score)
    levels = []
    for h in range(heads):
        hs = slice(h * HD, (h + 1) * HD)
        scores = (
            lax.dot_general(
                fresh[0, :, hs], fresh[1, :, hs], contract_last, preferred_element_type=f32
            )
            * scale
            + slope_row(h, rows) * new_gap
        )
        top = jnp.max(scores, axis=1, keepdims=True)
        weights = jnp.exp(scores - top)
        total = jnp.sum(weights, axis=1, keepdims=True)
        new_out[:, hs] = (
            jnp.dot(weights.astype(bf16), fresh[2, :, hs], preferred_element_type=f32) / total
        )
        levels.append(top + jnp.log(total))
    new_level = columns_to_tile(levels)

    pl.semaphore_wait(barrier, met)

    sends = []
    for i in range(1, G):
        copy = remote(
            fresh.at[0],
            q_buf.at[me],
            q_send.at[i],
            q_recv.at[me],
            (group_at(i), row, col),
        )
        copy.start()
        sends.append(copy)
    for copy in weight_copies:
        copy.start()
    for copy in small_copies[1:]:
        copy.wait()

    def attend(i):
        g = group_at(i)
        prefix_copy(g).wait()
        tail_copy(g).wait()
        cont = g * lax.div(rows, 2) + row_cont
        prompt_of_row = lax.div(cont, CONT)
        spots = lax.broadcasted_iota(i32, (rows, tail_row.shape[0]), 1)
        tail_spans = tail_row[...].reshape(1, tail_row.shape[0]).astype(f32)
        own_tail = jnp.sum(
            jnp.where(spots == cont, tail_spans, 0.0), axis=1, keepdims=True
        )
        query_off = own_tail + step.astype(f32)

        lane = lax.broadcasted_iota(i32, (1, pair_pages * tokens), 1)
        slot = lax.div(lane, tokens)
        token = lax.rem(lane, tokens) + row * tokens
        owner = jnp.zeros_like(lane)
        place = jnp.zeros_like(lane)
        length = jnp.zeros_like(lane)
        for k in range(pair_pages):
            item = prefix_item[me * slots + g * pair_pages + k]
            prompt = lax.div(item, MAXPAGES)
            hit = slot == k
            owner = jnp.where(hit, prompt, owner)
            place = jnp.where(hit, (item - prompt * MAXPAGES) * PAGE, place)
            length = jnp.where(hit, prefix_length[prompt], length)
        place = place + token
        gap = (place - length).astype(f32)
        open_prompt = jnp.where(place < length, owner, -1)
        prefix_gap = jnp.where(open_prompt == prompt_of_row, gap - query_off, masked_score)

        lane = lax.broadcasted_iota(i32, (1, pair_tails * tokens), 1)
        slot = lax.div(lane, tokens)
        token = lax.rem(lane, tokens) + row * tokens
        owner = jnp.zeros_like(lane)
        length = jnp.zeros_like(lane)
        for k in range(pair_tails):
            item = tail_item[me * tails + g * pair_tails + k]
            hit = slot == k
            owner = jnp.where(hit, item, owner)
            length = jnp.where(hit, tail_length[item], length)
        gap = (token - length).astype(f32)
        open_cont = jnp.where(token < length, owner, -1)
        tail_gap = jnp.where(open_cont == cont, gap - step.astype(f32), masked_score)

        pre = pl.ds(g * pair_pages, pair_pages)
        tai = pl.ds(g * pair_tails, pair_tails)
        levels = []
        for h in range(heads):
            hs = slice(h * HD, (h + 1) * HD)
            query = q_buf[g, :, hs]
            keys = prefix_v[pre, 0, :, hs].reshape(pair_pages * tokens, HD)
            tail_keys = tail_v[tai, 0, :, hs].reshape(pair_tails * tokens, HD)
            s_one = (
                lax.dot_general(query, keys, contract_last, preferred_element_type=f32) * scale
                + slope_row(h, pair_pages * tokens) * prefix_gap
            )
            s_two = (
                lax.dot_general(query, tail_keys, contract_last, preferred_element_type=f32)
                * scale
                + slope_row(h, pair_tails * tokens) * tail_gap
            )
            top = jnp.maximum(
                jnp.max(s_one, axis=1, keepdims=True), jnp.max(s_two, axis=1, keepdims=True)
            )
            top = jnp.maximum(top, empty_floor)
            w_one = jnp.exp(s_one - top)
            w_two = jnp.exp(s_two - top)
            total = jnp.sum(w_one, axis=1, keepdims=True) + jnp.sum(w_two, axis=1, keepdims=True)
            total = jnp.maximum(total, 1e-30)
            values = prefix_v[pre, 1, :, hs].reshape(pair_pages * tokens, HD)
            tail_values = tail_v[tai, 1, :, hs].reshape(pair_tails * tokens, HD)
            out = jnp.dot(w_one.astype(bf16), values, preferred_element_type=f32) + jnp.dot(
                w_two.astype(bf16), tail_values, preferred_element_type=f32
            )
            p_stage[g, :, hs] = (out / total).astype(bf16)
            levels.append(top + jnp.log(total))
        l_stage[g] = columns_to_tile(levels)

    def partial_copies(i, k):
        g = group_at(i)
        target = (g, row_at(k), col)
        return (
            remote(
                p_stage.at[g], p_buf.at[me, row], p_send.at[g, k], p_recv.at[me, row], target
            ),
            remote(
                l_stage.at[g], l_buf.at[me, row], l_send.at[g, k], l_recv.at[me, row], target
            ),
        )

    def partial_arrivals(i, k):
        g, r = group_at(i), row_at(k)
        return (
            remote(p_stage.at[g], p_buf.at[g, r], p_send.at[g, k], p_recv.at[g, r], (g, r, col)),
            remote(l_stage.at[g], l_buf.at[g, r], l_send.at[g, k], l_recv.at[g, r], (g, r, col)),
        )

    attend(0)
    for k in range(1, R):
        for copy in partial_copies(0, k):
            copy.start()
    p_buf[me, row] = p_stage[me]
    l_buf[me, row] = l_stage[me]

    def next_group(i, carry):
        g = group_at(i)
        remote(fresh.at[0], q_buf.at[g], q_send.at[i], q_recv.at[g], (g, row, col)).wait_recv()
        attend(i)
        for k in range(R):
            for copy in partial_copies(i, k):
                copy.start()
        return carry

    lax.fori_loop(1, G, next_group, 0)

    for i in range(G):
        for k in range(R):
            if i or k:
                for copy in partial_arrivals(i, k):
                    copy.wait_recv()

    peers = [l_buf[g, r] for g in range(G) for r in range(R)] + [new_level]
    peak = peers[0]
    for level in peers[1:]:
        peak = jnp.maximum(peak, level)
    shares = [jnp.exp(level - peak) for level in peers]
    total = shares[0]
    for part in shares[1:]:
        total = total + part
    scaled = [part / total for part in shares]
    groups_of_tiles = [
        tile_to_columns(jnp.concatenate(scaled[at : at + LANES // STAT], axis=0), rows)
        for at in range(0, len(scaled), LANES // STAT)
    ]

    def weight_of(peer, h):
        block, spot = divmod(peer, LANES // STAT)
        at = spot * STAT + h
        return groups_of_tiles[block][:, at : at + 1]

    for h in range(heads):
        hs = slice(h * HD, (h + 1) * HD)
        joined = weight_of(G * R, h) * new_out[:, hs]
        for g in range(G):
            for r in range(R):
                joined = joined + weight_of(g * R + r, h) * p_buf[g, r, :, hs].astype(f32)
        att[:, hs] = joined.astype(bf16)

    def share_of(k):
        return pl.ds(pl.multiple_of(col_at(k) * share, LANES), share)

    weight_copies[0].wait()
    for k in range(1, C):
        t = col_at(k)
        a_stage[k] = jnp.dot(
            att[...], out_w[:, share_of(k)], preferred_element_type=f32
        ).astype(bf16)
        copy = remote(a_stage.at[k], a_buf.at[col], a_send.at[k], a_recv.at[col], (me, row, t))
        copy.start()
        sends.append(copy)

    def vector(ref):
        return ref[...].astype(f32).reshape(1, ref.shape[0])

    total = (
        jnp.dot(att[...], out_w[:, share_of(0)], preferred_element_type=f32)
        + residual[...].astype(f32).reshape(rows, share)
        + vector(out_bias)
    )
    for k in range(1, C):
        src = col_at(C - k)
        remote(
            a_stage.at[k], a_buf.at[src], a_send.at[k], a_recv.at[src], (me, row, src)
        ).wait_recv()
        total = total + a_buf[src].astype(f32)
    hidden[...] = total

    def gather(own, tile, wide_buf, wide_send, wide_recv, small_buf, small_send, small_recv):
        small_buf[row, col] = tile
        wide_buf[col] = own
        for k in range(R):
            for j in range(C):
                if k or j:
                    copy = remote(
                        small_buf.at[row, col],
                        small_buf.at[row, col],
                        small_send.at[k, j],
                        small_recv.at[row, col],
                        (me, row_at(k), col_at(j)),
                    )
                    copy.start()
                    sends.append(copy)
        for j in range(1, C):
            copy = remote(
                wide_buf.at[col],
                wide_buf.at[col],
                wide_send.at[j],
                wide_recv.at[col],
                (me, row, col_at(j)),
            )
            copy.start()
            sends.append(copy)
        for k in range(R):
            for j in range(C):
                if k or j:
                    r, c = row_at(k), col_at(j)
                    remote(
                        small_buf.at[row, col],
                        small_buf.at[r, c],
                        small_send.at[k, j],
                        small_recv.at[r, c],
                        (me, r, c),
                    ).wait_recv()
        sums = small_buf[0, 0]
        for k in range(1, R * C):
            sums = sums + small_buf[k // C, k % C]
        for j in range(1, C):
            c = col_at(j)
            remote(
                wide_buf.at[col], wide_buf.at[c], wide_send.at[j], wide_recv.at[c], (me, row, c)
            ).wait_recv()
        return sums

    def norm_into(sums, wide_buf, gain, shift):
        columns = tile_to_columns(sums, rows)
        center = columns[:, 0:1] / D
        spread = columns[:, 1:2] / D - center * center
        factor = lax.rsqrt(spread + norm_eps)
        gains, shifts = vector(gain), vector(shift)
        for c in range(C):
            at = slice(c * share, (c + 1) * share)
            normed[:, at] = (
                (wide_buf[c].astype(f32) - center) * factor * gains[:, at] + shifts[:, at]
            ).astype(bf16)
        return columns

    sums = gather(
        total.astype(bf16),
        columns_to_tile(
            [
                jnp.sum(total, axis=1, keepdims=True),
                jnp.sum(total * total, axis=1, keepdims=True),
            ]
        ),
        x_buf,
        x_send,
        x_recv,
        s_buf,
        s_send,
        s_recv,
    )
    norm_into(sums, x_buf, mlp_gain, mlp_shift)

    partner = (me, row_at(1), col)
    weight_copies[1].wait()
    per_row = chunks // R
    up_shift = vector(up_bias)
    for n in range(chunks):
        part = jnp.dot(
            normed[...], up_w[:, n * chunk : (n + 1) * chunk], preferred_element_type=f32
        )
        mine = jnp.where(jnp.full((1, chunk), row, i32) == n // per_row, 1.0, 0.0)
        part = part + mine * up_shift[:, (n % per_row) * chunk : (n % per_row + 1) * chunk]
        u_own[n] = part
        u_stage[n] = part.astype(bf16)
        copy = remote(u_stage.at[n], u_buf.at[n], u_send.at[n], u_recv.at[n], partner)
        copy.start()
        sends.append(copy)

    weight_copies[2].wait()
    last = chunks - 1
    for n in range(chunks):
        remote(u_stage.at[n], u_buf.at[n], u_send.at[n], u_recv.at[n], partner).wait_recv()
        v = u_own[n] + u_buf[n].astype(f32)
        gelu = (0.5 * v * (1.0 + jnp.tanh(0.7978845608 * (v + 0.044715 * (v * v * v))))).astype(
            bf16
        )
        if n < last:
            term = jnp.dot(
                gelu, down_w[n * chunk : (n + 1) * chunk, :], preferred_element_type=f32
            )
            acc[...] = term if n == 0 else acc[...] + term

    def down_for(k):
        return acc[:, share_of(k)] + jnp.dot(
            gelu, down_w[last * chunk :, share_of(k)], preferred_element_type=f32
        )

    for k in range(1, C):
        d_stage[k] = down_for(k).astype(bf16)
        copy = remote(
            d_stage.at[k], d_buf.at[col], d_send.at[k], d_recv.at[col], (me, row, col_at(k))
        )
        copy.start()
        sends.append(copy)
    total = down_for(0) + hidden[...] + vector(down_bias)
    for k in range(1, C):
        src = col_at(C - k)
        remote(
            d_stage.at[k], d_buf.at[src], d_send.at[k], d_recv.at[src], (me, row, src)
        ).wait_recv()
        total = total + d_buf[src].astype(f32)
    layer_out = total.astype(bf16)
    wide = layer_out.astype(f32)
    scores = vector(score_weight)
    score_part = scores[:, :share]
    for c in range(1, C):
        score_part = jnp.where(
            jnp.full((1, share), col, i32) == c, scores[:, c * share : (c + 1) * share], score_part
        )
    sums = gather(
        layer_out,
        columns_to_tile(
            [
                jnp.sum(wide, axis=1, keepdims=True),
                jnp.sum(wide * wide, axis=1, keepdims=True),
                jnp.sum(wide * score_part, axis=1, keepdims=True),
            ]
        ),
        y_buf,
        y_send,
        y_recv,
        t_buf,
        t_send,
        t_recv,
    )
    columns = norm_into(sums, y_buf, next_gain, next_shift)

    weight_copies[3].wait()
    half = pieces * piece
    qkv_shift = vector(qkv_bias)

    def qkv_piece(r, n):
        at = pl.ds(pl.multiple_of(r * half + n * piece, LANES), piece)
        return jnp.dot(normed[...], qkv_w[:, at], preferred_element_type=f32)

    for n in range(pieces):
        z_stage[n] = qkv_piece(row_at(1), n).astype(bf16)
        copy = remote(z_stage.at[n], z_buf.at[n], z_send.at[n], z_recv.at[n], partner)
        copy.start()
        sends.append(copy)
    layer_ref[...] = wide.reshape(layer_ref.shape).astype(bf16)
    seat = lax.broadcasted_iota(i32, (rows, rows // 2), 1)
    score_ref[...] = jnp.concatenate(
        [
            jnp.sum(
                jnp.where(row_id == seat * 2 + u, columns[:, 2:3], 0.0), axis=0, keepdims=True
            )
            for u in range(2)
        ],
        axis=0,
    )
    for n in range(pieces):
        own = qkv_piece(row, n) + qkv_shift[:, n * piece : (n + 1) * piece]
        remote(z_stage.at[n], z_buf.at[n], z_send.at[n], z_recv.at[n], partner).wait_recv()
        own = own + z_buf[n].astype(f32)
        proj_ref[:, :, n * piece : (n + 1) * piece] = own.reshape(rows // 2, 2, piece).astype(
            bf16
        )

    for copy in sends:
        copy.wait_send()
    for i in range(G):
        for k in range(R):
            if i or k:
                for copy in partial_copies(i, k):
                    copy.wait_send()


def hand_out(*refs):
    sems = refs[6]
    copies = [pltpu.make_async_copy(refs[k], refs[3 + k], sems.at[k]) for k in range(3)]
    for copy in copies:
        copy.start()
    for copy in copies:
        copy.wait()


def fused_shards(
    sizes,
    residual,
    fresh_qkv,
    prefix_pages,
    tail_pages,
    prefix_item,
    tail_item,
    prefix_length,
    tail_length,
    out_weight,
    out_bias,
    mlp_gain,
    mlp_shift,
    up_weight,
    up_bias,
    down_weight,
    down_bias,
    next_gain,
    next_shift,
    score_weight,
    qkv_weight,
    qkv_bias,
):
    G, R, C = sizes["pages"], sizes["row"], sizes["col"]
    f32, bf16 = jnp.float32, jnp.bfloat16
    cont_local, _, share = residual.shape
    rows = cont_local * 2
    head_width = fresh_qkv.shape[3]
    ff_local = up_weight.shape[1]
    out_local = qkv_bias.shape[0]
    chunk = ff_local // 8
    piece = out_local // 2
    fresh = fresh_qkv.transpose(0, 2, 1, 3)
    one_row = (out_bias, mlp_gain, mlp_shift, up_bias, down_bias)
    one_row = one_row + (next_gain, next_shift, score_weight, qkv_bias)
    vmem = pl.BlockSpec(memory_space=pltpu.VMEM)
    hbm = pl.BlockSpec(memory_space=pltpu.MemorySpace.HBM)
    dma = pltpu.SemaphoreType.DMA
    results = pl.pallas_call(
        lambda *refs: layer_kernel(sizes, *refs),
        out_shape=(
            jax.ShapeDtypeStruct((cont_local, 2, share), bf16),
            jax.ShapeDtypeStruct((2, cont_local), f32),
            jax.ShapeDtypeStruct((cont_local, 2, out_local), bf16),
        ),
        in_specs=[hbm] * (12 + len(one_row)),
        out_specs=(vmem, vmem, vmem),
        scratch_shapes=[
            pltpu.SMEM(prefix_item.shape, jnp.int32),
            pltpu.SMEM(tail_item.shape, jnp.int32),
            pltpu.SMEM(prefix_length.shape, jnp.int32),
            pltpu.SMEM(tail_length.shape, jnp.int32),
            pltpu.VMEM(tail_length.shape, jnp.int32),
            pltpu.VMEM(fresh.shape, bf16),
            pltpu.VMEM(residual.shape, bf16),
            *(pltpu.VMEM(v.shape, bf16) for v in one_row),
            pltpu.VMEM((3, rows, head_width), bf16),
            pltpu.VMEM((rows, head_width), f32),
            dma((7 + len(one_row),)),
            pltpu.VMEM(prefix_pages.shape, bf16),
            pltpu.VMEM(tail_pages.shape, bf16),
            pltpu.VMEM(out_weight.shape, bf16),
            pltpu.VMEM(up_weight.shape, bf16),
            pltpu.VMEM(down_weight.shape, bf16),
            pltpu.VMEM(qkv_weight.shape, bf16),
            pltpu.VMEM((G, rows, head_width), bf16),
            pltpu.VMEM((G, rows, head_width), bf16),
            pltpu.VMEM((G, STAT, LANES), f32),
            pltpu.VMEM((G, R, rows, head_width), bf16),
            pltpu.VMEM((G, R, STAT, LANES), f32),
            pltpu.VMEM((rows, head_width), bf16),
            pltpu.VMEM((C, rows, share), bf16),
            pltpu.VMEM((C, rows, share), bf16),
            pltpu.VMEM((rows, share), f32),
            pltpu.VMEM((C, rows, share), bf16),
            pltpu.VMEM((R, C, STAT, LANES), f32),
            pltpu.VMEM((rows, C * share), bf16),
            pltpu.VMEM((ff_local // chunk, rows, chunk), f32),
            pltpu.VMEM((ff_local // chunk, rows, chunk), bf16),
            pltpu.VMEM((ff_local // chunk, rows, chunk), bf16),
            pltpu.VMEM((rows, C * share), f32),
            pltpu.VMEM((C, rows, share), bf16),
            pltpu.VMEM((C, rows, share), bf16),
            pltpu.VMEM((C, rows, share), bf16),
            pltpu.VMEM((R, C, STAT, LANES), f32),
            pltpu.VMEM((out_local // piece, rows, piece), bf16),
            pltpu.VMEM((out_local // piece, rows, piece), bf16),
            dma((G, 2)),
            dma((4,)),
            dma((G,)),
            dma((G,)),
            dma((G, R)),
            dma((G, R)),
            dma((G, R)),
            dma((G, R)),
            dma((C,)),
            dma((C,)),
            dma((C,)),
            dma((C,)),
            dma((R, C)),
            dma((R, C)),
            dma((ff_local // chunk,)),
            dma((ff_local // chunk,)),
            dma((C,)),
            dma((C,)),
            dma((C,)),
            dma((C,)),
            dma((R, C)),
            dma((R, C)),
            dma((out_local // piece,)),
            dma((out_local // piece,)),
        ],
        compiler_params=pltpu.CompilerParams(
            collective_id=0, has_side_effects=True, vmem_limit_bytes=64 * 1024 * 1024
        ),
        name="fused_layer",
    )(
        prefix_item,
        tail_item,
        prefix_length,
        tail_length,
        fresh,
        residual,
        *one_row,
        prefix_pages,
        tail_pages,
        out_weight,
        up_weight,
        down_weight,
        qkv_weight,
    )
    layer_out, scores, projected = pl.pallas_call(
        hand_out,
        out_shape=[jax.ShapeDtypeStruct(part.shape, part.dtype) for part in results],
        in_specs=[hbm] * 3,
        out_specs=[hbm] * 3,
        scratch_shapes=[dma((3,))],
        compiler_params=pltpu.CompilerParams(vmem_limit_bytes=64 * 1024 * 1024),
        name="hand_out",
    )(*results)
    return layer_out, scores.T, projected


def shards(residual, fresh_qkv, prefix_pages, *others):
    sizes = {axis: lax.axis_size(axis) for axis in ("pages", "row", "col")}
    share, tokens = residual.shape[2], prefix_pages.shape[2]
    if sizes["row"] == 2 and sizes["pages"] % 2 == 0 and share % LANES == 0 and tokens % 16 == 0:
        return fused_shards(sizes, residual, fresh_qkv, prefix_pages, *others)
    return plain_shards(residual, fresh_qkv, prefix_pages, *others)


def solution(mesh):
    in_specs = (
        P("pages", None, ("row", "col")),
        P("pages", None, None, "col"),
        P("pages", None, "row", "col"),
        P("pages", None, "row", "col"),
        P(),
        P(),
        P(),
        P(),
        P("col", "row"),
        P(("row", "col")),
        P("row"),
        P("row"),
        P("row", "col"),
        P(("col", "row")),
        P("col", "row"),
        P(("row", "col")),
        P("row"),
        P("row"),
        P("row"),
        P("row", "col"),
        P(("col", "row")),
    )
    out_specs = (
        P("pages", None, ("row", "col")),
        P("pages", None),
        P("pages", None, ("col", "row")),
    )
    return jax.shard_map(shards, mesh=mesh, in_specs=in_specs, out_specs=out_specs, check_vma=False)
```

```python
import math

import jax
import jax.numpy as jnp
from jax import lax
from jax.experimental import pallas as pl
from jax.experimental.pallas import tpu as pltpu
from jax.sharding import PartitionSpec as P

D = 2048
H = 16
HD = 128
PAGE = 128
MAXPAGES = 8
CONT = 16


masked_score = -1e30
norm_eps = 1e-05


def combined_all(shard, axis, combine):
    everything = jax.tree.map(lambda part: lax.all_gather(part, axis), shard)
    first = jax.tree.map(lambda part: part[0], everything)

    def step(k, so_far):
        return combine(so_far, jax.tree.map(lambda part: part[k], everything))

    return lax.fori_loop(1, lax.axis_size(axis), step, first)


def head_slopes(first_head, how_many):
    head_index = first_head + jnp.arange(how_many, dtype=jnp.int32)
    return jnp.exp2(-8.0 * (head_index + 1).astype(jnp.float32) / H)


def slot_partials(queries, page_keys, page_values, usable, offset, slopes):
    scores = jnp.einsum(
        "sqhd,skhd->sqhk", queries, page_keys, preferred_element_type=jnp.float32
    ) / math.sqrt(HD)
    scores = scores + slopes[None, None, :, None] * offset[:, :, None, :]
    usable_full = usable[:, :, None, :]
    scores = jnp.where(usable_full, scores, masked_score)
    maxima = jnp.max(scores, axis=3)
    weights = jnp.where(usable_full, jnp.exp(scores - maxima[..., None]), 0.0)
    totals = jnp.sum(weights, axis=3)
    outputs = jnp.einsum(
        "sqhk,skhd->sqhd", weights, page_values.astype(jnp.float32), precision=lax.Precision.HIGHEST
    )
    return (maxima, totals, outputs)


def merge_pair(left_part, right_part):
    left_max, left_total, left_out = left_part
    right_max, right_total, right_out = right_part
    joined = jnp.maximum(left_max, right_max)
    left_scale = jnp.exp(left_max - joined)
    right_scale = jnp.exp(right_max - joined)
    return (
        joined,
        left_scale * left_total + right_scale * right_total,
        left_scale[..., None] * left_out + right_scale[..., None] * right_out,
    )


def fold_sources(maxima, totals, outputs):
    joined = jnp.max(maxima, axis=0)
    rescale = jnp.exp(maxima - joined[None])
    return (
        joined,
        jnp.sum(rescale * totals, axis=0),
        jnp.sum(rescale[..., None] * outputs, axis=0),
    )


def cache_partials(
    queries,
    page_block,
    page_item,
    tail_block,
    tail_owner,
    prefix_length,
    tail_length,
    row_index,
    slopes,
):
    cont_count = queries.shape[0]
    prompts = cont_count // CONT
    head_count = queries.shape[2]
    slot_count = page_block.shape[0]
    tokens = page_block.shape[2]
    token_index = row_index * tokens + jnp.arange(tokens, dtype=jnp.int32)
    step_index = jnp.arange(2, dtype=jnp.int32)
    slot_prompt = page_item // MAXPAGES
    slot_page = page_item % MAXPAGES
    by_prompt = queries.reshape(prompts, CONT * 2, head_count, HD)
    key_pos = slot_page[:, None] * PAGE + token_index[None, :]
    slot_len = prefix_length[slot_prompt]
    slot_tails = tail_length.reshape(prompts, CONT)[slot_prompt]
    query_pos = (
        slot_len[:, None, None] + slot_tails[:, :, None] + step_index[None, None, :]
    ).reshape(slot_count, CONT * 2)
    offset = (key_pos[:, None, :] - query_pos[:, :, None]).astype(jnp.float32)
    usable = jnp.broadcast_to((key_pos < slot_len[:, None])[:, None, :], offset.shape)
    page_keys = page_block[:, 0].reshape(slot_count, tokens, head_count, HD)
    page_values = page_block[:, 1].reshape(slot_count, tokens, head_count, HD)
    maxima, totals, outputs = slot_partials(
        by_prompt[slot_prompt], page_keys, page_values, usable, offset, slopes
    )
    prompt_max = (
        jnp.full((prompts, CONT * 2, head_count), masked_score, jnp.float32)
        .at[slot_prompt]
        .max(maxima)
    )
    rescale = jnp.exp(maxima - prompt_max[slot_prompt])
    prompt_total = (
        jnp.zeros((prompts, CONT * 2, head_count), jnp.float32)
        .at[slot_prompt]
        .add(rescale * totals)
    )
    prompt_out = (
        jnp.zeros((prompts, CONT * 2, head_count, HD), jnp.float32)
        .at[slot_prompt]
        .add(rescale[..., None] * outputs)
    )
    prefix_part = (
        prompt_max.reshape(cont_count, 2, head_count),
        prompt_total.reshape(cont_count, 2, head_count),
        prompt_out.reshape(cont_count, 2, head_count, HD),
    )
    tail_count = tail_block.shape[0]
    tail_lens = tail_length[tail_owner]
    tail_usable = jnp.broadcast_to(
        (token_index[None, :] < tail_lens[:, None])[:, None, :], (tail_count, 2, tokens)
    )
    tail_offset = (
        token_index[None, None, :] - tail_lens[:, None, None] - step_index[None, :, None]
    ).astype(jnp.float32)
    tail_keys = tail_block[:, 0].reshape(tail_count, tokens, head_count, HD)
    tail_values = tail_block[:, 1].reshape(tail_count, tokens, head_count, HD)
    tail_max, tail_total, tail_out = slot_partials(
        queries[tail_owner], tail_keys, tail_values, tail_usable, tail_offset, slopes
    )
    cont_max = (
        jnp.full((cont_count, 2, head_count), masked_score, jnp.float32)
        .at[tail_owner]
        .set(tail_max)
    )
    cont_total = jnp.zeros((cont_count, 2, head_count), jnp.float32).at[tail_owner].set(tail_total)
    cont_out = jnp.zeros((cont_count, 2, head_count, HD), jnp.float32).at[tail_owner].set(tail_out)
    return merge_pair(prefix_part, (cont_max, cont_total, cont_out))


def normalize(values, sum_one, sum_two, gain, shift):
    center = sum_one / D
    spread = sum_two / D - center * center
    return (
        (values - center[:, None])
        * lax.rsqrt(spread + norm_eps)[:, None]
        * gain.astype(jnp.float32)
        + shift.astype(jnp.float32)
    ).astype(jnp.bfloat16)


def plain_shards(
    residual,
    fresh_qkv,
    prefix_pages,
    tail_pages,
    prefix_item,
    tail_item,
    prefix_length,
    tail_length,
    out_weight,
    out_bias,
    mlp_gain,
    mlp_shift,
    up_weight,
    up_bias,
    down_weight,
    down_bias,
    next_gain,
    next_shift,
    score_weight,
    qkv_weight,
    qkv_bias,
):
    group_index = lax.axis_index("pages")
    row_index = lax.axis_index("row")
    col_index = lax.axis_index("col")
    group_count = lax.axis_size("pages")
    cont_local = residual.shape[0]
    row_total = cont_local * 2
    share = residual.shape[2]
    head_count = fresh_qkv.shape[3] // HD
    slopes = head_slopes(col_index * head_count, head_count)
    fresh_rows = fresh_qkv.reshape(cont_local, 2, 3, head_count, HD)
    slot_count = prefix_pages.shape[0]
    tail_slots = tail_pages.shape[0]
    everyone = lax.all_gather(fresh_qkv[:, :, 0], "pages", axis=0, tiled=True)
    page_item = lax.dynamic_slice_in_dim(prefix_item, group_index * slot_count, slot_count)
    tail_owner = lax.dynamic_slice_in_dim(tail_item, group_index * tail_slots, tail_slots)
    maxima, totals, outputs = cache_partials(
        everyone.reshape(everyone.shape[0], 2, head_count, HD),
        prefix_pages,
        page_item,
        tail_pages,
        tail_owner,
        prefix_length,
        tail_length,
        row_index,
        slopes,
    )
    maxima, totals, outputs = (
        lax.all_to_all(
            maxima.reshape(group_count, row_total, head_count),
            "pages",
            split_axis=0,
            concat_axis=0,
            tiled=True,
        ),
        lax.all_to_all(
            totals.reshape(group_count, row_total, head_count),
            "pages",
            split_axis=0,
            concat_axis=0,
            tiled=True,
        ),
        lax.all_to_all(
            outputs.reshape(group_count, row_total, head_count, HD),
            "pages",
            split_axis=0,
            concat_axis=0,
            tiled=True,
        ),
    )
    cache_max, cache_total, cache_out = fold_sources(maxima, totals, outputs)
    cache_max, cache_total, cache_out = combined_all(
        (cache_max, cache_total, cache_out), "row", merge_pair
    )
    step_index = jnp.arange(2, dtype=jnp.int32)
    new_usable = jnp.broadcast_to(
        (step_index[None, :] <= step_index[:, None])[None], (cont_local, 2, 2)
    )
    new_offset = jnp.broadcast_to(
        (step_index[None, :] - step_index[:, None]).astype(jnp.float32)[None], (cont_local, 2, 2)
    )
    new_part = slot_partials(
        fresh_rows[:, :, 0],
        fresh_rows[:, :, 1],
        fresh_rows[:, :, 2],
        new_usable,
        new_offset,
        slopes,
    )
    joined_max, joined_total, joined_out = merge_pair(
        (
            cache_max.reshape(cont_local, 2, head_count),
            cache_total.reshape(cont_local, 2, head_count),
            cache_out.reshape(cont_local, 2, head_count, HD),
        ),
        new_part,
    )
    attended = (
        (joined_out / joined_total[..., None])
        .astype(jnp.bfloat16)
        .reshape(row_total, head_count * HD)
    )
    head_term = jnp.dot(attended, out_weight, preferred_element_type=jnp.float32)
    hidden_one = (
        residual.reshape(row_total, share).astype(jnp.float32)
        + lax.psum_scatter(head_term, "col", scatter_dimension=1, tiled=True)
        + out_bias.astype(jnp.float32)
    )
    gain_part = lax.dynamic_slice_in_dim(mlp_gain, col_index * share, share)
    shift_part = lax.dynamic_slice_in_dim(mlp_shift, col_index * share, share)
    sum_one, sum_two = lax.psum(
        (jnp.sum(hidden_one, axis=1), jnp.sum(hidden_one * hidden_one, axis=1)), ("row", "col")
    )
    normed_a = lax.all_gather(
        normalize(hidden_one, sum_one, sum_two, gain_part, shift_part), "col", axis=1, tiled=True
    )
    up_share = lax.psum_scatter(
        jnp.dot(normed_a, up_weight, preferred_element_type=jnp.float32),
        "row",
        scatter_dimension=1,
        tiled=True,
    )
    hidden_two = jax.nn.gelu(up_share + up_bias.astype(jnp.float32), approximate=True).astype(
        jnp.bfloat16
    )
    down_sum = jnp.dot(
        lax.all_gather(hidden_two, "row", axis=1, tiled=True),
        down_weight,
        preferred_element_type=jnp.float32,
    )
    down_share = lax.psum_scatter(
        down_sum.astype(jnp.bfloat16), "col", scatter_dimension=1, tiled=True
    ).astype(jnp.float32)
    layer_out = (hidden_one + down_share + down_bias.astype(jnp.float32)).astype(jnp.bfloat16)
    out_wide = layer_out.astype(jnp.float32)
    gain_part = lax.dynamic_slice_in_dim(next_gain, col_index * share, share)
    shift_part = lax.dynamic_slice_in_dim(next_shift, col_index * share, share)
    score_part = lax.dynamic_slice_in_dim(score_weight, col_index * share, share).astype(
        jnp.float32
    )
    sum_one, sum_two, score_sum = lax.psum(
        (
            jnp.sum(out_wide, axis=1),
            jnp.sum(out_wide * out_wide, axis=1),
            jnp.sum(out_wide * score_part, axis=1),
        ),
        ("row", "col"),
    )
    normed_b = lax.all_gather(
        normalize(out_wide, sum_one, sum_two, gain_part, shift_part), "col", axis=1, tiled=True
    )
    qkv_share = lax.psum_scatter(
        jnp.dot(normed_b, qkv_weight, preferred_element_type=jnp.float32).astype(jnp.bfloat16),
        "row",
        scatter_dimension=1,
        tiled=True,
    ).astype(jnp.float32)
    projected_next = (qkv_share + qkv_bias.astype(jnp.float32)).astype(jnp.bfloat16)
    return (
        layer_out.reshape(cont_local, 2, share),
        score_sum.reshape(cont_local, 2),
        projected_next.reshape(cont_local, 2, qkv_share.shape[1]),
    )


empty_floor = -1e20
STAT = 8
LANES = 128


def columns_to_tile(columns):
    rows = columns[0].shape[0]
    lane = lax.broadcasted_iota(jnp.int32, (rows, LANES), 1)
    wide = jnp.zeros((rows, LANES), jnp.float32)
    for k, column in enumerate(columns):
        wide = jnp.where(lane == k, column, wide)
    if rows < LANES:
        wide = jnp.concatenate([wide, jnp.zeros((LANES - rows, LANES), jnp.float32)], axis=0)
    return jnp.transpose(wide)[:STAT]


def tile_to_columns(tile, rows):
    have = tile.shape[0]
    if have < LANES:
        tile = jnp.concatenate([tile, jnp.zeros((LANES - have, LANES), jnp.float32)], axis=0)
    return jnp.transpose(tile)[:rows]


def layer_kernel(
    sizes,
    item_hbm,
    owner_hbm,
    length_hbm,
    span_hbm,
    fresh_hbm,
    residual_hbm,
    out_bias_hbm,
    mlp_gain_hbm,
    mlp_shift_hbm,
    up_bias_hbm,
    down_bias_hbm,
    next_gain_hbm,
    next_shift_hbm,
    score_hbm,
    qkv_bias_hbm,
    prefix_hbm,
    tail_hbm,
    out_hbm,
    up_hbm,
    down_hbm,
    qkv_hbm,
    layer_ref,
    score_ref,
    proj_ref,
    prefix_item,
    tail_item,
    prefix_length,
    tail_length,
    tail_row,
    fresh_raw,
    residual,
    out_bias,
    mlp_gain,
    mlp_shift,
    up_bias,
    down_bias,
    next_gain,
    next_shift,
    score_weight,
    qkv_bias,
    fresh,
    new_out,
    small_sem,
    prefix_v,
    tail_v,
    out_w,
    up_w,
    down_w,
    qkv_w,
    q_buf,
    p_stage,
    l_stage,
    p_buf,
    l_buf,
    att,
    a_stage,
    a_buf,
    hidden,
    x_buf,
    s_buf,
    normed,
    u_own,
    u_stage,
    u_buf,
    acc,
    d_stage,
    d_buf,
    y_buf,
    t_buf,
    z_stage,
    z_buf,
    page_sem,
    w_sem,
    q_send,
    q_recv,
    p_send,
    p_recv,
    l_send,
    l_recv,
    a_send,
    a_recv,
    x_send,
    x_recv,
    s_send,
    s_recv,
    u_send,
    u_recv,
    d_send,
    d_recv,
    y_send,
    y_recv,
    t_send,
    t_recv,
    z_send,
    z_recv,
):
    G, R, C = sizes["pages"], sizes["row"], sizes["col"]
    f32, bf16, i32 = jnp.float32, jnp.bfloat16, jnp.int32
    me = lax.axis_index("pages")
    row = lax.axis_index("row")
    col = lax.axis_index("col")
    rows = fresh.shape[1]
    share = residual.shape[2]
    width = C * share
    heads = fresh.shape[2] // HD
    slots, _, tokens, _ = prefix_v.shape
    tails = tail_v.shape[0]
    pair_pages, pair_tails = slots // G, tails // G
    _, chunks, _, chunk = u_buf.shape
    _, pieces, _, piece = z_buf.shape

    def group_at(i):
        if isinstance(i, int) and i == 0:
            return me
        j = lax.rem(jnp.int32(i), G - 1) + 1
        return lax.rem(lax.div(me, 2) + lax.div(j, 2), G // 2) * 2 + lax.rem(me + j, 2)

    def row_at(k):
        return lax.rem(row + k, R)

    def col_at(k):
        return lax.rem(col + k, C)

    def remote(src, dst, send_sem, recv_sem, target):
        return pltpu.make_async_remote_copy(
            src_ref=src,
            dst_ref=dst,
            send_sem=send_sem,
            recv_sem=recv_sem,
            device_id=target,
            device_id_type=pl.DeviceIdType.MESH,
        )

    def prefix_copy(g):
        part = pl.ds(g * pair_pages, pair_pages)
        return pltpu.make_async_copy(prefix_hbm.at[part], prefix_v.at[part], page_sem.at[g, 0])

    def tail_copy(g):
        part = pl.ds(g * pair_tails, pair_tails)
        return pltpu.make_async_copy(tail_hbm.at[part], tail_v.at[part], page_sem.at[g, 1])

    weight_copies = [
        pltpu.make_async_copy(src, dst, w_sem.at[k])
        for k, (src, dst) in enumerate(
            ((out_hbm, out_w), (up_hbm, up_w), (down_hbm, down_w), (qkv_hbm, qkv_w))
        )
    ]

    small_pairs = (
        (fresh_hbm, fresh_raw),
        (item_hbm, prefix_item),
        (owner_hbm, tail_item),
        (length_hbm, prefix_length),
        (span_hbm, tail_length),
        (span_hbm, tail_row),
        (residual_hbm, residual),
        (out_bias_hbm, out_bias),
        (mlp_gain_hbm, mlp_gain),
        (mlp_shift_hbm, mlp_shift),
        (up_bias_hbm, up_bias),
        (down_bias_hbm, down_bias),
        (next_gain_hbm, next_gain),
        (next_shift_hbm, next_shift),
        (score_hbm, score_weight),
        (qkv_bias_hbm, qkv_bias),
    )
    small_copies = [
        pltpu.make_async_copy(src, dst, small_sem.at[k])
        for k, (src, dst) in enumerate(small_pairs)
    ]

    barrier = pltpu.get_barrier_semaphore()
    met = 0
    for i in range(G):
        for k in range(R):
            if i or k:
                met += 1
                pl.semaphore_signal(
                    barrier,
                    inc=1,
                    device_id=(group_at(i), row_at(k), col),
                    device_id_type=pl.DeviceIdType.MESH,
                )
    for k in range(R):
        for j in range(1, C):
            met += 1
            pl.semaphore_signal(
                barrier,
                inc=1,
                device_id=(me, row_at(k), col_at(j)),
                device_id_type=pl.DeviceIdType.MESH,
            )
    for copy in small_copies[:6]:
        copy.start()
    for i in range(G):
        prefix_copy(group_at(i)).start()
        tail_copy(group_at(i)).start()
    for copy in small_copies[6:]:
        copy.start()

    row_id = lax.broadcasted_iota(i32, (rows, 1), 0)
    step = lax.rem(row_id, 2)
    row_cont = lax.div(row_id, 2)
    contract_last = (((1,), (1,)), ((), ()))
    scale = 1.0 / math.sqrt(HD)

    def slope_row(h, size):
        index = jnp.full((1, size), col * heads + h + 1, i32).astype(f32)
        return jnp.exp(index * (-8.0 / H * math.log(2.0)))

    small_copies[0].wait()
    for part in range(3):
        fresh[part] = fresh_raw[:, part].reshape(rows, heads * HD)
    q_buf[me] = fresh[0]
    key_id = lax.broadcasted_iota(i32, (rows, rows), 1)
    new_ok = jnp.logical_and(lax.div(key_id, 2) == row_cont, lax.rem(key_id, 2) <= step)
    new_gap = jnp.where(new_ok, (lax.rem(key_id, 2) - step).astype(f32), masked_score)
    levels = []
    for h in range(heads):
        hs = slice(h * HD, (h + 1) * HD)
        scores = (
            lax.dot_general(
                fresh[0, :, hs], fresh[1, :, hs], contract_last, preferred_element_type=f32
            )
            * scale
            + slope_row(h, rows) * new_gap
        )
        top = jnp.max(scores, axis=1, keepdims=True)
        weights = jnp.exp(scores - top)
        total = jnp.sum(weights, axis=1, keepdims=True)
        new_out[:, hs] = (
            jnp.dot(weights.astype(bf16), fresh[2, :, hs], preferred_element_type=f32) / total
        )
        levels.append(top + jnp.log(total))
    new_level = columns_to_tile(levels)

    pl.semaphore_wait(barrier, met)

    sends = []
    for i in range(1, G):
        copy = remote(
            fresh.at[0],
            q_buf.at[me],
            q_send.at[i],
            q_recv.at[me],
            (group_at(i), row, col),
        )
        copy.start()
        sends.append(copy)
    for copy in weight_copies:
        copy.start()
    for copy in small_copies[1:]:
        copy.wait()

    def attend(i):
        g = group_at(i)
        prefix_copy(g).wait()
        tail_copy(g).wait()
        cont = g * lax.div(rows, 2) + row_cont
        prompt_of_row = lax.div(cont, CONT)
        spots = lax.broadcasted_iota(i32, (rows, tail_row.shape[0]), 1)
        tail_spans = tail_row[...].reshape(1, tail_row.shape[0]).astype(f32)
        own_tail = jnp.sum(
            jnp.where(spots == cont, tail_spans, 0.0), axis=1, keepdims=True
        )
        query_off = own_tail + step.astype(f32)

        lane = lax.broadcasted_iota(i32, (1, pair_pages * tokens), 1)
        slot = lax.div(lane, tokens)
        token = lax.rem(lane, tokens) + row * tokens
        owner = jnp.zeros_like(lane)
        place = jnp.zeros_like(lane)
        length = jnp.zeros_like(lane)
        for k in range(pair_pages):
            item = prefix_item[me * slots + g * pair_pages + k]
            prompt = lax.div(item, MAXPAGES)
            hit = slot == k
            owner = jnp.where(hit, prompt, owner)
            place = jnp.where(hit, (item - prompt * MAXPAGES) * PAGE, place)
            length = jnp.where(hit, prefix_length[prompt], length)
        place = place + token
        gap = (place - length).astype(f32)
        open_prompt = jnp.where(place < length, owner, -1)
        prefix_gap = jnp.where(open_prompt == prompt_of_row, gap - query_off, masked_score)

        lane = lax.broadcasted_iota(i32, (1, pair_tails * tokens), 1)
        slot = lax.div(lane, tokens)
        token = lax.rem(lane, tokens) + row * tokens
        owner = jnp.zeros_like(lane)
        length = jnp.zeros_like(lane)
        for k in range(pair_tails):
            item = tail_item[me * tails + g * pair_tails + k]
            hit = slot == k
            owner = jnp.where(hit, item, owner)
            length = jnp.where(hit, tail_length[item], length)
        gap = (token - length).astype(f32)
        open_cont = jnp.where(token < length, owner, -1)
        tail_gap = jnp.where(open_cont == cont, gap - step.astype(f32), masked_score)

        pre = pl.ds(g * pair_pages, pair_pages)
        tai = pl.ds(g * pair_tails, pair_tails)
        levels = []
        for h in range(heads):
            hs = slice(h * HD, (h + 1) * HD)
            query = q_buf[g, :, hs]
            keys = prefix_v[pre, 0, :, hs].reshape(pair_pages * tokens, HD)
            tail_keys = tail_v[tai, 0, :, hs].reshape(pair_tails * tokens, HD)
            s_one = (
                lax.dot_general(query, keys, contract_last, preferred_element_type=f32) * scale
                + slope_row(h, pair_pages * tokens) * prefix_gap
            )
            s_two = (
                lax.dot_general(query, tail_keys, contract_last, preferred_element_type=f32)
                * scale
                + slope_row(h, pair_tails * tokens) * tail_gap
            )
            top = jnp.maximum(
                jnp.max(s_one, axis=1, keepdims=True), jnp.max(s_two, axis=1, keepdims=True)
            )
            top = jnp.maximum(top, empty_floor)
            w_one = jnp.exp(s_one - top)
            w_two = jnp.exp(s_two - top)
            total = jnp.sum(w_one, axis=1, keepdims=True) + jnp.sum(w_two, axis=1, keepdims=True)
            total = jnp.maximum(total, 1e-30)
            values = prefix_v[pre, 1, :, hs].reshape(pair_pages * tokens, HD)
            tail_values = tail_v[tai, 1, :, hs].reshape(pair_tails * tokens, HD)
            out = jnp.dot(w_one.astype(bf16), values, preferred_element_type=f32) + jnp.dot(
                w_two.astype(bf16), tail_values, preferred_element_type=f32
            )
            p_stage[g, :, hs] = (out / total).astype(bf16)
            levels.append(top + jnp.log(total))
        l_stage[g] = columns_to_tile(levels)

    def partial_copies(i, k):
        g = group_at(i)
        target = (g, row_at(k), col)
        return (
            remote(
                p_stage.at[g], p_buf.at[me, row], p_send.at[g, k], p_recv.at[me, row], target
            ),
            remote(
                l_stage.at[g], l_buf.at[me, row], l_send.at[g, k], l_recv.at[me, row], target
            ),
        )

    def partial_arrivals(i, k):
        g, r = group_at(i), row_at(k)
        return (
            remote(p_stage.at[g], p_buf.at[g, r], p_send.at[g, k], p_recv.at[g, r], (g, r, col)),
            remote(l_stage.at[g], l_buf.at[g, r], l_send.at[g, k], l_recv.at[g, r], (g, r, col)),
        )

    attend(0)
    for k in range(1, R):
        for copy in partial_copies(0, k):
            copy.start()
    p_buf[me, row] = p_stage[me]
    l_buf[me, row] = l_stage[me]

    def next_group(i, carry):
        g = group_at(i)
        remote(fresh.at[0], q_buf.at[g], q_send.at[i], q_recv.at[g], (g, row, col)).wait_recv()
        attend(i)
        for k in range(R):
            for copy in partial_copies(i, k):
                copy.start()
        return carry

    lax.fori_loop(1, G, next_group, 0)

    for i in range(G):
        for k in range(R):
            if i or k:
                for copy in partial_arrivals(i, k):
                    copy.wait_recv()

    peers = [l_buf[g, r] for g in range(G) for r in range(R)] + [new_level]
    peak = peers[0]
    for level in peers[1:]:
        peak = jnp.maximum(peak, level)
    shares = [jnp.exp(level - peak) for level in peers]
    total = shares[0]
    for part in shares[1:]:
        total = total + part
    scaled = [part / total for part in shares]
    groups_of_tiles = [
        tile_to_columns(jnp.concatenate(scaled[at : at + LANES // STAT], axis=0), rows)
        for at in range(0, len(scaled), LANES // STAT)
    ]

    def weight_of(peer, h):
        block, spot = divmod(peer, LANES // STAT)
        at = spot * STAT + h
        return groups_of_tiles[block][:, at : at + 1]

    for h in range(heads):
        hs = slice(h * HD, (h + 1) * HD)
        joined = weight_of(G * R, h) * new_out[:, hs]
        for g in range(G):
            for r in range(R):
                joined = joined + weight_of(g * R + r, h) * p_buf[g, r, :, hs].astype(f32)
        att[:, hs] = joined.astype(bf16)

    def share_of(k):
        return pl.ds(pl.multiple_of(col_at(k) * share, LANES), share)

    half_rows = rows // 2
    partner = (me, row_at(1), col)
    per_row = chunks // R
    last = chunks - 1

    def vector(ref):
        return ref[...].astype(f32).reshape(1, ref.shape[0])

    def push(src, dst, send_sem, recv_sem, target):
        copy = remote(src, dst, send_sem, recv_sem, target)
        copy.start()
        sends.append(copy)

    def project_out(b):
        part = att[b * half_rows : (b + 1) * half_rows, :]
        for k in range(1, C):
            a_stage[b, k] = jnp.dot(
                part, out_w[:, share_of(k)], preferred_element_type=f32
            ).astype(bf16)
            push(
                a_stage.at[b, k],
                a_buf.at[b, col],
                a_send.at[b, k],
                a_recv.at[b, col],
                (me, row, col_at(k)),
            )
        stream = residual[b * half_rows // 2 : (b + 1) * half_rows // 2].astype(f32)
        hidden[b] = (
            jnp.dot(part, out_w[:, share_of(0)], preferred_element_type=f32)
            + stream.reshape(half_rows, share)
            + vector(out_bias)
        )

    def summed(b, total, stage, buf, send, recv):
        for k in range(1, C):
            src = col_at(C - k)
            remote(
                stage.at[b, k], buf.at[b, src], send.at[b, k], recv.at[b, src], (me, row, src)
            ).wait_recv()
            total = total + buf[b, src].astype(f32)
        return total

    def gather_start(b, own, parts, wide_buf, wide_send, wide_recv, small_buf, small_send, small_recv):
        wide_buf[b, col] = own
        small_buf[b, row, col] = columns_to_tile(
            [jnp.sum(part, axis=1, keepdims=True) for part in parts]
        )
        for k in range(R):
            for j in range(C):
                if k or j:
                    push(
                        small_buf.at[b, row, col],
                        small_buf.at[b, row, col],
                        small_send.at[b, k, j],
                        small_recv.at[b, row, col],
                        (me, row_at(k), col_at(j)),
                    )
        for j in range(1, C):
            push(
                wide_buf.at[b, col],
                wide_buf.at[b, col],
                wide_send.at[b, j],
                wide_recv.at[b, col],
                (me, row, col_at(j)),
            )

    def gather_norm(
        b, gain, shift, wide_buf, wide_send, wide_recv, small_buf, small_send, small_recv
    ):
        for k in range(R):
            for j in range(C):
                if k or j:
                    r, c = row_at(k), col_at(j)
                    remote(
                        small_buf.at[b, row, col],
                        small_buf.at[b, r, c],
                        small_send.at[b, k, j],
                        small_recv.at[b, r, c],
                        (me, r, c),
                    ).wait_recv()
        sums = small_buf[b, 0, 0]
        for k in range(1, R * C):
            sums = sums + small_buf[b, k // C, k % C]
        columns = tile_to_columns(sums, half_rows)
        center = columns[:, 0:1] / D
        spread = columns[:, 1:2] / D - center * center
        factor = lax.rsqrt(spread + norm_eps)
        gains, shifts = vector(gain), vector(shift)
        for j in range(1, C):
            c = col_at(j)
            remote(
                wide_buf.at[b, col],
                wide_buf.at[b, c],
                wide_send.at[b, j],
                wide_recv.at[b, c],
                (me, row, c),
            ).wait_recv()
        for c in range(C):
            at = slice(c * share, (c + 1) * share)
            normed[b, :, at] = (
                (wide_buf[b, c].astype(f32) - center) * factor * gains[:, at] + shifts[:, at]
            ).astype(bf16)
        return columns

    first_gather = (x_buf, x_send, x_recv, s_buf, s_send, s_recv)
    second_gather = (y_buf, y_send, y_recv, t_buf, t_send, t_recv)

    def up_copy(b, n):
        return (u_stage.at[b, n], u_buf.at[b, n], u_send.at[b, n], u_recv.at[b, n], partner)

    def project_up(b):
        up_shift = vector(up_bias)
        for n in range(chunks):
            part = jnp.dot(
                normed[b], up_w[:, n * chunk : (n + 1) * chunk], preferred_element_type=f32
            )
            mine = jnp.where(jnp.full((1, chunk), row, i32) == n // per_row, 1.0, 0.0)
            spot = n % per_row
            part = part + mine * up_shift[:, spot * chunk : (spot + 1) * chunk]
            u_own[b, n] = part
            u_stage[b, n] = part.astype(bf16)
            push(*up_copy(b, n))

    def project_down(b):
        for n in range(chunks):
            remote(*up_copy(b, n)).wait_recv()
            v = u_own[b, n] + u_buf[b, n].astype(f32)
            gelu = (
                0.5 * v * (1.0 + jnp.tanh(0.7978845608 * (v + 0.044715 * (v * v * v))))
            ).astype(bf16)
            if n < last:
                term = jnp.dot(
                    gelu, down_w[n * chunk : (n + 1) * chunk, :], preferred_element_type=f32
                )
                acc[b] = term if n == 0 else acc[b] + term

        def down_for(k):
            return acc[b, :, share_of(k)] + jnp.dot(
                gelu, down_w[last * chunk :, share_of(k)], preferred_element_type=f32
            )

        for k in range(1, C):
            d_stage[b, k] = down_for(k).astype(bf16)
            push(
                d_stage.at[b, k],
                d_buf.at[b, col],
                d_send.at[b, k],
                d_recv.at[b, col],
                (me, row, col_at(k)),
            )
        hidden[b] = hidden[b] + down_for(0) + vector(down_bias)

    half = pieces * piece

    def qkv_piece(b, r, n):
        at = pl.ds(pl.multiple_of(r * half + n * piece, LANES), piece)
        return jnp.dot(normed[b], qkv_w[:, at], preferred_element_type=f32)

    def z_copy(b, n):
        return (z_stage.at[b, n], z_buf.at[b, n], z_send.at[b, n], z_recv.at[b, n], partner)

    weight_copies[0].wait()
    for b in range(2):
        project_out(b)
    for b in range(2):
        total = summed(b, hidden[b], a_stage, a_buf, a_send, a_recv)
        hidden[b] = total
        gather_start(b, total.astype(bf16), [total, total * total], *first_gather)
    weight_copies[1].wait()
    for b in range(2):
        gather_norm(b, mlp_gain, mlp_shift, *first_gather)
        project_up(b)
    weight_copies[2].wait()
    for b in range(2):
        project_down(b)

    scores = vector(score_weight)
    score_part = scores[:, :share]
    for c in range(1, C):
        score_part = jnp.where(
            jnp.full((1, share), col, i32) == c, scores[:, c * share : (c + 1) * share], score_part
        )
    quarter = half_rows // 2
    for b in range(2):
        layer_out = summed(b, hidden[b], d_stage, d_buf, d_send, d_recv).astype(bf16)
        wide = layer_out.astype(f32)
        gather_start(b, layer_out, [wide, wide * wide, wide * score_part], *second_gather)
        layer_ref[b * quarter : (b + 1) * quarter] = wide.reshape(quarter, 2, share).astype(bf16)
    weight_copies[3].wait()
    score_columns = []
    for b in range(2):
        columns = gather_norm(b, next_gain, next_shift, *second_gather)
        score_columns.append(columns[:, 2:3])
        for n in range(pieces):
            z_stage[b, n] = qkv_piece(b, row_at(1), n).astype(bf16)
            push(*z_copy(b, n))
    seat = lax.broadcasted_iota(i32, (rows, rows // 2), 1)
    score_column = jnp.concatenate(score_columns, axis=0)
    score_ref[...] = jnp.concatenate(
        [
            jnp.sum(jnp.where(row_id == seat * 2 + u, score_column, 0.0), axis=0, keepdims=True)
            for u in range(2)
        ],
        axis=0,
    )
    qkv_shift = vector(qkv_bias)
    for b in range(2):
        for n in range(pieces):
            at = slice(n * piece, (n + 1) * piece)
            own = qkv_piece(b, row, n) + qkv_shift[:, at]
            remote(*z_copy(b, n)).wait_recv()
            own = own + z_buf[b, n].astype(f32)
            proj_ref[b * quarter : (b + 1) * quarter, :, at] = own.reshape(
                quarter, 2, piece
            ).astype(bf16)

    for copy in sends:
        copy.wait_send()
    for i in range(G):
        for k in range(R):
            if i or k:
                for copy in partial_copies(i, k):
                    copy.wait_send()


def hand_out(*refs):
    for k in range(3):
        refs[3 + k][...] = refs[k][...]


def fused_shards(
    sizes,
    residual,
    fresh_qkv,
    prefix_pages,
    tail_pages,
    prefix_item,
    tail_item,
    prefix_length,
    tail_length,
    out_weight,
    out_bias,
    mlp_gain,
    mlp_shift,
    up_weight,
    up_bias,
    down_weight,
    down_bias,
    next_gain,
    next_shift,
    score_weight,
    qkv_weight,
    qkv_bias,
):
    G, R, C = sizes["pages"], sizes["row"], sizes["col"]
    f32, bf16 = jnp.float32, jnp.bfloat16
    cont_local, _, share = residual.shape
    rows = cont_local * 2
    half = rows // 2
    head_width = fresh_qkv.shape[3]
    ff_local = up_weight.shape[1]
    out_local = qkv_bias.shape[0]
    chunk = ff_local // 4
    piece = out_local
    fresh = fresh_qkv.transpose(0, 2, 1, 3)
    one_row = (out_bias, mlp_gain, mlp_shift, up_bias, down_bias)
    one_row = one_row + (next_gain, next_shift, score_weight, qkv_bias)
    vmem = pl.BlockSpec(memory_space=pltpu.VMEM)
    hbm = pl.BlockSpec(memory_space=pltpu.MemorySpace.HBM)
    dma = pltpu.SemaphoreType.DMA
    results = pl.pallas_call(
        lambda *refs: layer_kernel(sizes, *refs),
        out_shape=(
            jax.ShapeDtypeStruct((cont_local, 2, share), bf16),
            jax.ShapeDtypeStruct((2, cont_local), f32),
            jax.ShapeDtypeStruct((cont_local, 2, out_local), bf16),
        ),
        in_specs=[hbm] * (12 + len(one_row)),
        out_specs=(vmem, vmem, vmem),
        scratch_shapes=[
            pltpu.SMEM(prefix_item.shape, jnp.int32),
            pltpu.SMEM(tail_item.shape, jnp.int32),
            pltpu.SMEM(prefix_length.shape, jnp.int32),
            pltpu.SMEM(tail_length.shape, jnp.int32),
            pltpu.VMEM(tail_length.shape, jnp.int32),
            pltpu.VMEM(fresh.shape, bf16),
            pltpu.VMEM(residual.shape, bf16),
            *(pltpu.VMEM(v.shape, bf16) for v in one_row),
            pltpu.VMEM((3, rows, head_width), bf16),
            pltpu.VMEM((rows, head_width), f32),
            dma((7 + len(one_row),)),
            pltpu.VMEM(prefix_pages.shape, bf16),
            pltpu.VMEM(tail_pages.shape, bf16),
            pltpu.VMEM(out_weight.shape, bf16),
            pltpu.VMEM(up_weight.shape, bf16),
            pltpu.VMEM(down_weight.shape, bf16),
            pltpu.VMEM(qkv_weight.shape, bf16),
            pltpu.VMEM((G, rows, head_width), bf16),
            pltpu.VMEM((G, rows, head_width), bf16),
            pltpu.VMEM((G, STAT, LANES), f32),
            pltpu.VMEM((G, R, rows, head_width), bf16),
            pltpu.VMEM((G, R, STAT, LANES), f32),
            pltpu.VMEM((rows, head_width), bf16),
            pltpu.VMEM((2, C, half, share), bf16),
            pltpu.VMEM((2, C, half, share), bf16),
            pltpu.VMEM((2, half, share), f32),
            pltpu.VMEM((2, C, half, share), bf16),
            pltpu.VMEM((2, R, C, STAT, LANES), f32),
            pltpu.VMEM((2, half, C * share), bf16),
            pltpu.VMEM((2, ff_local // chunk, half, chunk), f32),
            pltpu.VMEM((2, ff_local // chunk, half, chunk), bf16),
            pltpu.VMEM((2, ff_local // chunk, half, chunk), bf16),
            pltpu.VMEM((2, half, C * share), f32),
            pltpu.VMEM((2, C, half, share), bf16),
            pltpu.VMEM((2, C, half, share), bf16),
            pltpu.VMEM((2, C, half, share), bf16),
            pltpu.VMEM((2, R, C, STAT, LANES), f32),
            pltpu.VMEM((2, out_local // piece, half, piece), bf16),
            pltpu.VMEM((2, out_local // piece, half, piece), bf16),
            dma((G, 2)),
            dma((4,)),
            dma((G,)),
            dma((G,)),
            dma((G, R)),
            dma((G, R)),
            dma((G, R)),
            dma((G, R)),
            dma((2, C)),
            dma((2, C)),
            dma((2, C)),
            dma((2, C)),
            dma((2, R, C)),
            dma((2, R, C)),
            dma((2, ff_local // chunk)),
            dma((2, ff_local // chunk)),
            dma((2, C)),
            dma((2, C)),
            dma((2, C)),
            dma((2, C)),
            dma((2, R, C)),
            dma((2, R, C)),
            dma((2, out_local // piece)),
            dma((2, out_local // piece)),
        ],
        compiler_params=pltpu.CompilerParams(
            collective_id=0, has_side_effects=True, vmem_limit_bytes=64 * 1024 * 1024
        ),
        name="fused_layer",
    )(
        prefix_item,
        tail_item,
        prefix_length,
        tail_length,
        fresh,
        residual,
        *one_row,
        prefix_pages,
        tail_pages,
        out_weight,
        up_weight,
        down_weight,
        qkv_weight,
    )
    layer_out, scores, projected = pl.pallas_call(
        hand_out,
        out_shape=[jax.ShapeDtypeStruct(part.shape, part.dtype) for part in results],
        in_specs=[vmem] * 3,
        out_specs=[vmem] * 3,
        compiler_params=pltpu.CompilerParams(vmem_limit_bytes=64 * 1024 * 1024),
        name="hand_out",
    )(*results)
    return layer_out, scores.T, projected


def shards(residual, fresh_qkv, prefix_pages, *others):
    sizes = {axis: lax.axis_size(axis) for axis in ("pages", "row", "col")}
    share, tokens = residual.shape[2], prefix_pages.shape[2]
    if sizes["row"] == 2 and sizes["pages"] % 2 == 0 and share % LANES == 0 and tokens % 16 == 0:
        return fused_shards(sizes, residual, fresh_qkv, prefix_pages, *others)
    return plain_shards(residual, fresh_qkv, prefix_pages, *others)


def solution(mesh):
    in_specs = (
        P("pages", None, ("row", "col")),
        P("pages", None, None, "col"),
        P("pages", None, "row", "col"),
        P("pages", None, "row", "col"),
        P(),
        P(),
        P(),
        P(),
        P("col", "row"),
        P(("row", "col")),
        P("row"),
        P("row"),
        P("row", "col"),
        P(("col", "row")),
        P("col", "row"),
        P(("row", "col")),
        P("row"),
        P("row"),
        P("row"),
        P("row", "col"),
        P(("col", "row")),
    )
    out_specs = (
        P("pages", None, ("row", "col")),
        P("pages", None),
        P("pages", None, ("col", "row")),
    )
    return jax.shard_map(shards, mesh=mesh, in_specs=in_specs, out_specs=out_specs, check_vma=False)
```

```python
import math

import jax
import jax.numpy as jnp
from jax import lax
from jax.experimental import pallas as pl
from jax.experimental.pallas import tpu as pltpu
from jax.sharding import PartitionSpec as P

D = 2048
H = 16
HD = 128
PAGE = 128
MAXPAGES = 8
CONT = 16


masked_score = -1e30
norm_eps = 1e-05


def combined_all(shard, axis, combine):
    everything = jax.tree.map(lambda part: lax.all_gather(part, axis), shard)
    first = jax.tree.map(lambda part: part[0], everything)

    def step(k, so_far):
        return combine(so_far, jax.tree.map(lambda part: part[k], everything))

    return lax.fori_loop(1, lax.axis_size(axis), step, first)


def head_slopes(first_head, how_many):
    head_index = first_head + jnp.arange(how_many, dtype=jnp.int32)
    return jnp.exp2(-8.0 * (head_index + 1).astype(jnp.float32) / H)


def slot_partials(queries, page_keys, page_values, usable, offset, slopes):
    scores = jnp.einsum(
        "sqhd,skhd->sqhk", queries, page_keys, preferred_element_type=jnp.float32
    ) / math.sqrt(HD)
    scores = scores + slopes[None, None, :, None] * offset[:, :, None, :]
    usable_full = usable[:, :, None, :]
    scores = jnp.where(usable_full, scores, masked_score)
    maxima = jnp.max(scores, axis=3)
    weights = jnp.where(usable_full, jnp.exp(scores - maxima[..., None]), 0.0)
    totals = jnp.sum(weights, axis=3)
    outputs = jnp.einsum(
        "sqhk,skhd->sqhd", weights, page_values.astype(jnp.float32), precision=lax.Precision.HIGHEST
    )
    return (maxima, totals, outputs)


def merge_pair(left_part, right_part):
    left_max, left_total, left_out = left_part
    right_max, right_total, right_out = right_part
    joined = jnp.maximum(left_max, right_max)
    left_scale = jnp.exp(left_max - joined)
    right_scale = jnp.exp(right_max - joined)
    return (
        joined,
        left_scale * left_total + right_scale * right_total,
        left_scale[..., None] * left_out + right_scale[..., None] * right_out,
    )


def fold_sources(maxima, totals, outputs):
    joined = jnp.max(maxima, axis=0)
    rescale = jnp.exp(maxima - joined[None])
    return (
        joined,
        jnp.sum(rescale * totals, axis=0),
        jnp.sum(rescale[..., None] * outputs, axis=0),
    )


def cache_partials(
    queries,
    page_block,
    page_item,
    tail_block,
    tail_owner,
    prefix_length,
    tail_length,
    row_index,
    slopes,
):
    cont_count = queries.shape[0]
    prompts = cont_count // CONT
    head_count = queries.shape[2]
    slot_count = page_block.shape[0]
    tokens = page_block.shape[2]
    token_index = row_index * tokens + jnp.arange(tokens, dtype=jnp.int32)
    step_index = jnp.arange(2, dtype=jnp.int32)
    slot_prompt = page_item // MAXPAGES
    slot_page = page_item % MAXPAGES
    by_prompt = queries.reshape(prompts, CONT * 2, head_count, HD)
    key_pos = slot_page[:, None] * PAGE + token_index[None, :]
    slot_len = prefix_length[slot_prompt]
    slot_tails = tail_length.reshape(prompts, CONT)[slot_prompt]
    query_pos = (
        slot_len[:, None, None] + slot_tails[:, :, None] + step_index[None, None, :]
    ).reshape(slot_count, CONT * 2)
    offset = (key_pos[:, None, :] - query_pos[:, :, None]).astype(jnp.float32)
    usable = jnp.broadcast_to((key_pos < slot_len[:, None])[:, None, :], offset.shape)
    page_keys = page_block[:, 0].reshape(slot_count, tokens, head_count, HD)
    page_values = page_block[:, 1].reshape(slot_count, tokens, head_count, HD)
    maxima, totals, outputs = slot_partials(
        by_prompt[slot_prompt], page_keys, page_values, usable, offset, slopes
    )
    prompt_max = (
        jnp.full((prompts, CONT * 2, head_count), masked_score, jnp.float32)
        .at[slot_prompt]
        .max(maxima)
    )
    rescale = jnp.exp(maxima - prompt_max[slot_prompt])
    prompt_total = (
        jnp.zeros((prompts, CONT * 2, head_count), jnp.float32)
        .at[slot_prompt]
        .add(rescale * totals)
    )
    prompt_out = (
        jnp.zeros((prompts, CONT * 2, head_count, HD), jnp.float32)
        .at[slot_prompt]
        .add(rescale[..., None] * outputs)
    )
    prefix_part = (
        prompt_max.reshape(cont_count, 2, head_count),
        prompt_total.reshape(cont_count, 2, head_count),
        prompt_out.reshape(cont_count, 2, head_count, HD),
    )
    tail_count = tail_block.shape[0]
    tail_lens = tail_length[tail_owner]
    tail_usable = jnp.broadcast_to(
        (token_index[None, :] < tail_lens[:, None])[:, None, :], (tail_count, 2, tokens)
    )
    tail_offset = (
        token_index[None, None, :] - tail_lens[:, None, None] - step_index[None, :, None]
    ).astype(jnp.float32)
    tail_keys = tail_block[:, 0].reshape(tail_count, tokens, head_count, HD)
    tail_values = tail_block[:, 1].reshape(tail_count, tokens, head_count, HD)
    tail_max, tail_total, tail_out = slot_partials(
        queries[tail_owner], tail_keys, tail_values, tail_usable, tail_offset, slopes
    )
    cont_max = (
        jnp.full((cont_count, 2, head_count), masked_score, jnp.float32)
        .at[tail_owner]
        .set(tail_max)
    )
    cont_total = jnp.zeros((cont_count, 2, head_count), jnp.float32).at[tail_owner].set(tail_total)
    cont_out = jnp.zeros((cont_count, 2, head_count, HD), jnp.float32).at[tail_owner].set(tail_out)
    return merge_pair(prefix_part, (cont_max, cont_total, cont_out))


def normalize(values, sum_one, sum_two, gain, shift):
    center = sum_one / D
    spread = sum_two / D - center * center
    return (
        (values - center[:, None])
        * lax.rsqrt(spread + norm_eps)[:, None]
        * gain.astype(jnp.float32)
        + shift.astype(jnp.float32)
    ).astype(jnp.bfloat16)


def plain_shards(
    residual,
    fresh_qkv,
    prefix_pages,
    tail_pages,
    prefix_item,
    tail_item,
    prefix_length,
    tail_length,
    out_weight,
    out_bias,
    mlp_gain,
    mlp_shift,
    up_weight,
    up_bias,
    down_weight,
    down_bias,
    next_gain,
    next_shift,
    score_weight,
    qkv_weight,
    qkv_bias,
):
    group_index = lax.axis_index("pages")
    row_index = lax.axis_index("row")
    col_index = lax.axis_index("col")
    group_count = lax.axis_size("pages")
    cont_local = residual.shape[0]
    row_total = cont_local * 2
    share = residual.shape[2]
    head_count = fresh_qkv.shape[3] // HD
    slopes = head_slopes(col_index * head_count, head_count)
    fresh_rows = fresh_qkv.reshape(cont_local, 2, 3, head_count, HD)
    slot_count = prefix_pages.shape[0]
    tail_slots = tail_pages.shape[0]
    everyone = lax.all_gather(fresh_qkv[:, :, 0], "pages", axis=0, tiled=True)
    page_item = lax.dynamic_slice_in_dim(prefix_item, group_index * slot_count, slot_count)
    tail_owner = lax.dynamic_slice_in_dim(tail_item, group_index * tail_slots, tail_slots)
    maxima, totals, outputs = cache_partials(
        everyone.reshape(everyone.shape[0], 2, head_count, HD),
        prefix_pages,
        page_item,
        tail_pages,
        tail_owner,
        prefix_length,
        tail_length,
        row_index,
        slopes,
    )
    maxima, totals, outputs = (
        lax.all_to_all(
            maxima.reshape(group_count, row_total, head_count),
            "pages",
            split_axis=0,
            concat_axis=0,
            tiled=True,
        ),
        lax.all_to_all(
            totals.reshape(group_count, row_total, head_count),
            "pages",
            split_axis=0,
            concat_axis=0,
            tiled=True,
        ),
        lax.all_to_all(
            outputs.reshape(group_count, row_total, head_count, HD),
            "pages",
            split_axis=0,
            concat_axis=0,
            tiled=True,
        ),
    )
    cache_max, cache_total, cache_out = fold_sources(maxima, totals, outputs)
    cache_max, cache_total, cache_out = combined_all(
        (cache_max, cache_total, cache_out), "row", merge_pair
    )
    step_index = jnp.arange(2, dtype=jnp.int32)
    new_usable = jnp.broadcast_to(
        (step_index[None, :] <= step_index[:, None])[None], (cont_local, 2, 2)
    )
    new_offset = jnp.broadcast_to(
        (step_index[None, :] - step_index[:, None]).astype(jnp.float32)[None], (cont_local, 2, 2)
    )
    new_part = slot_partials(
        fresh_rows[:, :, 0],
        fresh_rows[:, :, 1],
        fresh_rows[:, :, 2],
        new_usable,
        new_offset,
        slopes,
    )
    joined_max, joined_total, joined_out = merge_pair(
        (
            cache_max.reshape(cont_local, 2, head_count),
            cache_total.reshape(cont_local, 2, head_count),
            cache_out.reshape(cont_local, 2, head_count, HD),
        ),
        new_part,
    )
    attended = (
        (joined_out / joined_total[..., None])
        .astype(jnp.bfloat16)
        .reshape(row_total, head_count * HD)
    )
    head_term = jnp.dot(attended, out_weight, preferred_element_type=jnp.float32)
    hidden_one = (
        residual.reshape(row_total, share).astype(jnp.float32)
        + lax.psum_scatter(head_term, "col", scatter_dimension=1, tiled=True)
        + out_bias.astype(jnp.float32)
    )
    gain_part = lax.dynamic_slice_in_dim(mlp_gain, col_index * share, share)
    shift_part = lax.dynamic_slice_in_dim(mlp_shift, col_index * share, share)
    sum_one, sum_two = lax.psum(
        (jnp.sum(hidden_one, axis=1), jnp.sum(hidden_one * hidden_one, axis=1)), ("row", "col")
    )
    normed_a = lax.all_gather(
        normalize(hidden_one, sum_one, sum_two, gain_part, shift_part), "col", axis=1, tiled=True
    )
    up_share = lax.psum_scatter(
        jnp.dot(normed_a, up_weight, preferred_element_type=jnp.float32),
        "row",
        scatter_dimension=1,
        tiled=True,
    )
    hidden_two = jax.nn.gelu(up_share + up_bias.astype(jnp.float32), approximate=True).astype(
        jnp.bfloat16
    )
    down_sum = jnp.dot(
        lax.all_gather(hidden_two, "row", axis=1, tiled=True),
        down_weight,
        preferred_element_type=jnp.float32,
    )
    down_share = lax.psum_scatter(
        down_sum.astype(jnp.bfloat16), "col", scatter_dimension=1, tiled=True
    ).astype(jnp.float32)
    layer_out = (hidden_one + down_share + down_bias.astype(jnp.float32)).astype(jnp.bfloat16)
    out_wide = layer_out.astype(jnp.float32)
    gain_part = lax.dynamic_slice_in_dim(next_gain, col_index * share, share)
    shift_part = lax.dynamic_slice_in_dim(next_shift, col_index * share, share)
    score_part = lax.dynamic_slice_in_dim(score_weight, col_index * share, share).astype(
        jnp.float32
    )
    sum_one, sum_two, score_sum = lax.psum(
        (
            jnp.sum(out_wide, axis=1),
            jnp.sum(out_wide * out_wide, axis=1),
            jnp.sum(out_wide * score_part, axis=1),
        ),
        ("row", "col"),
    )
    normed_b = lax.all_gather(
        normalize(out_wide, sum_one, sum_two, gain_part, shift_part), "col", axis=1, tiled=True
    )
    qkv_share = lax.psum_scatter(
        jnp.dot(normed_b, qkv_weight, preferred_element_type=jnp.float32).astype(jnp.bfloat16),
        "row",
        scatter_dimension=1,
        tiled=True,
    ).astype(jnp.float32)
    projected_next = (qkv_share + qkv_bias.astype(jnp.float32)).astype(jnp.bfloat16)
    return (
        layer_out.reshape(cont_local, 2, share),
        score_sum.reshape(cont_local, 2),
        projected_next.reshape(cont_local, 2, qkv_share.shape[1]),
    )


empty_floor = -1e20
STAT = 8
LANES = 128


def columns_to_tile(columns):
    rows = columns[0].shape[0]
    lane = lax.broadcasted_iota(jnp.int32, (rows, LANES), 1)
    wide = jnp.zeros((rows, LANES), jnp.float32)
    for k, column in enumerate(columns):
        wide = jnp.where(lane == k, column, wide)
    if rows < LANES:
        wide = jnp.concatenate([wide, jnp.zeros((LANES - rows, LANES), jnp.float32)], axis=0)
    return jnp.transpose(wide)[:STAT]


def tile_to_columns(tile, rows):
    have = tile.shape[0]
    if have < LANES:
        tile = jnp.concatenate([tile, jnp.zeros((LANES - have, LANES), jnp.float32)], axis=0)
    return jnp.transpose(tile)[:rows]


def split_level(tile, width):
    high = tile.astype(jnp.bfloat16).astype(jnp.float32)
    middle = (tile - high).astype(jnp.bfloat16).astype(jnp.float32)
    parts = [high, middle, tile - high - middle]
    parts += [jnp.zeros_like(tile)] * (width // LANES - len(parts))
    block = jnp.concatenate(parts, axis=1)
    return jnp.concatenate([block, jnp.zeros_like(block)], axis=0).astype(jnp.bfloat16)


def join_level(block):
    parts = block.astype(jnp.float32)[:STAT]
    return parts[:, :LANES] + parts[:, LANES : 2 * LANES] + parts[:, 2 * LANES : 3 * LANES]


def layer_kernel(
    sizes,
    item_hbm,
    owner_hbm,
    length_hbm,
    span_hbm,
    fresh_hbm,
    residual_hbm,
    out_bias_hbm,
    mlp_gain_hbm,
    mlp_shift_hbm,
    up_bias_hbm,
    down_bias_hbm,
    next_gain_hbm,
    next_shift_hbm,
    score_hbm,
    qkv_bias_hbm,
    prefix_hbm,
    tail_hbm,
    out_hbm,
    up_hbm,
    down_hbm,
    qkv_hbm,
    layer_ref,
    score_ref,
    proj_ref,
    prefix_item,
    tail_item,
    prefix_length,
    tail_length,
    tail_row,
    fresh_raw,
    residual,
    out_bias,
    mlp_gain,
    mlp_shift,
    up_bias,
    down_bias,
    next_gain,
    next_shift,
    score_weight,
    qkv_bias,
    fresh,
    new_out,
    small_sem,
    prefix_v,
    tail_v,
    out_w,
    up_w,
    down_w,
    qkv_w,
    q_buf,
    p_stage,
    p_buf,
    att,
    a_stage,
    a_buf,
    hidden,
    x_buf,
    s_buf,
    normed,
    u_own,
    u_stage,
    u_buf,
    acc,
    d_stage,
    d_buf,
    y_buf,
    t_buf,
    z_stage,
    z_buf,
    page_sem,
    w_sem,
    q_send,
    q_recv,
    p_send,
    p_recv,
    a_send,
    a_recv,
    x_send,
    x_recv,
    s_send,
    s_recv,
    u_send,
    u_recv,
    d_send,
    d_recv,
    y_send,
    y_recv,
    t_send,
    t_recv,
    z_send,
    z_recv,
):
    G, R, C = sizes["pages"], sizes["row"], sizes["col"]
    f32, bf16, i32 = jnp.float32, jnp.bfloat16, jnp.int32
    me = lax.axis_index("pages")
    row = lax.axis_index("row")
    col = lax.axis_index("col")
    rows = fresh.shape[1]
    share = residual.shape[2]
    width = C * share
    heads = fresh.shape[2] // HD
    slots, _, tokens, _ = prefix_v.shape
    tails = tail_v.shape[0]
    pair_pages, pair_tails = slots // G, tails // G
    _, chunks, _, chunk = u_buf.shape
    _, pieces, _, piece = z_buf.shape

    def group_at(i):
        if isinstance(i, int) and i == 0:
            return me
        j = lax.rem(jnp.int32(i), G - 1) + 1
        return lax.rem(lax.div(me, 2) + lax.div(j, 2), G // 2) * 2 + lax.rem(me + j, 2)

    def row_at(k):
        return lax.rem(row + k, R)

    def col_at(k):
        return lax.rem(col + k, C)

    def remote(src, dst, send_sem, recv_sem, target):
        return pltpu.make_async_remote_copy(
            src_ref=src,
            dst_ref=dst,
            send_sem=send_sem,
            recv_sem=recv_sem,
            device_id=target,
            device_id_type=pl.DeviceIdType.MESH,
        )

    def prefix_copy(g):
        part = pl.ds(g * pair_pages, pair_pages)
        return pltpu.make_async_copy(prefix_hbm.at[part], prefix_v.at[part], page_sem.at[g, 0])

    def tail_copy(g):
        part = pl.ds(g * pair_tails, pair_tails)
        return pltpu.make_async_copy(tail_hbm.at[part], tail_v.at[part], page_sem.at[g, 1])

    weight_copies = [
        pltpu.make_async_copy(src, dst, w_sem.at[k])
        for k, (src, dst) in enumerate(
            ((out_hbm, out_w), (up_hbm, up_w), (down_hbm, down_w), (qkv_hbm, qkv_w))
        )
    ]

    small_pairs = (
        (fresh_hbm, fresh_raw),
        (item_hbm, prefix_item),
        (owner_hbm, tail_item),
        (length_hbm, prefix_length),
        (span_hbm, tail_length),
        (span_hbm, tail_row),
        (residual_hbm, residual),
        (out_bias_hbm, out_bias),
        (mlp_gain_hbm, mlp_gain),
        (mlp_shift_hbm, mlp_shift),
        (up_bias_hbm, up_bias),
        (down_bias_hbm, down_bias),
        (next_gain_hbm, next_gain),
        (next_shift_hbm, next_shift),
        (score_hbm, score_weight),
        (qkv_bias_hbm, qkv_bias),
    )
    small_copies = [
        pltpu.make_async_copy(src, dst, small_sem.at[k])
        for k, (src, dst) in enumerate(small_pairs)
    ]

    barrier = pltpu.get_barrier_semaphore()
    met = 0
    for i in range(G):
        for k in range(R):
            if i or k:
                met += 1
                pl.semaphore_signal(
                    barrier,
                    inc=1,
                    device_id=(group_at(i), row_at(k), col),
                    device_id_type=pl.DeviceIdType.MESH,
                )
    for k in range(R):
        for j in range(1, C):
            met += 1
            pl.semaphore_signal(
                barrier,
                inc=1,
                device_id=(me, row_at(k), col_at(j)),
                device_id_type=pl.DeviceIdType.MESH,
            )
    for copy in small_copies[:6]:
        copy.start()
    for i in range(G):
        prefix_copy(group_at(i)).start()
        tail_copy(group_at(i)).start()
    for copy in small_copies[6:]:
        copy.start()

    row_id = lax.broadcasted_iota(i32, (rows, 1), 0)
    step = lax.rem(row_id, 2)
    row_cont = lax.div(row_id, 2)
    contract_last = (((1,), (1,)), ((), ()))
    scale = 1.0 / math.sqrt(HD)

    def slope_row(h, size):
        index = jnp.full((1, size), col * heads + h + 1, i32).astype(f32)
        return jnp.exp(index * (-8.0 / H * math.log(2.0)))

    small_copies[0].wait()
    for part in range(3):
        fresh[part] = fresh_raw[:, part].reshape(rows, heads * HD)
    q_buf[me] = fresh[0]
    key_id = lax.broadcasted_iota(i32, (rows, rows), 1)
    new_ok = jnp.logical_and(lax.div(key_id, 2) == row_cont, lax.rem(key_id, 2) <= step)
    new_gap = jnp.where(new_ok, (lax.rem(key_id, 2) - step).astype(f32), masked_score)
    levels = []
    for h in range(heads):
        hs = slice(h * HD, (h + 1) * HD)
        scores = (
            lax.dot_general(
                fresh[0, :, hs], fresh[1, :, hs], contract_last, preferred_element_type=f32
            )
            * scale
            + slope_row(h, rows) * new_gap
        )
        top = jnp.max(scores, axis=1, keepdims=True)
        weights = jnp.exp(scores - top)
        total = jnp.sum(weights, axis=1, keepdims=True)
        new_out[:, hs] = (
            jnp.dot(weights.astype(bf16), fresh[2, :, hs], preferred_element_type=f32) / total
        )
        levels.append(top + jnp.log(total))
    new_level = columns_to_tile(levels)

    pl.semaphore_wait(barrier, met)

    sends = []
    for i in range(1, G):
        copy = remote(
            fresh.at[0],
            q_buf.at[me],
            q_send.at[i],
            q_recv.at[me],
            (group_at(i), row, col),
        )
        copy.start()
        sends.append(copy)
    for copy in weight_copies:
        copy.start()
    for copy in small_copies[1:]:
        copy.wait()

    def attend(i):
        g = group_at(i)
        prefix_copy(g).wait()
        tail_copy(g).wait()
        cont = g * lax.div(rows, 2) + row_cont
        prompt_of_row = lax.div(cont, CONT)
        spots = lax.broadcasted_iota(i32, (rows, tail_row.shape[0]), 1)
        tail_spans = tail_row[...].reshape(1, tail_row.shape[0]).astype(f32)
        own_tail = jnp.sum(
            jnp.where(spots == cont, tail_spans, 0.0), axis=1, keepdims=True
        )
        query_off = own_tail + step.astype(f32)

        lane = lax.broadcasted_iota(i32, (1, pair_pages * tokens), 1)
        slot = lax.div(lane, tokens)
        token = lax.rem(lane, tokens) + row * tokens
        owner = jnp.zeros_like(lane)
        place = jnp.zeros_like(lane)
        length = jnp.zeros_like(lane)
        for k in range(pair_pages):
            item = prefix_item[me * slots + g * pair_pages + k]
            prompt = lax.div(item, MAXPAGES)
            hit = slot == k
            owner = jnp.where(hit, prompt, owner)
            place = jnp.where(hit, (item - prompt * MAXPAGES) * PAGE, place)
            length = jnp.where(hit, prefix_length[prompt], length)
        place = place + token
        gap = (place - length).astype(f32)
        open_prompt = jnp.where(place < length, owner, -1)
        prefix_gap = jnp.where(open_prompt == prompt_of_row, gap - query_off, masked_score)

        lane = lax.broadcasted_iota(i32, (1, pair_tails * tokens), 1)
        slot = lax.div(lane, tokens)
        token = lax.rem(lane, tokens) + row * tokens
        owner = jnp.zeros_like(lane)
        length = jnp.zeros_like(lane)
        for k in range(pair_tails):
            item = tail_item[me * tails + g * pair_tails + k]
            hit = slot == k
            owner = jnp.where(hit, item, owner)
            length = jnp.where(hit, tail_length[item], length)
        gap = (token - length).astype(f32)
        open_cont = jnp.where(token < length, owner, -1)
        tail_gap = jnp.where(open_cont == cont, gap - step.astype(f32), masked_score)

        pre = pl.ds(g * pair_pages, pair_pages)
        tai = pl.ds(g * pair_tails, pair_tails)
        levels = []
        for h in range(heads):
            hs = slice(h * HD, (h + 1) * HD)
            query = q_buf[g, :, hs]
            keys = prefix_v[pre, 0, :, hs].reshape(pair_pages * tokens, HD)
            tail_keys = tail_v[tai, 0, :, hs].reshape(pair_tails * tokens, HD)
            s_one = (
                lax.dot_general(query, keys, contract_last, preferred_element_type=f32) * scale
                + slope_row(h, pair_pages * tokens) * prefix_gap
            )
            s_two = (
                lax.dot_general(query, tail_keys, contract_last, preferred_element_type=f32)
                * scale
                + slope_row(h, pair_tails * tokens) * tail_gap
            )
            top = jnp.maximum(
                jnp.max(s_one, axis=1, keepdims=True), jnp.max(s_two, axis=1, keepdims=True)
            )
            top = jnp.maximum(top, empty_floor)
            w_one = jnp.exp(s_one - top)
            w_two = jnp.exp(s_two - top)
            total = jnp.sum(w_one, axis=1, keepdims=True) + jnp.sum(w_two, axis=1, keepdims=True)
            total = jnp.maximum(total, 1e-30)
            values = prefix_v[pre, 1, :, hs].reshape(pair_pages * tokens, HD)
            tail_values = tail_v[tai, 1, :, hs].reshape(pair_tails * tokens, HD)
            out = jnp.dot(w_one.astype(bf16), values, preferred_element_type=f32) + jnp.dot(
                w_two.astype(bf16), tail_values, preferred_element_type=f32
            )
            p_stage[g, :rows, hs] = (out / total).astype(bf16)
            levels.append(top + jnp.log(total))
        p_stage[g, rows:, :] = split_level(columns_to_tile(levels), heads * HD)

    def partial_copy(i, k):
        g = group_at(i)
        return remote(
            p_stage.at[g],
            p_buf.at[me, row],
            p_send.at[g, k],
            p_recv.at[me, row],
            (g, row_at(k), col),
        )

    def partial_arrival(i, k):
        g, r = group_at(i), row_at(k)
        return remote(
            p_stage.at[g], p_buf.at[g, r], p_send.at[g, k], p_recv.at[g, r], (g, r, col)
        )

    attend(0)
    for k in range(1, R):
        partial_copy(0, k).start()
    p_buf[me, row] = p_stage[me]

    def next_group(i, carry):
        g = group_at(i)
        remote(fresh.at[0], q_buf.at[g], q_send.at[i], q_recv.at[g], (g, row, col)).wait_recv()
        attend(i)
        for k in range(R):
            partial_copy(i, k).start()
        return carry

    lax.fori_loop(1, G, next_group, 0)

    for i in range(G):
        for k in range(R):
            if i or k:
                partial_arrival(i, k).wait_recv()

    peers = [join_level(p_buf[g, r, rows:, :]) for g in range(G) for r in range(R)] + [new_level]
    peak = peers[0]
    for level in peers[1:]:
        peak = jnp.maximum(peak, level)
    shares = [jnp.exp(level - peak) for level in peers]
    total = shares[0]
    for part in shares[1:]:
        total = total + part
    scaled = [part / total for part in shares]
    groups_of_tiles = [
        tile_to_columns(jnp.concatenate(scaled[at : at + LANES // STAT], axis=0), rows)
        for at in range(0, len(scaled), LANES // STAT)
    ]

    def weight_of(peer, h):
        block, spot = divmod(peer, LANES // STAT)
        at = spot * STAT + h
        return groups_of_tiles[block][:, at : at + 1]

    def merge(b):
        part = slice(b * half_rows, (b + 1) * half_rows)
        for h in range(heads):
            hs = slice(h * HD, (h + 1) * HD)
            joined = weight_of(G * R, h)[part] * new_out[part, hs]
            for g in range(G):
                for r in range(R):
                    share_now = weight_of(g * R + r, h)[part]
                    joined = joined + share_now * p_buf[g, r, part, hs].astype(f32)
            att[part, hs] = joined.astype(bf16)

    def share_of(k):
        return pl.ds(pl.multiple_of(col_at(k) * share, LANES), share)

    half_rows = rows // 2
    partner = (me, row_at(1), col)
    per_row = chunks // R
    last = chunks - 1

    def vector(ref):
        return ref[...].astype(f32).reshape(1, ref.shape[0])

    def push(src, dst, send_sem, recv_sem, target):
        copy = remote(src, dst, send_sem, recv_sem, target)
        copy.start()
        sends.append(copy)

    def project_out(b):
        part = att[b * half_rows : (b + 1) * half_rows, :]
        for k in range(1, C):
            a_stage[b, k] = jnp.dot(
                part, out_w[:, share_of(k)], preferred_element_type=f32
            ).astype(bf16)
            push(
                a_stage.at[b, k],
                a_buf.at[b, col],
                a_send.at[b, k],
                a_recv.at[b, col],
                (me, row, col_at(k)),
            )
        stream = residual[b * half_rows // 2 : (b + 1) * half_rows // 2].astype(f32)
        hidden[b] = (
            jnp.dot(part, out_w[:, share_of(0)], preferred_element_type=f32)
            + stream.reshape(half_rows, share)
            + vector(out_bias)
        )

    def summed(b, total, stage, buf, send, recv):
        for k in range(1, C):
            src = col_at(C - k)
            remote(
                stage.at[b, k], buf.at[b, src], send.at[b, k], recv.at[b, src], (me, row, src)
            ).wait_recv()
            total = total + buf[b, src].astype(f32)
        return total

    def gather_start(b, own, parts, wide_buf, wide_send, wide_recv, small_buf, small_send, small_recv):
        wide_buf[b, col] = own
        small_buf[b, row, col] = columns_to_tile(
            [jnp.sum(part, axis=1, keepdims=True) for part in parts]
        )
        for k in range(R):
            for j in range(C):
                if k or j:
                    push(
                        small_buf.at[b, row, col],
                        small_buf.at[b, row, col],
                        small_send.at[b, k, j],
                        small_recv.at[b, row, col],
                        (me, row_at(k), col_at(j)),
                    )
        for j in range(1, C):
            push(
                wide_buf.at[b, col],
                wide_buf.at[b, col],
                wide_send.at[b, j],
                wide_recv.at[b, col],
                (me, row, col_at(j)),
            )

    def gather_norm(
        b, gain, shift, wide_buf, wide_send, wide_recv, small_buf, small_send, small_recv
    ):
        for k in range(R):
            for j in range(C):
                if k or j:
                    r, c = row_at(k), col_at(j)
                    remote(
                        small_buf.at[b, row, col],
                        small_buf.at[b, r, c],
                        small_send.at[b, k, j],
                        small_recv.at[b, r, c],
                        (me, r, c),
                    ).wait_recv()
        sums = small_buf[b, 0, 0]
        for k in range(1, R * C):
            sums = sums + small_buf[b, k // C, k % C]
        columns = tile_to_columns(sums, half_rows)
        center = columns[:, 0:1] / D
        spread = columns[:, 1:2] / D - center * center
        factor = lax.rsqrt(spread + norm_eps)
        gains, shifts = vector(gain), vector(shift)
        for j in range(1, C):
            c = col_at(j)
            remote(
                wide_buf.at[b, col],
                wide_buf.at[b, c],
                wide_send.at[b, j],
                wide_recv.at[b, c],
                (me, row, c),
            ).wait_recv()
        for c in range(C):
            at = slice(c * share, (c + 1) * share)
            normed[b, :, at] = (
                (wide_buf[b, c].astype(f32) - center) * factor * gains[:, at] + shifts[:, at]
            ).astype(bf16)
        return columns

    first_gather = (x_buf, x_send, x_recv, s_buf, s_send, s_recv)
    second_gather = (y_buf, y_send, y_recv, t_buf, t_send, t_recv)

    def up_copy(b, n):
        return (u_stage.at[b, n], u_buf.at[b, n], u_send.at[b, n], u_recv.at[b, n], partner)

    def project_up(b):
        up_shift = vector(up_bias)
        for n in range(chunks):
            part = jnp.dot(
                normed[b], up_w[:, n * chunk : (n + 1) * chunk], preferred_element_type=f32
            )
            mine = jnp.where(jnp.full((1, chunk), row, i32) == n // per_row, 1.0, 0.0)
            spot = n % per_row
            part = part + mine * up_shift[:, spot * chunk : (spot + 1) * chunk]
            u_own[b, n] = part
            u_stage[b, n] = part.astype(bf16)
            push(*up_copy(b, n))

    def project_down(b):
        for n in range(chunks):
            remote(*up_copy(b, n)).wait_recv()
            v = u_own[b, n] + u_buf[b, n].astype(f32)
            gelu = (
                0.5 * v * (1.0 + jnp.tanh(0.7978845608 * (v + 0.044715 * (v * v * v))))
            ).astype(bf16)
            if n < last:
                term = jnp.dot(
                    gelu, down_w[n * chunk : (n + 1) * chunk, :], preferred_element_type=f32
                )
                acc[b] = term if n == 0 else acc[b] + term

        def down_for(k):
            return acc[b, :, share_of(k)] + jnp.dot(
                gelu, down_w[last * chunk :, share_of(k)], preferred_element_type=f32
            )

        for k in range(1, C):
            d_stage[b, k] = down_for(k).astype(bf16)
            push(
                d_stage.at[b, k],
                d_buf.at[b, col],
                d_send.at[b, k],
                d_recv.at[b, col],
                (me, row, col_at(k)),
            )
        hidden[b] = hidden[b] + down_for(0) + vector(down_bias)

    half = pieces * piece

    def qkv_piece(b, r, n):
        at = pl.ds(pl.multiple_of(r * half + n * piece, LANES), piece)
        return jnp.dot(normed[b], qkv_w[:, at], preferred_element_type=f32)

    def z_copy(b, n):
        return (z_stage.at[b, n], z_buf.at[b, n], z_send.at[b, n], z_recv.at[b, n], partner)

    weight_copies[0].wait()
    for b in range(2):
        merge(b)
        project_out(b)
    for b in range(2):
        total = summed(b, hidden[b], a_stage, a_buf, a_send, a_recv)
        hidden[b] = total
        gather_start(b, total.astype(bf16), [total, total * total], *first_gather)
    weight_copies[1].wait()
    for b in range(2):
        gather_norm(b, mlp_gain, mlp_shift, *first_gather)
        project_up(b)
    weight_copies[2].wait()
    for b in range(2):
        project_down(b)

    scores = vector(score_weight)
    score_part = scores[:, :share]
    for c in range(1, C):
        score_part = jnp.where(
            jnp.full((1, share), col, i32) == c, scores[:, c * share : (c + 1) * share], score_part
        )
    quarter = half_rows // 2
    for b in range(2):
        layer_out = summed(b, hidden[b], d_stage, d_buf, d_send, d_recv).astype(bf16)
        wide = layer_out.astype(f32)
        gather_start(b, layer_out, [wide, wide * wide, wide * score_part], *second_gather)
        layer_ref[b * quarter : (b + 1) * quarter] = wide.reshape(quarter, 2, share).astype(bf16)
    weight_copies[3].wait()
    score_columns = []
    for b in range(2):
        columns = gather_norm(b, next_gain, next_shift, *second_gather)
        score_columns.append(columns[:, 2:3])
        for n in range(pieces):
            z_stage[b, n] = qkv_piece(b, row_at(1), n).astype(bf16)
            push(*z_copy(b, n))
    seat = lax.broadcasted_iota(i32, (rows, rows // 2), 1)
    score_column = jnp.concatenate(score_columns, axis=0)
    score_ref[...] = jnp.concatenate(
        [
            jnp.sum(jnp.where(row_id == seat * 2 + u, score_column, 0.0), axis=0, keepdims=True)
            for u in range(2)
        ],
        axis=0,
    )
    qkv_shift = vector(qkv_bias)
    for b in range(2):
        for n in range(pieces):
            at = slice(n * piece, (n + 1) * piece)
            own = qkv_piece(b, row, n) + qkv_shift[:, at]
            remote(*z_copy(b, n)).wait_recv()
            own = own + z_buf[b, n].astype(f32)
            proj_ref[b * quarter : (b + 1) * quarter, :, at] = own.reshape(
                quarter, 2, piece
            ).astype(bf16)

    for copy in sends:
        copy.wait_send()
    for i in range(G):
        for k in range(R):
            if i or k:
                partial_copy(i, k).wait_send()


def hand_out(*refs):
    for k in range(3):
        refs[3 + k][...] = refs[k][...]


def fused_shards(
    sizes,
    residual,
    fresh_qkv,
    prefix_pages,
    tail_pages,
    prefix_item,
    tail_item,
    prefix_length,
    tail_length,
    out_weight,
    out_bias,
    mlp_gain,
    mlp_shift,
    up_weight,
    up_bias,
    down_weight,
    down_bias,
    next_gain,
    next_shift,
    score_weight,
    qkv_weight,
    qkv_bias,
):
    G, R, C = sizes["pages"], sizes["row"], sizes["col"]
    f32, bf16 = jnp.float32, jnp.bfloat16
    cont_local, _, share = residual.shape
    rows = cont_local * 2
    half = rows // 2
    head_width = fresh_qkv.shape[3]
    ff_local = up_weight.shape[1]
    out_local = qkv_bias.shape[0]
    chunk = ff_local // 4
    piece = out_local
    fresh = fresh_qkv.transpose(0, 2, 1, 3)
    one_row = (out_bias, mlp_gain, mlp_shift, up_bias, down_bias)
    one_row = one_row + (next_gain, next_shift, score_weight, qkv_bias)
    vmem = pl.BlockSpec(memory_space=pltpu.VMEM)
    hbm = pl.BlockSpec(memory_space=pltpu.MemorySpace.HBM)
    dma = pltpu.SemaphoreType.DMA
    results = pl.pallas_call(
        lambda *refs: layer_kernel(sizes, *refs),
        out_shape=(
            jax.ShapeDtypeStruct((cont_local, 2, share), bf16),
            jax.ShapeDtypeStruct((2, cont_local), f32),
            jax.ShapeDtypeStruct((cont_local, 2, out_local), bf16),
        ),
        in_specs=[hbm] * (12 + len(one_row)),
        out_specs=(vmem, vmem, vmem),
        scratch_shapes=[
            pltpu.SMEM(prefix_item.shape, jnp.int32),
            pltpu.SMEM(tail_item.shape, jnp.int32),
            pltpu.SMEM(prefix_length.shape, jnp.int32),
            pltpu.SMEM(tail_length.shape, jnp.int32),
            pltpu.VMEM(tail_length.shape, jnp.int32),
            pltpu.VMEM(fresh.shape, bf16),
            pltpu.VMEM(residual.shape, bf16),
            *(pltpu.VMEM(v.shape, bf16) for v in one_row),
            pltpu.VMEM((3, rows, head_width), bf16),
            pltpu.VMEM((rows, head_width), f32),
            dma((7 + len(one_row),)),
            pltpu.VMEM(prefix_pages.shape, bf16),
            pltpu.VMEM(tail_pages.shape, bf16),
            pltpu.VMEM(out_weight.shape, bf16),
            pltpu.VMEM(up_weight.shape, bf16),
            pltpu.VMEM(down_weight.shape, bf16),
            pltpu.VMEM(qkv_weight.shape, bf16),
            pltpu.VMEM((G, rows, head_width), bf16),
            pltpu.VMEM((G, rows + 2 * STAT, head_width), bf16),
            pltpu.VMEM((G, R, rows + 2 * STAT, head_width), bf16),
            pltpu.VMEM((rows, head_width), bf16),
            pltpu.VMEM((2, C, half, share), bf16),
            pltpu.VMEM((2, C, half, share), bf16),
            pltpu.VMEM((2, half, share), f32),
            pltpu.VMEM((2, C, half, share), bf16),
            pltpu.VMEM((2, R, C, STAT, LANES), f32),
            pltpu.VMEM((2, half, C * share), bf16),
            pltpu.VMEM((2, ff_local // chunk, half, chunk), f32),
            pltpu.VMEM((2, ff_local // chunk, half, chunk), bf16),
            pltpu.VMEM((2, ff_local // chunk, half, chunk), bf16),
            pltpu.VMEM((2, half, C * share), f32),
            pltpu.VMEM((2, C, half, share), bf16),
            pltpu.VMEM((2, C, half, share), bf16),
            pltpu.VMEM((2, C, half, share), bf16),
            pltpu.VMEM((2, R, C, STAT, LANES), f32),
            pltpu.VMEM((2, out_local // piece, half, piece), bf16),
            pltpu.VMEM((2, out_local // piece, half, piece), bf16),
            dma((G, 2)),
            dma((4,)),
            dma((G,)),
            dma((G,)),
            dma((G, R)),
            dma((G, R)),
            dma((2, C)),
            dma((2, C)),
            dma((2, C)),
            dma((2, C)),
            dma((2, R, C)),
            dma((2, R, C)),
            dma((2, ff_local // chunk)),
            dma((2, ff_local // chunk)),
            dma((2, C)),
            dma((2, C)),
            dma((2, C)),
            dma((2, C)),
            dma((2, R, C)),
            dma((2, R, C)),
            dma((2, out_local // piece)),
            dma((2, out_local // piece)),
        ],
        compiler_params=pltpu.CompilerParams(
            collective_id=0, has_side_effects=True, vmem_limit_bytes=64 * 1024 * 1024
        ),
        name="fused_layer",
    )(
        prefix_item,
        tail_item,
        prefix_length,
        tail_length,
        fresh,
        residual,
        *one_row,
        prefix_pages,
        tail_pages,
        out_weight,
        up_weight,
        down_weight,
        qkv_weight,
    )
    layer_out, scores, projected = pl.pallas_call(
        hand_out,
        out_shape=[jax.ShapeDtypeStruct(part.shape, part.dtype) for part in results],
        in_specs=[vmem] * 3,
        out_specs=[vmem] * 3,
        compiler_params=pltpu.CompilerParams(vmem_limit_bytes=64 * 1024 * 1024),
        name="hand_out",
    )(*results)
    return layer_out, scores.T, projected


def shards(residual, fresh_qkv, prefix_pages, *others):
    sizes = {axis: lax.axis_size(axis) for axis in ("pages", "row", "col")}
    share, tokens, width = residual.shape[2], prefix_pages.shape[2], fresh_qkv.shape[3]
    whole = share % LANES == 0 and tokens % 16 == 0 and width >= 3 * LANES
    if sizes["row"] == 2 and sizes["pages"] % 2 == 0 and whole:
        return fused_shards(sizes, residual, fresh_qkv, prefix_pages, *others)
    return plain_shards(residual, fresh_qkv, prefix_pages, *others)


def solution(mesh):
    in_specs = (
        P("pages", None, ("row", "col")),
        P("pages", None, None, "col"),
        P("pages", None, "row", "col"),
        P("pages", None, "row", "col"),
        P(),
        P(),
        P(),
        P(),
        P("col", "row"),
        P(("row", "col")),
        P("row"),
        P("row"),
        P("row", "col"),
        P(("col", "row")),
        P("col", "row"),
        P(("row", "col")),
        P("row"),
        P("row"),
        P("row"),
        P("row", "col"),
        P(("col", "row")),
    )
    out_specs = (
        P("pages", None, ("row", "col")),
        P("pages", None),
        P("pages", None, ("col", "row")),
    )
    return jax.shard_map(shards, mesh=mesh, in_specs=in_specs, out_specs=out_specs, check_vma=False)
```

```python
import math

import jax
import jax.numpy as jnp
from jax import lax
from jax.experimental import pallas as pl
from jax.experimental.pallas import tpu as pltpu
from jax.sharding import PartitionSpec as P

D = 2048
H = 16
HD = 128
PAGE = 128
MAXPAGES = 8
CONT = 16


masked_score = -1e30
norm_eps = 1e-05


def combined_all(shard, axis, combine):
    everything = jax.tree.map(lambda part: lax.all_gather(part, axis), shard)
    first = jax.tree.map(lambda part: part[0], everything)

    def step(k, so_far):
        return combine(so_far, jax.tree.map(lambda part: part[k], everything))

    return lax.fori_loop(1, lax.axis_size(axis), step, first)


def head_slopes(first_head, how_many):
    head_index = first_head + jnp.arange(how_many, dtype=jnp.int32)
    return jnp.exp2(-8.0 * (head_index + 1).astype(jnp.float32) / H)


def slot_partials(queries, page_keys, page_values, usable, offset, slopes):
    scores = jnp.einsum(
        "sqhd,skhd->sqhk", queries, page_keys, preferred_element_type=jnp.float32
    ) / math.sqrt(HD)
    scores = scores + slopes[None, None, :, None] * offset[:, :, None, :]
    usable_full = usable[:, :, None, :]
    scores = jnp.where(usable_full, scores, masked_score)
    maxima = jnp.max(scores, axis=3)
    weights = jnp.where(usable_full, jnp.exp(scores - maxima[..., None]), 0.0)
    totals = jnp.sum(weights, axis=3)
    outputs = jnp.einsum(
        "sqhk,skhd->sqhd", weights, page_values.astype(jnp.float32), precision=lax.Precision.HIGHEST
    )
    return (maxima, totals, outputs)


def merge_pair(left_part, right_part):
    left_max, left_total, left_out = left_part
    right_max, right_total, right_out = right_part
    joined = jnp.maximum(left_max, right_max)
    left_scale = jnp.exp(left_max - joined)
    right_scale = jnp.exp(right_max - joined)
    return (
        joined,
        left_scale * left_total + right_scale * right_total,
        left_scale[..., None] * left_out + right_scale[..., None] * right_out,
    )


def fold_sources(maxima, totals, outputs):
    joined = jnp.max(maxima, axis=0)
    rescale = jnp.exp(maxima - joined[None])
    return (
        joined,
        jnp.sum(rescale * totals, axis=0),
        jnp.sum(rescale[..., None] * outputs, axis=0),
    )


def cache_partials(
    queries,
    page_block,
    page_item,
    tail_block,
    tail_owner,
    prefix_length,
    tail_length,
    row_index,
    slopes,
):
    cont_count = queries.shape[0]
    prompts = cont_count // CONT
    head_count = queries.shape[2]
    slot_count = page_block.shape[0]
    tokens = page_block.shape[2]
    token_index = row_index * tokens + jnp.arange(tokens, dtype=jnp.int32)
    step_index = jnp.arange(2, dtype=jnp.int32)
    slot_prompt = page_item // MAXPAGES
    slot_page = page_item % MAXPAGES
    by_prompt = queries.reshape(prompts, CONT * 2, head_count, HD)
    key_pos = slot_page[:, None] * PAGE + token_index[None, :]
    slot_len = prefix_length[slot_prompt]
    slot_tails = tail_length.reshape(prompts, CONT)[slot_prompt]
    query_pos = (
        slot_len[:, None, None] + slot_tails[:, :, None] + step_index[None, None, :]
    ).reshape(slot_count, CONT * 2)
    offset = (key_pos[:, None, :] - query_pos[:, :, None]).astype(jnp.float32)
    usable = jnp.broadcast_to((key_pos < slot_len[:, None])[:, None, :], offset.shape)
    page_keys = page_block[:, 0].reshape(slot_count, tokens, head_count, HD)
    page_values = page_block[:, 1].reshape(slot_count, tokens, head_count, HD)
    maxima, totals, outputs = slot_partials(
        by_prompt[slot_prompt], page_keys, page_values, usable, offset, slopes
    )
    prompt_max = (
        jnp.full((prompts, CONT * 2, head_count), masked_score, jnp.float32)
        .at[slot_prompt]
        .max(maxima)
    )
    rescale = jnp.exp(maxima - prompt_max[slot_prompt])
    prompt_total = (
        jnp.zeros((prompts, CONT * 2, head_count), jnp.float32)
        .at[slot_prompt]
        .add(rescale * totals)
    )
    prompt_out = (
        jnp.zeros((prompts, CONT * 2, head_count, HD), jnp.float32)
        .at[slot_prompt]
        .add(rescale[..., None] * outputs)
    )
    prefix_part = (
        prompt_max.reshape(cont_count, 2, head_count),
        prompt_total.reshape(cont_count, 2, head_count),
        prompt_out.reshape(cont_count, 2, head_count, HD),
    )
    tail_count = tail_block.shape[0]
    tail_lens = tail_length[tail_owner]
    tail_usable = jnp.broadcast_to(
        (token_index[None, :] < tail_lens[:, None])[:, None, :], (tail_count, 2, tokens)
    )
    tail_offset = (
        token_index[None, None, :] - tail_lens[:, None, None] - step_index[None, :, None]
    ).astype(jnp.float32)
    tail_keys = tail_block[:, 0].reshape(tail_count, tokens, head_count, HD)
    tail_values = tail_block[:, 1].reshape(tail_count, tokens, head_count, HD)
    tail_max, tail_total, tail_out = slot_partials(
        queries[tail_owner], tail_keys, tail_values, tail_usable, tail_offset, slopes
    )
    cont_max = (
        jnp.full((cont_count, 2, head_count), masked_score, jnp.float32)
        .at[tail_owner]
        .set(tail_max)
    )
    cont_total = jnp.zeros((cont_count, 2, head_count), jnp.float32).at[tail_owner].set(tail_total)
    cont_out = jnp.zeros((cont_count, 2, head_count, HD), jnp.float32).at[tail_owner].set(tail_out)
    return merge_pair(prefix_part, (cont_max, cont_total, cont_out))


def normalize(values, sum_one, sum_two, gain, shift):
    center = sum_one / D
    spread = sum_two / D - center * center
    return (
        (values - center[:, None])
        * lax.rsqrt(spread + norm_eps)[:, None]
        * gain.astype(jnp.float32)
        + shift.astype(jnp.float32)
    ).astype(jnp.bfloat16)


def plain_shards(
    residual,
    fresh_qkv,
    prefix_pages,
    tail_pages,
    prefix_item,
    tail_item,
    prefix_length,
    tail_length,
    out_weight,
    out_bias,
    mlp_gain,
    mlp_shift,
    up_weight,
    up_bias,
    down_weight,
    down_bias,
    next_gain,
    next_shift,
    score_weight,
    qkv_weight,
    qkv_bias,
):
    group_index = lax.axis_index("pages")
    row_index = lax.axis_index("row")
    col_index = lax.axis_index("col")
    group_count = lax.axis_size("pages")
    cont_local = residual.shape[0]
    row_total = cont_local * 2
    share = residual.shape[2]
    head_count = fresh_qkv.shape[3] // HD
    slopes = head_slopes(col_index * head_count, head_count)
    fresh_rows = fresh_qkv.reshape(cont_local, 2, 3, head_count, HD)
    slot_count = prefix_pages.shape[0]
    tail_slots = tail_pages.shape[0]
    everyone = lax.all_gather(fresh_qkv[:, :, 0], "pages", axis=0, tiled=True)
    page_item = lax.dynamic_slice_in_dim(prefix_item, group_index * slot_count, slot_count)
    tail_owner = lax.dynamic_slice_in_dim(tail_item, group_index * tail_slots, tail_slots)
    maxima, totals, outputs = cache_partials(
        everyone.reshape(everyone.shape[0], 2, head_count, HD),
        prefix_pages,
        page_item,
        tail_pages,
        tail_owner,
        prefix_length,
        tail_length,
        row_index,
        slopes,
    )
    maxima, totals, outputs = (
        lax.all_to_all(
            maxima.reshape(group_count, row_total, head_count),
            "pages",
            split_axis=0,
            concat_axis=0,
            tiled=True,
        ),
        lax.all_to_all(
            totals.reshape(group_count, row_total, head_count),
            "pages",
            split_axis=0,
            concat_axis=0,
            tiled=True,
        ),
        lax.all_to_all(
            outputs.reshape(group_count, row_total, head_count, HD),
            "pages",
            split_axis=0,
            concat_axis=0,
            tiled=True,
        ),
    )
    cache_max, cache_total, cache_out = fold_sources(maxima, totals, outputs)
    cache_max, cache_total, cache_out = combined_all(
        (cache_max, cache_total, cache_out), "row", merge_pair
    )
    step_index = jnp.arange(2, dtype=jnp.int32)
    new_usable = jnp.broadcast_to(
        (step_index[None, :] <= step_index[:, None])[None], (cont_local, 2, 2)
    )
    new_offset = jnp.broadcast_to(
        (step_index[None, :] - step_index[:, None]).astype(jnp.float32)[None], (cont_local, 2, 2)
    )
    new_part = slot_partials(
        fresh_rows[:, :, 0],
        fresh_rows[:, :, 1],
        fresh_rows[:, :, 2],
        new_usable,
        new_offset,
        slopes,
    )
    joined_max, joined_total, joined_out = merge_pair(
        (
            cache_max.reshape(cont_local, 2, head_count),
            cache_total.reshape(cont_local, 2, head_count),
            cache_out.reshape(cont_local, 2, head_count, HD),
        ),
        new_part,
    )
    attended = (
        (joined_out / joined_total[..., None])
        .astype(jnp.bfloat16)
        .reshape(row_total, head_count * HD)
    )
    head_term = jnp.dot(attended, out_weight, preferred_element_type=jnp.float32)
    hidden_one = (
        residual.reshape(row_total, share).astype(jnp.float32)
        + lax.psum_scatter(head_term, "col", scatter_dimension=1, tiled=True)
        + out_bias.astype(jnp.float32)
    )
    gain_part = lax.dynamic_slice_in_dim(mlp_gain, col_index * share, share)
    shift_part = lax.dynamic_slice_in_dim(mlp_shift, col_index * share, share)
    sum_one, sum_two = lax.psum(
        (jnp.sum(hidden_one, axis=1), jnp.sum(hidden_one * hidden_one, axis=1)), ("row", "col")
    )
    normed_a = lax.all_gather(
        normalize(hidden_one, sum_one, sum_two, gain_part, shift_part), "col", axis=1, tiled=True
    )
    up_share = lax.psum_scatter(
        jnp.dot(normed_a, up_weight, preferred_element_type=jnp.float32),
        "row",
        scatter_dimension=1,
        tiled=True,
    )
    hidden_two = jax.nn.gelu(up_share + up_bias.astype(jnp.float32), approximate=True).astype(
        jnp.bfloat16
    )
    down_sum = jnp.dot(
        lax.all_gather(hidden_two, "row", axis=1, tiled=True),
        down_weight,
        preferred_element_type=jnp.float32,
    )
    down_share = lax.psum_scatter(
        down_sum.astype(jnp.bfloat16), "col", scatter_dimension=1, tiled=True
    ).astype(jnp.float32)
    layer_out = (hidden_one + down_share + down_bias.astype(jnp.float32)).astype(jnp.bfloat16)
    out_wide = layer_out.astype(jnp.float32)
    gain_part = lax.dynamic_slice_in_dim(next_gain, col_index * share, share)
    shift_part = lax.dynamic_slice_in_dim(next_shift, col_index * share, share)
    score_part = lax.dynamic_slice_in_dim(score_weight, col_index * share, share).astype(
        jnp.float32
    )
    sum_one, sum_two, score_sum = lax.psum(
        (
            jnp.sum(out_wide, axis=1),
            jnp.sum(out_wide * out_wide, axis=1),
            jnp.sum(out_wide * score_part, axis=1),
        ),
        ("row", "col"),
    )
    normed_b = lax.all_gather(
        normalize(out_wide, sum_one, sum_two, gain_part, shift_part), "col", axis=1, tiled=True
    )
    qkv_share = lax.psum_scatter(
        jnp.dot(normed_b, qkv_weight, preferred_element_type=jnp.float32).astype(jnp.bfloat16),
        "row",
        scatter_dimension=1,
        tiled=True,
    ).astype(jnp.float32)
    projected_next = (qkv_share + qkv_bias.astype(jnp.float32)).astype(jnp.bfloat16)
    return (
        layer_out.reshape(cont_local, 2, share),
        score_sum.reshape(cont_local, 2),
        projected_next.reshape(cont_local, 2, qkv_share.shape[1]),
    )


empty_floor = -1e20
STAT = 8
LANES = 128


def columns_to_tile(columns):
    rows = columns[0].shape[0]
    lane = lax.broadcasted_iota(jnp.int32, (rows, LANES), 1)
    wide = jnp.zeros((rows, LANES), jnp.float32)
    for k, column in enumerate(columns):
        wide = jnp.where(lane == k, column, wide)
    if rows < LANES:
        wide = jnp.concatenate([wide, jnp.zeros((LANES - rows, LANES), jnp.float32)], axis=0)
    return jnp.transpose(wide)[:STAT]


def tile_to_columns(tile, rows):
    have = tile.shape[0]
    if have < LANES:
        tile = jnp.concatenate([tile, jnp.zeros((LANES - have, LANES), jnp.float32)], axis=0)
    return jnp.transpose(tile)[:rows]


def layer_kernel(
    sizes,
    item_hbm,
    owner_hbm,
    length_hbm,
    span_hbm,
    fresh_hbm,
    residual_hbm,
    out_bias_hbm,
    mlp_gain_hbm,
    mlp_shift_hbm,
    up_bias_hbm,
    down_bias_hbm,
    next_gain_hbm,
    next_shift_hbm,
    score_hbm,
    qkv_bias_hbm,
    prefix_hbm,
    tail_hbm,
    out_hbm,
    up_hbm,
    down_hbm,
    qkv_hbm,
    layer_ref,
    score_ref,
    proj_ref,
    prefix_item,
    tail_item,
    prefix_length,
    tail_length,
    tail_row,
    fresh_raw,
    residual,
    out_bias,
    mlp_gain,
    mlp_shift,
    up_bias,
    down_bias,
    next_gain,
    next_shift,
    score_weight,
    qkv_bias,
    fresh,
    new_out,
    small_sem,
    prefix_v,
    tail_v,
    out_w,
    up_w,
    down_w,
    qkv_w,
    q_buf,
    p_stage,
    l_stage,
    p_buf,
    l_buf,
    att,
    a_stage,
    a_buf,
    hidden,
    x_buf,
    s_buf,
    normed,
    u_own,
    u_stage,
    u_buf,
    acc,
    d_stage,
    d_buf,
    y_buf,
    t_buf,
    z_stage,
    z_buf,
    page_sem,
    w_sem,
    q_send,
    q_recv,
    p_send,
    p_recv,
    l_send,
    l_recv,
    a_send,
    a_recv,
    x_send,
    x_recv,
    s_send,
    s_recv,
    u_send,
    u_recv,
    d_send,
    d_recv,
    y_send,
    y_recv,
    t_send,
    t_recv,
    z_send,
    z_recv,
):
    G, R, C = sizes["pages"], sizes["row"], sizes["col"]
    f32, bf16, i32 = jnp.float32, jnp.bfloat16, jnp.int32
    me = lax.axis_index("pages")
    row = lax.axis_index("row")
    col = lax.axis_index("col")
    rows = fresh.shape[1]
    share = residual.shape[2]
    width = C * share
    heads = fresh.shape[2] // HD
    slots, _, tokens, _ = prefix_v.shape
    tails = tail_v.shape[0]
    pair_pages, pair_tails = slots // G, tails // G
    _, chunks, _, chunk = u_buf.shape
    _, pieces, _, piece = z_buf.shape

    def group_at(i):
        if isinstance(i, int) and i == 0:
            return me
        j = lax.rem(jnp.int32(i), G - 1) + 1
        return lax.rem(lax.div(me, 2) + lax.div(j, 2), G // 2) * 2 + lax.rem(me + j, 2)

    def row_at(k):
        return lax.rem(row + k, R)

    def col_at(k):
        return lax.rem(col + k, C)

    def remote(src, dst, send_sem, recv_sem, target):
        return pltpu.make_async_remote_copy(
            src_ref=src,
            dst_ref=dst,
            send_sem=send_sem,
            recv_sem=recv_sem,
            device_id=target,
            device_id_type=pl.DeviceIdType.MESH,
        )

    def prefix_copy(g):
        part = pl.ds(g * pair_pages, pair_pages)
        return pltpu.make_async_copy(prefix_hbm.at[part], prefix_v.at[part], page_sem.at[g, 0])

    def tail_copy(g):
        part = pl.ds(g * pair_tails, pair_tails)
        return pltpu.make_async_copy(tail_hbm.at[part], tail_v.at[part], page_sem.at[g, 1])

    weight_copies = [
        pltpu.make_async_copy(src, dst, w_sem.at[k])
        for k, (src, dst) in enumerate(
            ((out_hbm, out_w), (up_hbm, up_w), (down_hbm, down_w), (qkv_hbm, qkv_w))
        )
    ]

    small_pairs = (
        (fresh_hbm, fresh_raw),
        (item_hbm, prefix_item),
        (owner_hbm, tail_item),
        (length_hbm, prefix_length),
        (span_hbm, tail_length),
        (span_hbm, tail_row),
        (residual_hbm, residual),
        (out_bias_hbm, out_bias),
        (mlp_gain_hbm, mlp_gain),
        (mlp_shift_hbm, mlp_shift),
        (up_bias_hbm, up_bias),
        (down_bias_hbm, down_bias),
        (next_gain_hbm, next_gain),
        (next_shift_hbm, next_shift),
        (score_hbm, score_weight),
        (qkv_bias_hbm, qkv_bias),
    )
    small_copies = [
        pltpu.make_async_copy(src, dst, small_sem.at[k])
        for k, (src, dst) in enumerate(small_pairs)
    ]

    barrier = pltpu.get_barrier_semaphore()
    met = 0
    for i in range(G):
        for k in range(R):
            if i or k:
                met += 1
                pl.semaphore_signal(
                    barrier,
                    inc=1,
                    device_id=(group_at(i), row_at(k), col),
                    device_id_type=pl.DeviceIdType.MESH,
                )
    for k in range(R):
        for j in range(1, C):
            met += 1
            pl.semaphore_signal(
                barrier,
                inc=1,
                device_id=(me, row_at(k), col_at(j)),
                device_id_type=pl.DeviceIdType.MESH,
            )
    for copy in small_copies[:6]:
        copy.start()
    for i in range(G):
        prefix_copy(group_at(i)).start()
        tail_copy(group_at(i)).start()
    for copy in small_copies[6:]:
        copy.start()

    row_id = lax.broadcasted_iota(i32, (rows, 1), 0)
    step = lax.rem(row_id, 2)
    row_cont = lax.div(row_id, 2)
    contract_last = (((1,), (1,)), ((), ()))
    scale = 1.0 / math.sqrt(HD)

    def slope_row(h, size):
        index = jnp.full((1, size), col * heads + h + 1, i32).astype(f32)
        return jnp.exp(index * (-8.0 / H * math.log(2.0)))

    small_copies[0].wait()
    for part in range(3):
        fresh[part] = fresh_raw[:, part].reshape(rows, heads * HD)
    q_buf[me] = fresh[0]
    key_id = lax.broadcasted_iota(i32, (rows, rows), 1)
    new_ok = jnp.logical_and(lax.div(key_id, 2) == row_cont, lax.rem(key_id, 2) <= step)
    new_gap = jnp.where(new_ok, (lax.rem(key_id, 2) - step).astype(f32), masked_score)
    levels = []
    for h in range(heads):
        hs = slice(h * HD, (h + 1) * HD)
        scores = (
            lax.dot_general(
                fresh[0, :, hs], fresh[1, :, hs], contract_last, preferred_element_type=f32
            )
            * scale
            + slope_row(h, rows) * new_gap
        )
        top = jnp.max(scores, axis=1, keepdims=True)
        weights = jnp.exp(scores - top)
        total = jnp.sum(weights, axis=1, keepdims=True)
        new_out[:, hs] = (
            jnp.dot(weights.astype(bf16), fresh[2, :, hs], preferred_element_type=f32) / total
        )
        levels.append(top + jnp.log(total))
    new_level = columns_to_tile(levels)

    pl.semaphore_wait(barrier, met)

    sends = []
    for i in range(1, G):
        copy = remote(
            fresh.at[0],
            q_buf.at[me],
            q_send.at[i],
            q_recv.at[me],
            (group_at(i), row, col),
        )
        copy.start()
        sends.append(copy)
    for copy in weight_copies:
        copy.start()
    for copy in small_copies[1:]:
        copy.wait()

    def attend(i):
        g = group_at(i)
        prefix_copy(g).wait()
        tail_copy(g).wait()
        cont = g * lax.div(rows, 2) + row_cont
        prompt_of_row = lax.div(cont, CONT)
        spots = lax.broadcasted_iota(i32, (rows, tail_row.shape[0]), 1)
        tail_spans = tail_row[...].reshape(1, tail_row.shape[0]).astype(f32)
        own_tail = jnp.sum(
            jnp.where(spots == cont, tail_spans, 0.0), axis=1, keepdims=True
        )
        query_off = own_tail + step.astype(f32)

        lane = lax.broadcasted_iota(i32, (1, pair_pages * tokens), 1)
        slot = lax.div(lane, tokens)
        token = lax.rem(lane, tokens) + row * tokens
        owner = jnp.zeros_like(lane)
        place = jnp.zeros_like(lane)
        length = jnp.zeros_like(lane)
        for k in range(pair_pages):
            item = prefix_item[me * slots + g * pair_pages + k]
            prompt = lax.div(item, MAXPAGES)
            hit = slot == k
            owner = jnp.where(hit, prompt, owner)
            place = jnp.where(hit, (item - prompt * MAXPAGES) * PAGE, place)
            length = jnp.where(hit, prefix_length[prompt], length)
        place = place + token
        gap = (place - length).astype(f32)
        open_prompt = jnp.where(place < length, owner, -1)
        prefix_gap = jnp.where(open_prompt == prompt_of_row, gap - query_off, masked_score)

        lane = lax.broadcasted_iota(i32, (1, pair_tails * tokens), 1)
        slot = lax.div(lane, tokens)
        token = lax.rem(lane, tokens) + row * tokens
        owner = jnp.zeros_like(lane)
        length = jnp.zeros_like(lane)
        for k in range(pair_tails):
            item = tail_item[me * tails + g * pair_tails + k]
            hit = slot == k
            owner = jnp.where(hit, item, owner)
            length = jnp.where(hit, tail_length[item], length)
        gap = (token - length).astype(f32)
        open_cont = jnp.where(token < length, owner, -1)
        tail_gap = jnp.where(open_cont == cont, gap - step.astype(f32), masked_score)

        pre = pl.ds(g * pair_pages, pair_pages)
        tai = pl.ds(g * pair_tails, pair_tails)
        spans = [slice(h * HD, (h + 1) * HD) for h in range(heads)]
        scored = []
        for h, hs in enumerate(spans):
            query = q_buf[g, :, hs]
            keys = prefix_v[pre, 0, :, hs].reshape(pair_pages * tokens, HD)
            tail_keys = tail_v[tai, 0, :, hs].reshape(pair_tails * tokens, HD)
            s_one = lax.dot_general(query, keys, contract_last, preferred_element_type=f32)
            s_two = lax.dot_general(query, tail_keys, contract_last, preferred_element_type=f32)
            scored.append(
                (
                    s_one * scale + slope_row(h, pair_pages * tokens) * prefix_gap,
                    s_two * scale + slope_row(h, pair_tails * tokens) * tail_gap,
                )
            )
        tops = [
            jnp.maximum(
                jnp.maximum(
                    jnp.max(s_one, axis=1, keepdims=True), jnp.max(s_two, axis=1, keepdims=True)
                ),
                empty_floor,
            )
            for s_one, s_two in scored
        ]
        weighed = [
            (jnp.exp(s_one - top), jnp.exp(s_two - top))
            for (s_one, s_two), top in zip(scored, tops)
        ]
        totals = [
            jnp.maximum(
                jnp.sum(w_one, axis=1, keepdims=True) + jnp.sum(w_two, axis=1, keepdims=True),
                1e-30,
            )
            for w_one, w_two in weighed
        ]
        for hs, (w_one, w_two), total in zip(spans, weighed, totals):
            values = prefix_v[pre, 1, :, hs].reshape(pair_pages * tokens, HD)
            tail_values = tail_v[tai, 1, :, hs].reshape(pair_tails * tokens, HD)
            out = jnp.dot(w_one.astype(bf16), values, preferred_element_type=f32) + jnp.dot(
                w_two.astype(bf16), tail_values, preferred_element_type=f32
            )
            p_stage[g, :, hs] = (out * (1.0 / total)).astype(bf16)
        levels = [top + jnp.log(total) for top, total in zip(tops, totals)]
        l_stage[g] = columns_to_tile(levels)

    def partial_copies(i, k):
        g = group_at(i)
        target = (g, row_at(k), col)
        return (
            remote(
                p_stage.at[g], p_buf.at[me, row], p_send.at[g, k], p_recv.at[me, row], target
            ),
            remote(
                l_stage.at[g], l_buf.at[me, row], l_send.at[g, k], l_recv.at[me, row], target
            ),
        )

    def partial_arrivals(i, k):
        g, r = group_at(i), row_at(k)
        return (
            remote(p_stage.at[g], p_buf.at[g, r], p_send.at[g, k], p_recv.at[g, r], (g, r, col)),
            remote(l_stage.at[g], l_buf.at[g, r], l_send.at[g, k], l_recv.at[g, r], (g, r, col)),
        )

    attend(0)
    for k in range(1, R):
        for copy in partial_copies(0, k):
            copy.start()
    p_buf[me, row] = p_stage[me]
    l_buf[me, row] = l_stage[me]

    def next_group(i, carry):
        g = group_at(i)
        remote(fresh.at[0], q_buf.at[g], q_send.at[i], q_recv.at[g], (g, row, col)).wait_recv()
        attend(i)
        for k in range(R):
            for copy in partial_copies(i, k):
                copy.start()
        return carry

    lax.fori_loop(1, G, next_group, 0)

    for i in range(G):
        for k in range(R):
            if i or k:
                for copy in partial_arrivals(i, k):
                    copy.wait_recv()

    peers = [l_buf[g, r] for g in range(G) for r in range(R)] + [new_level]
    peak = peers[0]
    for level in peers[1:]:
        peak = jnp.maximum(peak, level)
    shares = [jnp.exp(level - peak) for level in peers]
    total = shares[0]
    for part in shares[1:]:
        total = total + part
    scaled = [part / total for part in shares]
    groups_of_tiles = [
        tile_to_columns(jnp.concatenate(scaled[at : at + LANES // STAT], axis=0), rows)
        for at in range(0, len(scaled), LANES // STAT)
    ]

    def weight_of(peer, h):
        block, spot = divmod(peer, LANES // STAT)
        at = spot * STAT + h
        return groups_of_tiles[block][:, at : at + 1]

    for h in range(heads):
        hs = slice(h * HD, (h + 1) * HD)
        joined = weight_of(G * R, h) * new_out[:, hs]
        for g in range(G):
            for r in range(R):
                joined = joined + weight_of(g * R + r, h) * p_buf[g, r, :, hs].astype(f32)
        att[:, hs] = joined.astype(bf16)

    def share_of(k):
        return pl.ds(pl.multiple_of(col_at(k) * share, LANES), share)

    half_rows = rows // 2
    partner = (me, row_at(1), col)
    per_row = chunks // R
    last = chunks - 1

    def vector(ref):
        return ref[...].astype(f32).reshape(1, ref.shape[0])

    def push(src, dst, send_sem, recv_sem, target):
        copy = remote(src, dst, send_sem, recv_sem, target)
        copy.start()
        sends.append(copy)

    def project_out(b):
        part = att[b * half_rows : (b + 1) * half_rows, :]
        for k in range(1, C):
            a_stage[b, k] = jnp.dot(
                part, out_w[:, share_of(k)], preferred_element_type=f32
            ).astype(bf16)
            push(
                a_stage.at[b, k],
                a_buf.at[b, col],
                a_send.at[b, k],
                a_recv.at[b, col],
                (me, row, col_at(k)),
            )
        stream = residual[b * half_rows // 2 : (b + 1) * half_rows // 2].astype(f32)
        hidden[b] = (
            jnp.dot(part, out_w[:, share_of(0)], preferred_element_type=f32)
            + stream.reshape(half_rows, share)
            + vector(out_bias)
        )

    def summed(b, total, stage, buf, send, recv):
        for k in range(1, C):
            src = col_at(C - k)
            remote(
                stage.at[b, k], buf.at[b, src], send.at[b, k], recv.at[b, src], (me, row, src)
            ).wait_recv()
            total = total + buf[b, src].astype(f32)
        return total

    def gather_start(b, own, parts, wide_buf, wide_send, wide_recv, small_buf, small_send, small_recv):
        wide_buf[b, col] = own
        small_buf[b, row, col] = columns_to_tile(
            [jnp.sum(part, axis=1, keepdims=True) for part in parts]
        )
        for k in range(R):
            for j in range(C):
                if k or j:
                    push(
                        small_buf.at[b, row, col],
                        small_buf.at[b, row, col],
                        small_send.at[b, k, j],
                        small_recv.at[b, row, col],
                        (me, row_at(k), col_at(j)),
                    )
        for j in range(1, C):
            push(
                wide_buf.at[b, col],
                wide_buf.at[b, col],
                wide_send.at[b, j],
                wide_recv.at[b, col],
                (me, row, col_at(j)),
            )

    def gather_norm(
        b, gain, shift, wide_buf, wide_send, wide_recv, small_buf, small_send, small_recv
    ):
        for k in range(R):
            for j in range(C):
                if k or j:
                    r, c = row_at(k), col_at(j)
                    remote(
                        small_buf.at[b, row, col],
                        small_buf.at[b, r, c],
                        small_send.at[b, k, j],
                        small_recv.at[b, r, c],
                        (me, r, c),
                    ).wait_recv()
        sums = small_buf[b, 0, 0]
        for k in range(1, R * C):
            sums = sums + small_buf[b, k // C, k % C]
        columns = tile_to_columns(sums, half_rows)
        center = columns[:, 0:1] / D
        spread = columns[:, 1:2] / D - center * center
        factor = lax.rsqrt(spread + norm_eps)
        gains, shifts = vector(gain), vector(shift)
        for j in range(1, C):
            c = col_at(j)
            remote(
                wide_buf.at[b, col],
                wide_buf.at[b, c],
                wide_send.at[b, j],
                wide_recv.at[b, c],
                (me, row, c),
            ).wait_recv()
        for c in range(C):
            at = slice(c * share, (c + 1) * share)
            normed[b, :, at] = (
                (wide_buf[b, c].astype(f32) - center) * factor * gains[:, at] + shifts[:, at]
            ).astype(bf16)
        return columns

    first_gather = (x_buf, x_send, x_recv, s_buf, s_send, s_recv)
    second_gather = (y_buf, y_send, y_recv, t_buf, t_send, t_recv)

    def up_copy(b, n):
        return (u_stage.at[b, n], u_buf.at[b, n], u_send.at[b, n], u_recv.at[b, n], partner)

    def project_up(b):
        up_shift = vector(up_bias)
        for n in range(chunks):
            part = jnp.dot(
                normed[b], up_w[:, n * chunk : (n + 1) * chunk], preferred_element_type=f32
            )
            mine = jnp.where(jnp.full((1, chunk), row, i32) == n // per_row, 1.0, 0.0)
            spot = n % per_row
            part = part + mine * up_shift[:, spot * chunk : (spot + 1) * chunk]
            u_own[b, n] = part
            u_stage[b, n] = part.astype(bf16)
            push(*up_copy(b, n))

    def project_down(b):
        for n in range(chunks):
            remote(*up_copy(b, n)).wait_recv()
            v = u_own[b, n] + u_buf[b, n].astype(f32)
            gelu = (
                0.5 * v * (1.0 + jnp.tanh(0.7978845608 * (v + 0.044715 * (v * v * v))))
            ).astype(bf16)
            if n < last:
                term = jnp.dot(
                    gelu, down_w[n * chunk : (n + 1) * chunk, :], preferred_element_type=f32
                )
                acc[b] = term if n == 0 else acc[b] + term

        def down_for(k):
            return acc[b, :, share_of(k)] + jnp.dot(
                gelu, down_w[last * chunk :, share_of(k)], preferred_element_type=f32
            )

        for k in range(1, C):
            d_stage[b, k] = down_for(k).astype(bf16)
            push(
                d_stage.at[b, k],
                d_buf.at[b, col],
                d_send.at[b, k],
                d_recv.at[b, col],
                (me, row, col_at(k)),
            )
        hidden[b] = hidden[b] + down_for(0) + vector(down_bias)

    half = pieces * piece

    def qkv_piece(b, r, n):
        at = pl.ds(pl.multiple_of(r * half + n * piece, LANES), piece)
        return jnp.dot(normed[b], qkv_w[:, at], preferred_element_type=f32)

    def z_copy(b, n):
        return (z_stage.at[b, n], z_buf.at[b, n], z_send.at[b, n], z_recv.at[b, n], partner)

    weight_copies[0].wait()
    for b in range(2):
        project_out(b)
    for b in range(2):
        total = summed(b, hidden[b], a_stage, a_buf, a_send, a_recv)
        hidden[b] = total
        gather_start(b, total.astype(bf16), [total, total * total], *first_gather)
    weight_copies[1].wait()
    for b in range(2):
        gather_norm(b, mlp_gain, mlp_shift, *first_gather)
        project_up(b)
    weight_copies[2].wait()
    for b in range(2):
        project_down(b)

    scores = vector(score_weight)
    score_part = scores[:, :share]
    for c in range(1, C):
        score_part = jnp.where(
            jnp.full((1, share), col, i32) == c, scores[:, c * share : (c + 1) * share], score_part
        )
    quarter = half_rows // 2
    for b in range(2):
        layer_out = summed(b, hidden[b], d_stage, d_buf, d_send, d_recv).astype(bf16)
        wide = layer_out.astype(f32)
        gather_start(b, layer_out, [wide, wide * wide, wide * score_part], *second_gather)
        layer_ref[b * quarter : (b + 1) * quarter] = wide.reshape(quarter, 2, share).astype(bf16)
    weight_copies[3].wait()
    score_columns = []
    for b in range(2):
        columns = gather_norm(b, next_gain, next_shift, *second_gather)
        score_columns.append(columns[:, 2:3])
        for n in range(pieces):
            z_stage[b, n] = qkv_piece(b, row_at(1), n).astype(bf16)
            push(*z_copy(b, n))
    seat = lax.broadcasted_iota(i32, (rows, rows // 2), 1)
    score_column = jnp.concatenate(score_columns, axis=0)
    score_ref[...] = jnp.concatenate(
        [
            jnp.sum(jnp.where(row_id == seat * 2 + u, score_column, 0.0), axis=0, keepdims=True)
            for u in range(2)
        ],
        axis=0,
    )
    qkv_shift = vector(qkv_bias)
    for b in range(2):
        for n in range(pieces):
            at = slice(n * piece, (n + 1) * piece)
            own = qkv_piece(b, row, n) + qkv_shift[:, at]
            remote(*z_copy(b, n)).wait_recv()
            own = own + z_buf[b, n].astype(f32)
            proj_ref[b * quarter : (b + 1) * quarter, :, at] = own.reshape(
                quarter, 2, piece
            ).astype(bf16)

    for copy in sends:
        copy.wait_send()
    for i in range(G):
        for k in range(R):
            if i or k:
                for copy in partial_copies(i, k):
                    copy.wait_send()


def hand_out(*refs):
    for k in range(3):
        refs[3 + k][...] = refs[k][...]


def fused_shards(
    sizes,
    residual,
    fresh_qkv,
    prefix_pages,
    tail_pages,
    prefix_item,
    tail_item,
    prefix_length,
    tail_length,
    out_weight,
    out_bias,
    mlp_gain,
    mlp_shift,
    up_weight,
    up_bias,
    down_weight,
    down_bias,
    next_gain,
    next_shift,
    score_weight,
    qkv_weight,
    qkv_bias,
):
    G, R, C = sizes["pages"], sizes["row"], sizes["col"]
    f32, bf16 = jnp.float32, jnp.bfloat16
    cont_local, _, share = residual.shape
    rows = cont_local * 2
    half = rows // 2
    head_width = fresh_qkv.shape[3]
    ff_local = up_weight.shape[1]
    out_local = qkv_bias.shape[0]
    chunk = ff_local // 4
    piece = out_local
    fresh = fresh_qkv.transpose(0, 2, 1, 3)
    one_row = (out_bias, mlp_gain, mlp_shift, up_bias, down_bias)
    one_row = one_row + (next_gain, next_shift, score_weight, qkv_bias)
    vmem = pl.BlockSpec(memory_space=pltpu.VMEM)
    hbm = pl.BlockSpec(memory_space=pltpu.MemorySpace.HBM)
    dma = pltpu.SemaphoreType.DMA
    results = pl.pallas_call(
        lambda *refs: layer_kernel(sizes, *refs),
        out_shape=(
            jax.ShapeDtypeStruct((cont_local, 2, share), bf16),
            jax.ShapeDtypeStruct((2, cont_local), f32),
            jax.ShapeDtypeStruct((cont_local, 2, out_local), bf16),
        ),
        in_specs=[hbm] * (12 + len(one_row)),
        out_specs=(vmem, vmem, vmem),
        scratch_shapes=[
            pltpu.SMEM(prefix_item.shape, jnp.int32),
            pltpu.SMEM(tail_item.shape, jnp.int32),
            pltpu.SMEM(prefix_length.shape, jnp.int32),
            pltpu.SMEM(tail_length.shape, jnp.int32),
            pltpu.VMEM(tail_length.shape, jnp.int32),
            pltpu.VMEM(fresh.shape, bf16),
            pltpu.VMEM(residual.shape, bf16),
            *(pltpu.VMEM(v.shape, bf16) for v in one_row),
            pltpu.VMEM((3, rows, head_width), bf16),
            pltpu.VMEM((rows, head_width), f32),
            dma((7 + len(one_row),)),
            pltpu.VMEM(prefix_pages.shape, bf16),
            pltpu.VMEM(tail_pages.shape, bf16),
            pltpu.VMEM(out_weight.shape, bf16),
            pltpu.VMEM(up_weight.shape, bf16),
            pltpu.VMEM(down_weight.shape, bf16),
            pltpu.VMEM(qkv_weight.shape, bf16),
            pltpu.VMEM((G, rows, head_width), bf16),
            pltpu.VMEM((G, rows, head_width), bf16),
            pltpu.VMEM((G, STAT, LANES), f32),
            pltpu.VMEM((G, R, rows, head_width), bf16),
            pltpu.VMEM((G, R, STAT, LANES), f32),
            pltpu.VMEM((rows, head_width), bf16),
            pltpu.VMEM((2, C, half, share), bf16),
            pltpu.VMEM((2, C, half, share), bf16),
            pltpu.VMEM((2, half, share), f32),
            pltpu.VMEM((2, C, half, share), bf16),
            pltpu.VMEM((2, R, C, STAT, LANES), f32),
            pltpu.VMEM((2, half, C * share), bf16),
            pltpu.VMEM((2, ff_local // chunk, half, chunk), f32),
            pltpu.VMEM((2, ff_local // chunk, half, chunk), bf16),
            pltpu.VMEM((2, ff_local // chunk, half, chunk), bf16),
            pltpu.VMEM((2, half, C * share), f32),
            pltpu.VMEM((2, C, half, share), bf16),
            pltpu.VMEM((2, C, half, share), bf16),
            pltpu.VMEM((2, C, half, share), bf16),
            pltpu.VMEM((2, R, C, STAT, LANES), f32),
            pltpu.VMEM((2, out_local // piece, half, piece), bf16),
            pltpu.VMEM((2, out_local // piece, half, piece), bf16),
            dma((G, 2)),
            dma((4,)),
            dma((G,)),
            dma((G,)),
            dma((G, R)),
            dma((G, R)),
            dma((G, R)),
            dma((G, R)),
            dma((2, C)),
            dma((2, C)),
            dma((2, C)),
            dma((2, C)),
            dma((2, R, C)),
            dma((2, R, C)),
            dma((2, ff_local // chunk)),
            dma((2, ff_local // chunk)),
            dma((2, C)),
            dma((2, C)),
            dma((2, C)),
            dma((2, C)),
            dma((2, R, C)),
            dma((2, R, C)),
            dma((2, out_local // piece)),
            dma((2, out_local // piece)),
        ],
        compiler_params=pltpu.CompilerParams(
            collective_id=0, has_side_effects=True, vmem_limit_bytes=64 * 1024 * 1024
        ),
        name="fused_layer",
    )(
        prefix_item,
        tail_item,
        prefix_length,
        tail_length,
        fresh,
        residual,
        *one_row,
        prefix_pages,
        tail_pages,
        out_weight,
        up_weight,
        down_weight,
        qkv_weight,
    )
    layer_out, scores, projected = pl.pallas_call(
        hand_out,
        out_shape=[jax.ShapeDtypeStruct(part.shape, part.dtype) for part in results],
        in_specs=[vmem] * 3,
        out_specs=[vmem] * 3,
        compiler_params=pltpu.CompilerParams(vmem_limit_bytes=64 * 1024 * 1024),
        name="hand_out",
    )(*results)
    return layer_out, scores.T, projected


def shards(residual, fresh_qkv, prefix_pages, *others):
    sizes = {axis: lax.axis_size(axis) for axis in ("pages", "row", "col")}
    share, tokens = residual.shape[2], prefix_pages.shape[2]
    if sizes["row"] == 2 and sizes["pages"] % 2 == 0 and share % LANES == 0 and tokens % 16 == 0:
        return fused_shards(sizes, residual, fresh_qkv, prefix_pages, *others)
    return plain_shards(residual, fresh_qkv, prefix_pages, *others)


def solution(mesh):
    in_specs = (
        P("pages", None, ("row", "col")),
        P("pages", None, None, "col"),
        P("pages", None, "row", "col"),
        P("pages", None, "row", "col"),
        P(),
        P(),
        P(),
        P(),
        P("col", "row"),
        P(("row", "col")),
        P("row"),
        P("row"),
        P("row", "col"),
        P(("col", "row")),
        P("col", "row"),
        P(("row", "col")),
        P("row"),
        P("row"),
        P("row"),
        P("row", "col"),
        P(("col", "row")),
    )
    out_specs = (
        P("pages", None, ("row", "col")),
        P("pages", None),
        P("pages", None, ("col", "row")),
    )
    return jax.shard_map(shards, mesh=mesh, in_specs=in_specs, out_specs=out_specs, check_vma=False)
```
